32 devices in a mesh: dp: 8 (over y, x, core), tensor: 4 (over z).
Axes of the slice: x: 2, y: 2, z: 4, core: 2. Of those that a mesh axis runs over, the one named last changes fastest.
Arguments:
- stream: float32 [16384, 768], P(('dp', 'tensor')), may hold values from -6 to 6
- cotangent: float32 [16384, 768], P(('dp', 'tensor')), may hold values from -6 to 6
- gain_attention: float32 [768], replicated, may hold values from 0.5 to 1.5
- w_inputs: bfloat16 [3, 768, 768], P(None, None, 'tensor'), may hold values from -0.21875 to 0.21875
- w_output: bfloat16 [768, 768], P('tensor'), may hold values from -0.625 to 0.625
- gain_experts: float32 [768], replicated, may hold values from 0.5 to 1.5
- w_router: bfloat16 [768, 10], replicated, may hold values from -0.109375 to 0.109375
- w_carry: float32 [10, 10], replicated, may hold values from -2 to 2
- w_gate_up: bfloat16 [6, 768, 2, 2048], P(None, None, None, 'tensor'), may hold values from -0.21875 to 0.21875
- w_down: bfloat16 [6, 2048, 768], P(None, 'tensor'), may hold values from -0.1875 to 0.1875
- w_constant: float32 [2, 2, 768], replicated, may hold values from -0.21875 to 0.21875
- constant_vectors: float32 [2, 768], replicated, may hold values from -6 to 6
- previous_logits: float32 [16384, 10], P('dp'), may hold values from -3 to 3
- routes: int32 [16384, 2], P('dp'), may hold values from 0 to 9, all different within a row; in each aligned block of 2048 rows (0 to 2047, 2048 to 4095, ...) at most 768 rows name the same one
- valid: int32 [16384], P('dp'), may hold values from 0 to 1
- prefix: int32 [16], P('dp'), may hold values from 1 to 1024
Outputs:
- block_out: float32 [16384, 768], P(('dp', 'tensor'))
- grad_stream: float32 [16384, 768], P(('dp', 'tensor'))
- grad_gain_attention: float32 [768], replicated
- grad_inputs: float32 [3, 768, 768], P(None, None, 'tensor')
- grad_output: float32 [768, 768], P('tensor')
- grad_gain_experts: float32 [768], replicated
- grad_router: float32 [768, 10], replicated
- grad_carry: float32 [10, 10], replicated
- grad_gate_up: float32 [6, 768, 2, 2048], P(None, None, None, 'tensor')
- grad_down: float32 [6, 2048, 768], P(None, 'tensor')
- grad_constant: float32 [2, 2, 768], replicated
- grad_vectors: float32 [2, 768], replicated
- grad_previous: float32 [16384, 10], P(('dp', 'tensor'))
- rms_values: float32 [3], replicated
The draws below stay inside these ranges and needn't reach their ends.
Inputs may be any that keep to these rules, and one draw needn't show every extreme that they name: `routes`: each row names two different experts: 0 to 5 feed-forward, 6 zero, 7 copy, the last two constant; among the rows of one index of dp no expert is named more than 768 times.
All inputs are finite; a program needn't handle non-finite values.
Results may differ from the reference program's by a relative error of at most 0.022.
Values may be sent and summed in bfloat16 or wider, within the bound.
No kernel may reach another device: no remote copies, remote signals or barrier semaphores. Data moves between devices by JAX's collectives and lax.ppermute only.
A program may use at most 192 MiB of HBM per device.

```python
import math
import jax
import jax.numpy as jnp
import numpy as np
from jax import lax

D = 768
HEADS = 12
HEAD_DIM = 64
FF = 2048
EXP_FFN = 6
SEQ_LEN = 1024
N_ROUTE = 10
TOK_DEV = 2048
CAP = 768
SEQS = 16
TOKENS = 16384
N_DP = 8


def draw_valid(key, part):
    key = jax.random.fold_in(key, 7)
    sequence = jnp.arange(TOKENS, dtype=jnp.int32) // SEQ_LEN
    level = 3 + 6 * sequence // max(SEQS - 1, 1)
    return (jax.random.randint(key, (TOKENS,), 0, 10) < level).astype(jnp.int32)


def plant(array, own_key, least, top_value):
    dims = array.shape
    spot = [jax.random.randint(jax.random.fold_in(own_key, axis), (), 0, dims[axis]) for axis in range(len(dims))]
    array = array.at[tuple(spot)].set(least)
    longest = dims.index(max(dims))
    spot[longest] = (spot[longest] + 1) % dims[longest]
    return array.at[tuple(spot)].set(top_value)


def block_scale(own_key, shape, cuts, smallest, largest):
    level, own = 1.0, jax.random.fold_in(own_key, 6)
    for dim, blocks in cuts:
        heights = jnp.exp(jax.random.uniform(jax.random.fold_in(own, dim), (blocks,), jnp.float32, smallest / len(cuts), largest / len(cuts)))
        level = level * jnp.repeat(heights, shape[dim] // blocks).reshape([-1 if axis == dim else 1 for axis in range(len(shape))])
    return level


def shared_out(rng, own, number, rows, number_of, top, most, lean):
    order = jax.random.permutation(rng, number_of)
    heavy_load, usual = load_shares(number_of, rows * top, most, lean, True), load_shares(number_of, rows * top, most, lean, False)
    places = jnp.arange(number_of)

    def named(tallies, offset_by):
        used = int((tallies > 0).sum())
        fixed = max(1, used // 4)
        passed = fixed + (places - fixed + offset_by * (used - fixed)) % max(1, number_of - fixed)
        return jnp.zeros((number_of,), jnp.int32).at[order[jnp.where(places < fixed, places, passed)]].set(jnp.asarray(tallies, jnp.int32))

    tallies = jnp.where(number % 4 == 0, named(heavy_load, number // 4), named(usual, number - number // 4 - 1))
    mixed = jax.random.permutation(jax.random.fold_in(own, 3), number_of)
    donor, sink = mixed[0:number_of // 2 * 2:2], mixed[1:number_of // 2 * 2:2]
    margin = jnp.minimum(tallies[donor] - 1, most - tallies[sink]) // 2
    margin = jnp.where((donor == order[0]) | (sink == order[0]) | (tallies[sink] == 0), 0, jnp.maximum(margin, 0))
    passed = jax.random.randint(jax.random.fold_in(own, 4), (number_of // 2,), 0, 1 << 20) % (margin + 1)
    tallies = tallies.at[donor].add(-passed).at[sink].add(passed)
    labels = jnp.searchsorted(jnp.cumsum(tallies), jnp.arange(rows * top), side="right").astype(jnp.int32)
    grid = labels.reshape(top, rows).T
    grid = grid[jax.random.permutation(jax.random.fold_in(own, 1), rows)]
    offset_by = jax.random.randint(jax.random.fold_in(own, 2), (rows, 1), 0, top)
    return jnp.take_along_axis(grid, (jnp.arange(top)[None, :] + offset_by) % top, axis=1)


def load_shares(amount, total, reach, slope, full):
    portions = [(1 << 20) // math.isqrt(standing ** slope) + 1 for standing in range(1, amount + 1)]
    largest = reach if full else min(reach, max(-(-total // amount), total * portions[0] // sum(portions)))
    least = 1 if total - largest >= amount - 1 else 0
    given, surplus = [largest] + [least] * (amount - 1), total - largest - least * (amount - 1)
    while surplus > 0:
        candidates = [i for i in range(1, amount) if given[i] < largest] or [i for i in range(1, amount) if given[i] < reach]
        whole, left = sum([portions[i] for i in candidates]), surplus
        for i in candidates:
            more = min(reach - given[i], max(1, left * portions[i] // whole), surplus)
            given[i] = given[i] + more
            surplus = surplus - more
    return np.array(given)


def centred(rng, extent, width, reach, cuts=(), kind=jnp.bfloat16):
    values = jax.random.normal(rng, extent, jnp.float32) * width
    if len(cuts) > 0:
        values = block_scale(rng, extent, cuts, -0.22, 0.18) * values
    return jnp.clip(values, min=-reach, max=reach).astype(kind)


def setup_inputs(seed: int = 0) -> dict:
    key_list = jax.random.split(jax.random.key(seed), 17)
    stream = centred(key_list[0], (TOKENS, D), 1.0, 6.0, ((0, 32),), jnp.float32)
    cotangent = centred(key_list[1], (TOKENS, D), 1.0, 6.0, ((0, 32),), jnp.float32)
    gain_attention = jnp.clip(1.0 + 0.1 * jax.random.normal(key_list[2], (D,), jnp.float32), 0.5, 1.5)
    w_inputs = centred(key_list[3], (3, D, HEADS * HEAD_DIM), D ** -0.5, 0.21875, ((2, 4),))
    w_output = centred(key_list[4], (HEADS * HEAD_DIM, D), (HEADS * HEAD_DIM // 8) ** -0.5, 0.625, ((0, 4),))
    gain_experts = jnp.clip(1.0 + 0.1 * jax.random.normal(key_list[5], (D,), jnp.float32), 0.5, 1.5)
    w_router = centred(key_list[6], (D, N_ROUTE), (4 * D) ** -0.5, 0.109375)
    w_carry = centred(key_list[7], (N_ROUTE, N_ROUTE), N_ROUTE ** -0.5, 2.0, (), jnp.float32)
    w_gate_up = centred(key_list[8], (EXP_FFN, D, 2, FF), D ** -0.5, 0.21875, ((3, 4),))
    w_down = centred(key_list[9], (EXP_FFN, FF, D), (FF // 2) ** -0.5, 0.1875, ((1, 4),))
    w_constant = centred(key_list[10], (2, 2, D), D ** -0.5, 0.21875, (), jnp.float32)
    constant_vectors = centred(key_list[11], (2, D), 1.0, 6.0, (), jnp.float32)
    previous_logits = centred(key_list[12], (TOKENS, N_ROUTE), 0.5, 3.0, ((0, 8),), jnp.float32)
    routes_keys = jax.random.split(jax.random.fold_in(key_list[13], 1), TOKENS // TOK_DEV)
    routes_turns = jax.random.permutation(jax.random.fold_in(key_list[13], 3), TOKENS // TOK_DEV)
    routes = jax.vmap(lambda own, number: shared_out(jax.random.fold_in(key_list[13], 2), own, number, TOK_DEV, N_ROUTE, 2, CAP, 1))(routes_keys, routes_turns).reshape((TOKENS, 2))
    valid = draw_valid(jax.random.fold_in(key_list[16], 71), 0)
    prefix = plant(jax.random.randint(key_list[15], (SEQS,), 1, SEQ_LEN + 1), jax.random.fold_in(key_list[15], 1), 1, SEQ_LEN).astype(jnp.int32)
    return {"stream": stream, "cotangent": cotangent, "gain_attention": gain_attention, "w_inputs": w_inputs, "w_output": w_output, "gain_experts": gain_experts, "w_router": w_router, "w_carry": w_carry, "w_gate_up": w_gate_up, "w_down": w_down, "w_constant": w_constant, "constant_vectors": constant_vectors, "previous_logits": previous_logits, "routes": routes, "valid": valid, "prefix": prefix}


EPSILON = 1e-05
HIGHEST = lax.Precision.HIGHEST

@jax.custom_vjp
def low(v):
    return lax.optimization_barrier(v.astype(jnp.bfloat16)).astype(jnp.float32)

@jax.custom_vjp
def low_back(v):
    return v

def low_keep(v):
    return (low(v), None)

def low_pass(kept, grad):
    return (grad,)

def back_keep(v):
    return (v, None)

def back_low(kept, grad):
    return (low(grad),)
low.defvjp(low_keep, low_pass)
low_back.defvjp(back_keep, back_low)

def matrix(left, right):
    return jnp.dot(left, right, precision=HIGHEST, preferred_element_type=jnp.float32)

def norm(values, gain):
    return values * lax.rsqrt(lax.optimization_barrier(jnp.mean(values * values, axis=-1, keepdims=True)) + EPSILON) * gain

def tables(length):
    half = HEAD_DIM // 2
    frequency = 10000.0 ** (-jnp.arange(half, dtype=jnp.float32) / half)
    position = (jnp.arange(length, dtype=jnp.int32) % SEQ_LEN).astype(jnp.float32)
    angles = position[:, None] * frequency[None, :]
    return (jnp.cos(angles), jnp.sin(angles))

def rotate(values, cosine, sine):
    half = values.shape[-1] // 2
    first = values[..., :half]
    second = values[..., half:]
    cosine = cosine[:, None, :]
    sine = sine[:, None, :]
    return jnp.concatenate([first * cosine - second * sine, first * sine + second * cosine], axis=-1)

def visible(start, rows, length, prefix_len, valid_rows):
    row = start + jnp.arange(rows, dtype=jnp.int32)[:, None]
    column = jnp.arange(length, dtype=jnp.int32)[None, :]
    return ((column <= row) | (column < prefix_len)) & ((valid_rows[None, :] > 0) | (column == row))

def attend_block(start, queries, keys, values, prefix_len, valid_rows):
    allowed = visible(start, queries.shape[0], keys.shape[0], prefix_len, valid_rows)
    raw = low_back(jnp.einsum('qhd,khd->hqk', queries, keys, precision=HIGHEST))
    scores = jnp.where(allowed[None], raw * HEAD_DIM ** (-0.5), -1e+30)
    shares = low(jax.nn.softmax(scores, axis=-1))
    return jnp.einsum('hqk,khd->qhd', shares, values, precision=HIGHEST)

def attend_sequence(item):
    queries, keys, values, valid_rows, prefix_len = item
    block = min(512, SEQ_LEN)
    number = SEQ_LEN // block
    starts = jnp.arange(number, dtype=jnp.int32) * block
    blocks = queries.reshape(number, block, HEADS, HEAD_DIM)
    checked = jax.checkpoint(attend_block)

    def one_block(pair):
        return checked(pair[0], pair[1], keys, values, prefix_len, valid_rows)
    return lax.map(one_block, (starts, blocks)).reshape(SEQ_LEN, HEADS, HEAD_DIM)

def expert_block(item, w_gate_up, w_down):
    second_low, routes, valid_rows, gates = item
    numbers = jnp.arange(EXP_FFN, dtype=jnp.int32)
    hit = routes[:, None, :] == numbers[None, :, None]
    used = jnp.any(hit, axis=-1)
    weight = lax.optimization_barrier(jnp.sum(jnp.where(hit, gates[:, None, :], 0.0), axis=-1)) * valid_rows[:, None]
    order = jnp.argsort(jnp.where(used, 0, 1).T.astype(jnp.int32), axis=1, stable=True)[:, :CAP].astype(jnp.int32)
    live = jnp.take_along_axis(used.T, order, axis=1)
    scale = jnp.where(live, jnp.take_along_axis(weight.T, order, axis=1), 0.0)
    inputs = second_low[order]
    both = low_back(jnp.einsum('ecd,edgf->ecgf', inputs, w_gate_up, precision=HIGHEST))
    hidden = low(jax.nn.silu(both[:, :, 0]) * both[:, :, 1])
    outputs = low_back(jnp.einsum('ecf,efd->ecd', hidden, w_down, precision=HIGHEST))
    terms = (outputs * scale[:, :, None]).reshape(-1, D)
    return jnp.zeros((second_low.shape[0], D), jnp.float32).at[order.reshape(-1)].add(terms)

def forward(stream, gain_attention, w_inputs, w_output, gain_experts, w_router, w_carry, w_gate_up, w_down, w_constant, constant_vectors, previous_logits, routes, valid, prefix):
    tokens = stream.shape[0]
    valid_all = valid.astype(jnp.float32)
    normed = low(norm(stream, gain_attention))
    linear = low_back(jnp.einsum('td,sdc->stc', normed, w_inputs, precision=HIGHEST))
    linear = linear.reshape(3, tokens, HEADS, HEAD_DIM)
    cosine, sine = tables(tokens)
    queries = low(rotate(linear[0], cosine, sine)).reshape(SEQS, SEQ_LEN, HEADS, HEAD_DIM)
    keys = low(rotate(linear[1], cosine, sine)).reshape(SEQS, SEQ_LEN, HEADS, HEAD_DIM)
    values = low(linear[2]).reshape(SEQS, SEQ_LEN, HEADS, HEAD_DIM)
    mixed = lax.map(attend_sequence, (queries, keys, values, valid.reshape(SEQS, SEQ_LEN), prefix))
    mixed = low(low_back(mixed.reshape(tokens, HEADS * HEAD_DIM)))
    attention = low_back(matrix(mixed, w_output))
    middle = stream + attention
    second = norm(middle, gain_experts)
    second_low = low(second)
    logits = matrix(second_low, w_router) + matrix(previous_logits, w_carry)
    gates = jax.nn.softmax(jnp.take_along_axis(logits, routes, axis=1), axis=-1)
    blocks = (second_low.reshape(N_DP, TOK_DEV, D), routes.reshape(N_DP, TOK_DEV, 2), valid_all.reshape(N_DP, TOK_DEV), gates.reshape(N_DP, TOK_DEV, 2))

    def one_device(item):
        return expert_block(item, w_gate_up, w_down)
    feed = lax.map(one_device, blocks).reshape(tokens, D)
    copy_gate = lax.optimization_barrier(jnp.sum(jnp.where(routes == EXP_FFN + 1, gates, 0.0), axis=-1))
    constant_gates = jnp.stack([lax.optimization_barrier(jnp.sum(jnp.where(routes == EXP_FFN + 2 + index, gates, 0.0), axis=-1)) for index in range(2)], axis=1)
    alphas = jax.nn.softmax(jnp.einsum('td,cad->tca', second, w_constant, precision=HIGHEST), axis=-1)
    constant_out = alphas[:, :, 0:1] * second[:, None, :] + alphas[:, :, 1:2] * constant_vectors[None, :, :]
    extra = copy_gate[:, None] * second + lax.optimization_barrier(jnp.sum(constant_gates[:, :, None] * constant_out, axis=1))
    experts = feed + valid_all[:, None] * extra
    return (middle + experts, attention, experts)

def reference(stream, cotangent, gain_attention, w_inputs, w_output, gain_experts, w_router, w_carry, w_gate_up, w_down, w_constant, constant_vectors, previous_logits, routes, valid, prefix):
    floats = tuple((entry.astype(jnp.float32) for entry in (stream, gain_attention, w_inputs, w_output, gain_experts, w_router, w_carry, w_gate_up, w_down, w_constant, constant_vectors, previous_logits)))

    def wrapped(*entries):
        return forward(*entries, routes, valid, prefix)
    outputs, pullback = jax.vjp(wrapped, *floats)
    block_out, attention, experts = outputs
    grads = pullback((cotangent.astype(jnp.float32), jnp.zeros_like(attention), jnp.zeros_like(experts)))
    valid_all = valid.astype(jnp.float32)
    counted = jnp.maximum(jnp.sum(valid_all), 1.0)
    rms_values = jnp.stack([jnp.sqrt(jnp.sum(valid_all[:, None] * part * part) / (counted * D)) for part in (block_out, attention, experts)])
    return (block_out, grads[0], grads[1], grads[2], grads[3], grads[4], grads[5], grads[6], grads[7], grads[8], grads[9], grads[10], grads[11], rms_values)
```

```python
import functools

import jax
import jax.numpy as jnp
from jax import lax
from jax.experimental import pallas as pl
from jax.experimental.pallas import tpu as pltpu
from jax.sharding import PartitionSpec as P

HEAD_DIM = 64
EXP_FFN = 6
SEQ_LEN = 1024
EPSILON = 1e-05
HIGHEST = lax.Precision.HIGHEST
F32 = jnp.float32
BF16 = jnp.bfloat16
I32 = jnp.int32

LANES = 128
TILE = 128
QUERY_BLOCK = 256

SIDE = ((0, 1), (1, 0), (2, 3), (3, 2))
CROSS = ((0, 2), (1, 3), (2, 0), (3, 1))
MIDDLE = ((1, 2), (2, 1))
OUTWARD = ((1, 0), (2, 3))
INWARD = ((0, 1), (3, 2))


def dot(left, right):
    return jnp.dot(left, right, preferred_element_type=F32)


def dot_nt(left, right):
    return lax.dot_general(left, right, (((1,), (1,)), ((), ())), preferred_element_type=F32)


def dot_tn(left, right):
    return lax.dot_general(left, right, (((0,), (0,)), ((), ())), preferred_element_type=F32)


def norm_forward(values, gain):
    inverse = lax.rsqrt(jnp.mean(values * values, axis=-1, keepdims=True) + EPSILON)
    return (values * inverse * gain, inverse)


def norm_backward(values, inverse, gain, grad):
    scaled = grad * gain
    inner = jnp.mean(scaled * values, axis=-1, keepdims=True)
    return inverse * scaled - values * inverse**3 * inner


def along_z(value, pairs):
    return lax.ppermute(value, "tensor", pairs)


def along_dp(value, bit, size):
    return lax.ppermute(value, "dp", [(i, i ^ (1 << bit)) for i in range(size)])


def gather_rows(own, outer):
    side = along_z(own, SIDE)
    middle = along_z(own, MIDDLE)
    far = along_z(middle, OUTWARD)
    across = along_z(side, MIDDLE)
    last = along_z(across, OUTWARD)
    return (own, side, jnp.where(outer, far, middle), jnp.where(outer, last, across))


def slot_chunks(here):
    table = jnp.array([[0, 1, 2, 3], [1, 0, 2, 3], [2, 3, 1, 0], [3, 2, 1, 0]], I32)
    return lax.dynamic_slice_in_dim(table, here, 1, 0)[0]


def scatter_rows(parts):
    last = parts[3] + along_z(parts[3], INWARD)
    third = parts[2] + along_z(parts[2], INWARD)
    second = parts[1] + along_z(last, MIDDLE)
    return (
        parts[0].astype(F32)
        + along_z(third, MIDDLE).astype(F32)
        + along_z(second, SIDE).astype(F32)
    )


def reduce_blocks(value, bits, index, size):
    for bit in bits:
        half = value.shape[0] // 2
        mine = (index >> bit) & 1
        sent = lax.dynamic_slice_in_dim(value, (1 - mine) * half, half, 0)
        kept = lax.dynamic_slice_in_dim(value, mine * half, half, 0)
        value = kept + along_dp(sent, bit, size)
    return value


def spread_blocks(value, bits, index, size):
    for bit in reversed(bits):
        mine = (index >> bit) & 1
        other = along_dp(value, bit, size)
        value = jnp.where(
            mine == 0,
            jnp.concatenate([value, other], axis=0),
            jnp.concatenate([other, value], axis=0),
        )
    return value


def sum_everywhere(value, bits, size):
    for bit in bits:
        value = value + along_dp(value, bit, size)
    value = value + along_z(value, SIDE)
    return value + along_z(value, CROSS)


def rope_tables(offset):
    lane = jnp.arange(LANES, dtype=I32)
    row = jnp.arange(SEQ_LEN, dtype=I32)
    position = jnp.where(row < SEQ_LEN // 2, row + offset, row - offset).astype(F32)
    half = HEAD_DIM // 2
    frequency = 10000.0 ** (-(lane % half).astype(F32) / half)
    angles = position[:, None] * frequency[None, :]
    sign = jnp.where(lane % HEAD_DIM < half, -1.0, 1.0)
    return (jnp.cos(angles), jnp.sin(angles) * sign[None, :])


def swap_halves(value):
    half = HEAD_DIM // 2
    lane = lax.broadcasted_iota(I32, value.shape, 1)
    return jnp.where(
        lane % HEAD_DIM < half,
        pltpu.roll(value, LANES - half, 1),
        pltpu.roll(value, half, 1),
    )


def fill_bias(scalars, valid_ref, bias):
    offset, prefix = scalars[0], scalars[1]
    keys = lax.broadcasted_iota(I32, (SEQ_LEN, 1), 0)
    keys = jnp.where(keys < SEQ_LEN // 2, keys + offset, keys - offset)
    queries = lax.broadcasted_iota(I32, (1, SEQ_LEN), 1)
    queries = jnp.where(queries < SEQ_LEN // 2, queries + offset, queries - offset)
    seen = jnp.where(valid_ref[...] > 0, keys, SEQ_LEN)
    shown = ((seen <= queries) | (seen < prefix)) | (keys == queries)
    bias[...] = jnp.where(shown, 0.0, -1e30)


def head_lanes(value, head):
    lane = lax.broadcasted_iota(I32, value.shape, 1)
    return jnp.where((lane >= head * HEAD_DIM) & (lane < (head + 1) * HEAD_DIM), value, 0)


def attention_kernel(
    scalars, own, other, weights, w_out, cosine, sine, valid,
    part_own, part_other, queries, keys, values, mixed, totals,
    bias, key_rows, value_columns, total,
):
    step = pl.program_id(0)
    half = SEQ_LEN // 2
    upper, lower = pl.ds(0, half), pl.ds(half, half)

    @pl.when(step == 0)
    def _():
        fill_bias(scalars, valid, bias)
        total[...] = jnp.zeros_like(total)

    for source, rows in ((own, upper), (other, lower)):
        x = source[...]
        for kind, target in ((0, queries), (1, keys), (2, values)):
            y = dot_nt(x, weights[kind])
            if kind < 2:
                y = y * cosine[rows, :] + swap_halves(y) * sine[rows, :]
            target[rows, :] = y.astype(BF16)
    key_rows[...] = keys[...]
    value_columns[...] = values[...].T

    @pl.loop(0, SEQ_LEN // QUERY_BLOCK)
    def _(index):
        columns = pl.ds(pl.multiple_of(index * QUERY_BLOCK, QUERY_BLOCK), QUERY_BLOCK)
        query = queries[columns, :] * 0.125
        outs = []
        for head in range(2):
            scores = dot_nt(key_rows[...], head_lanes(query, head)) + bias[:, columns]
            top = jnp.max(scores, axis=0, keepdims=True)
            raw = jnp.exp(scores - top)
            summed = jnp.sum(raw, axis=0, keepdims=True)
            shares = (raw * (1.0 / summed)).astype(BF16)
            outs.append(dot(value_columns[head * HEAD_DIM : (head + 1) * HEAD_DIM, :], shares))
            totals[0, head : head + 1, columns] = top + jnp.log(summed)
        mixed[columns, :] = jnp.concatenate(outs, axis=0).T.astype(BF16)

    total[...] += dot(mixed[...], w_out[...])

    @pl.when(step == pl.num_programs(0) - 1)
    def _():
        part_own[...] = total[upper, :].astype(BF16)
        part_other[...] = total[lower, :].astype(BF16)


def attention_specs(pairs, width):
    whole = lambda *shape: pl.BlockSpec(shape, lambda p, s: (0,) * len(shape))
    half = SEQ_LEN // 2
    rows = whole(half, width)
    weights = pl.BlockSpec((3, LANES, width), lambda p, s: (0, p, 0))
    w_out = pl.BlockSpec((LANES, width), lambda p, s: (p, 0))
    table = whole(SEQ_LEN, LANES)
    column = pl.BlockSpec((SEQ_LEN, LANES), lambda p, s: (0, p))
    totals = pl.BlockSpec((1, 8, SEQ_LEN), lambda p, s: (p, 0, 0))
    return (rows, weights, w_out, table, whole(SEQ_LEN, 1), column, totals)


def attention_forward(scalars, own, other, weights, w_out, cosine, sine, valid):
    width = own.shape[1]
    pairs = weights.shape[1] // LANES
    rows, spec_w, spec_o, table, spec_v, column, totals = attention_specs(pairs, width)
    half = SEQ_LEN // 2
    shape = jax.ShapeDtypeStruct
    flops = 2 * SEQ_LEN * pairs * LANES * (4 * width + 4 * SEQ_LEN)
    return pl.pallas_call(
        attention_kernel,
        grid_spec=pltpu.PrefetchScalarGridSpec(
            num_scalar_prefetch=1,
            grid=(pairs,),
            in_specs=[rows, rows, spec_w, spec_o, table, table, spec_v],
            out_specs=[rows, rows, column, column, column, column, totals],
            scratch_shapes=[
                pltpu.VMEM((SEQ_LEN, SEQ_LEN), F32),
                pltpu.VMEM((SEQ_LEN, LANES), BF16),
                pltpu.VMEM((LANES, SEQ_LEN), BF16),
                pltpu.VMEM((SEQ_LEN, width), F32),
            ],
        ),
        out_shape=[
            shape((half, width), BF16),
            shape((half, width), BF16),
            *[shape((SEQ_LEN, pairs * LANES), BF16)] * 4,
            shape((pairs, 8, SEQ_LEN), F32),
        ],
        compiler_params=pltpu.CompilerParams(vmem_limit_bytes=48 * 2**20),
        cost_estimate=pl.CostEstimate(
            flops=flops, bytes_accessed=12 * 2**20, transcendentals=2 * pairs * SEQ_LEN**2
        ),
        name="attention_forward",
    )(scalars, own, other, weights, w_out, cosine, sine, valid)


def attention_back_kernel(
    scalars, own, other, weights, w_out, cosine, sine, valid,
    grad_own, grad_other, queries, keys, values, mixed, totals,
    part_own, part_other, grad_w, grad_o, gain_row,
    bias, grad_rows, key_columns, total, grad_q, grad_k, grad_v,
):
    step = pl.program_id(0)
    half = SEQ_LEN // 2
    upper, lower = pl.ds(0, half), pl.ds(half, half)

    @pl.when(step == 0)
    def _():
        fill_bias(scalars, valid, bias)
        total[...] = jnp.zeros_like(total)

    grad_rows[upper, :] = dot_nt(grad_own[...], w_out[...]).astype(BF16)
    grad_rows[lower, :] = dot_nt(grad_other[...], w_out[...]).astype(BF16)
    columns_mixed = mixed[...].T
    grad_o[...] = (
        dot(columns_mixed[:, :half], grad_own[...]) + dot(columns_mixed[:, half:], grad_other[...])
    ).astype(BF16)
    key_columns[...] = keys[...].T
    grad_k[...] = jnp.zeros_like(grad_k)
    grad_v[...] = jnp.zeros_like(grad_v)

    @pl.loop(0, SEQ_LEN // QUERY_BLOCK)
    def _(index):
        columns = pl.ds(pl.multiple_of(index * QUERY_BLOCK, QUERY_BLOCK), QUERY_BLOCK)
        query = queries[columns, :] * 0.125
        grad = grad_rows[columns, :]
        outs = []
        for head in range(2):
            query_head = head_lanes(query, head)
            grad_head = head_lanes(grad, head)
            scores = dot_nt(keys[...], query_head) + bias[:, columns]
            shares = jnp.exp(scores - totals[0, head : head + 1, columns])
            grad_shares = dot_nt(values[...], grad_head)
            grad_v[...] += dot(shares.astype(BF16), grad_head)
            product = shares * grad_shares
            inner = jnp.sum(product, axis=0, keepdims=True)
            grad_scores = (product - shares * inner).astype(BF16)
            grad_k[...] += dot(grad_scores, query_head)
            outs.append(dot(key_columns[head * HEAD_DIM : (head + 1) * HEAD_DIM, :], grad_scores))
        grad_q[columns, :] = jnp.concatenate(outs, axis=0).T * 0.125

    for kind, source in ((0, grad_q), (1, grad_k), (2, grad_v)):
        y = source[...]
        if kind < 2:
            y = y * cosine[...] - swap_halves(y) * sine[...]
        y = y.astype(BF16)
        total[...] += dot(y, weights[kind])
        columns_y = y.T
        grad_w[kind] = (
            dot(columns_y[:, :half], own[...]) + dot(columns_y[:, half:], other[...])
        ).astype(BF16)

    @pl.when(step == pl.num_programs(0) - 1)
    def _():
        part_own[...] = total[upper, :].astype(BF16)
        part_other[...] = total[lower, :].astype(BF16)
        product = total[upper, :] * own[...].astype(F32) + total[lower, :] * other[...].astype(F32)
        gain_row[...] = jnp.sum(product.reshape(half // 8, 8, product.shape[1]), axis=0)


def attention_backward(
    scalars, own, other, weights, w_out, cosine, sine, valid, grad_own, grad_other, saved
):
    width = own.shape[1]
    pairs = weights.shape[1] // LANES
    rows, spec_w, spec_o, table, spec_v, column, totals = attention_specs(pairs, width)
    half = SEQ_LEN // 2
    shape = jax.ShapeDtypeStruct
    flops = 2 * SEQ_LEN * pairs * LANES * (8 * width + 10 * SEQ_LEN)
    return pl.pallas_call(
        attention_back_kernel,
        grid_spec=pltpu.PrefetchScalarGridSpec(
            num_scalar_prefetch=1,
            grid=(pairs,),
            in_specs=[
                rows, rows, spec_w, spec_o, table, table, spec_v,
                rows, rows, column, column, column, column, totals,
            ],
            out_specs=[
                rows,
                rows,
                spec_w,
                spec_o,
                pl.BlockSpec((8, width), lambda p, s: (0, 0)),
            ],
            scratch_shapes=[
                pltpu.VMEM((SEQ_LEN, SEQ_LEN), F32),
                pltpu.VMEM((SEQ_LEN, LANES), BF16),
                pltpu.VMEM((LANES, SEQ_LEN), BF16),
                pltpu.VMEM((SEQ_LEN, width), F32),
                *[pltpu.VMEM((SEQ_LEN, LANES), F32)] * 3,
            ],
        ),
        out_shape=[
            shape((half, width), BF16),
            shape((half, width), BF16),
            shape((3, pairs * LANES, width), BF16),
            shape((pairs * LANES, width), BF16),
            shape((8, width), F32),
        ],
        compiler_params=pltpu.CompilerParams(vmem_limit_bytes=48 * 2**20),
        cost_estimate=pl.CostEstimate(
            flops=flops, bytes_accessed=20 * 2**20, transcendentals=2 * pairs * SEQ_LEN**2
        ),
        name="attention_backward",
    )(
        scalars, own, other, weights, w_out, cosine, sine, valid, grad_own, grad_other, *saved
    )


def most_tiles(rows):
    return (2 * rows + EXP_FFN * (TILE - 1)) // TILE


def expert_plan(routes, valid, chunks):
    tokens = routes.shape[0]
    rows = tokens // chunks
    tiles = most_tiles(rows)
    numbers = jnp.arange(8, dtype=I32)[:, None]
    named = ((routes[:, 0][None, :] == numbers) | (routes[:, 1][None, :] == numbers)) & (
        valid[None, :] > 0
    )
    named = (named & (numbers < EXP_FFN)).reshape(8 * chunks, rows)
    before = (jnp.arange(rows)[:, None] < jnp.arange(rows)[None, :]).astype(BF16)
    place = dot(named.astype(BF16), before).astype(I32)
    place = jnp.where(named, place, -1).reshape(8, chunks, rows)
    count = jnp.sum(named.astype(I32), axis=1).reshape(8, chunks)[:EXP_FFN]
    number = (count + TILE - 1) // TILE
    number = jnp.where(jnp.arange(chunks)[None, :] == 0, jnp.maximum(number, 1), number)
    earlier = jnp.arange(EXP_FFN)[:, None] > jnp.arange(EXP_FFN)[None, :]
    first = jnp.sum(jnp.where(earlier[:, :, None], number[None], 0), axis=1)
    total = jnp.sum(number, axis=0)
    slot = jnp.arange(tiles, dtype=I32)
    expert = jnp.sum((first + number)[:, :, None] <= slot, axis=0)
    expert = jnp.minimum(expert, EXP_FFN - 1)
    pick = jnp.arange(EXP_FFN)[:, None, None] == expert[None]
    base = (slot - jnp.sum(jnp.where(pick, first[:, :, None], 0), axis=0)) * TILE
    meta = jnp.concatenate([expert, base, total[:, None]], axis=1).astype(I32)
    flat = number.reshape(-1)
    groups = flat.shape[0]
    earlier = jnp.arange(groups)[:, None] > jnp.arange(groups)[None, :]
    start = jnp.sum(jnp.where(earlier, flat[None, :], 0), axis=1)
    everything = jnp.sum(flat)
    step = jnp.minimum(jnp.arange(chunks * tiles, dtype=I32), everything - 1)
    group = jnp.sum((start + flat)[:, None] <= step[None, :], axis=0)
    pick = jnp.arange(groups)[:, None] == group[None, :]
    offset = jnp.arange(chunks)[None, :] * tiles + first
    block = jnp.sum(jnp.where(pick, (offset.reshape(-1) - start)[:, None], 0), axis=0) + step
    walk = jnp.concatenate([group // chunks, block, everything[None]]).astype(I32)
    return (place.transpose(1, 0, 2), meta.reshape(-1), walk)


def expert_kernel(tiles, span, meta, chunk, x, cot, place, carry, routes, w_router, w_up, w_down, *refs):
    part, feed, x_rows, hidden_rows, grad_rows, both_rows, table, total = refs[-8:]
    step = pl.program_id(0)
    width = x.shape[1]
    hidden_width = w_down.shape[1]
    offset = chunk[0] * span

    @pl.when(step == 0)
    def _():
        logits = dot(x[...], w_router[...]) + carry[0]
        lane = lax.broadcasted_iota(I32, logits.shape, 1)
        one, two = lane == routes[0, :, 0:1], lane == routes[0, :, 1:2]
        score_one = jnp.sum(jnp.where(one, logits, 0.0), axis=1, keepdims=True)
        score_two = jnp.sum(jnp.where(two, logits, 0.0), axis=1, keepdims=True)
        top = jnp.maximum(score_one, score_two)
        score_one, score_two = jnp.exp(score_one - top), jnp.exp(score_two - top)
        both = score_one + score_two
        gates = jnp.where(one, score_one / both, 0.0) + jnp.where(two, score_two / both, 0.0)
        high = gates.astype(BF16).astype(F32)
        low = gates - high
        table[:, :width] = x[...]
        table[:, width : width + LANES] = (high + pltpu.roll(low, LANES // 2, 1)).astype(BF16)
        table[:, width + LANES :] = cot[...]
        total[...] = jnp.zeros_like(total)

    @pl.when(step < meta[offset + 2 * tiles])
    def _():
        expert = meta[offset + step]
        base = meta[offset + tiles + step]
        row = lax.broadcasted_iota(I32, (TILE, x.shape[0]), 0) + base
        hit = jnp.where(place[0, pl.ds(expert, 1), :] == row, 1.0, 0.0).astype(BF16)
        gathered = dot(hit, table[...])
        inputs = gathered[:, :width].astype(BF16)
        lane = lax.broadcasted_iota(I32, (TILE, LANES), 1)
        mine = (lane == expert) | (lane == expert + LANES // 2)
        scale = jnp.sum(
            jnp.where(mine, gathered[:, width : width + LANES], 0.0), axis=1, keepdims=True
        )
        upstream = gathered[:, width + LANES :]
        both = dot(inputs, w_up[0])
        gate, up = both[:, :hidden_width], both[:, hidden_width:]
        sigma = 1.0 / (1.0 + jnp.exp(-gate))
        active = gate * sigma
        hidden = (active * up).astype(BF16)
        outputs = dot(hidden, w_down[0])
        gate_term = jnp.sum(upstream * outputs, axis=1, keepdims=True)
        grad_row = (upstream * scale).astype(BF16)
        grad_hidden = dot_nt(grad_row, w_down[0])
        grad_gate = (grad_hidden * up * sigma * (1.0 + gate * (1.0 - sigma))).astype(BF16)
        grad_up = (grad_hidden * active).astype(BF16)
        grad_both = jnp.concatenate([grad_gate, grad_up], axis=1)
        grad_x = dot_nt(grad_both, w_up[0])
        x_rows[...] = inputs
        hidden_rows[...] = hidden
        grad_rows[...] = grad_row
        both_rows[...] = grad_both
        back = jnp.concatenate(
            [
                (outputs * scale).astype(BF16),
                grad_x.astype(BF16),
                jnp.where(lane == expert, gate_term, 0.0).astype(BF16),
            ],
            axis=1,
        )
        total[...] += dot_tn(hit, back)

    @pl.when(step == tiles - 1)
    def _():
        rows = x.shape[0]
        feed[...] = total[:, :width].astype(BF16)
        part[:rows, :] = total[:, width : 2 * width].astype(BF16)
        terms = total[:, 2 * width :].T[:16]
        part[rows:, :] = jnp.concatenate(
            [terms, jnp.zeros((16, width - rows), F32)], axis=1
        ).astype(BF16)


def expert_chunk(meta, chunk, x, cot, place, carry, routes, w_router, w_up, w_down, saved):
    rows, width = x.shape
    chunks = place.shape[0]
    hidden_width = w_down.shape[1]
    tiles = most_tiles(rows)
    span = 2 * tiles + 1
    shape = jax.ShapeDtypeStruct
    whole = lambda *dims: pl.BlockSpec(dims, lambda i, m, c: (0,) * len(dims))
    mine = lambda *dims: pl.BlockSpec((1, *dims), lambda i, m, c: (c[0], 0, 0))
    weight = lambda *dims: pl.BlockSpec((1, *dims), lambda i, m, c: (m[c[0] * span + i], 0, 0))

    def kept(columns):
        def index(i, m, c):
            last = jnp.maximum(m[c[0] * span + 2 * tiles] - 1, 0)
            return (c[0] * tiles + jnp.minimum(i, last), 0)

        return pl.BlockSpec((TILE, columns), index)

    columns = (width, hidden_width, width, 2 * hidden_width)
    extra = () if saved is None else tuple(saved)
    return pl.pallas_call(
        functools.partial(expert_kernel, tiles, span),
        grid_spec=pltpu.PrefetchScalarGridSpec(
            num_scalar_prefetch=2,
            grid=(tiles,),
            in_specs=[
                whole(rows, width),
                whole(rows, width),
                mine(8, rows),
                mine(rows, LANES),
                mine(rows, 2),
                whole(width, LANES),
                weight(width, 2 * hidden_width),
                weight(hidden_width, width),
                *[pl.BlockSpec(memory_space=pl.ANY)] * len(extra),
            ],
            out_specs=[
                whole(rows + 16, width),
                whole(rows, width),
                *[kept(c) for c in columns],
            ],
            scratch_shapes=[
                pltpu.VMEM((rows, 2 * width + LANES), BF16),
                pltpu.VMEM((rows, 2 * width + LANES), F32),
            ],
        ),
        out_shape=[
            shape((rows + 16, width), BF16),
            shape((rows, width), BF16),
            *[shape((chunks * tiles * TILE, c), BF16) for c in columns],
        ],
        input_output_aliases={10 + k: 2 + k for k in range(len(extra))},
        compiler_params=pltpu.CompilerParams(vmem_limit_bytes=48 * 2**20),
        cost_estimate=pl.CostEstimate(
            flops=8 * 10**9, bytes_accessed=24 * 2**20, transcendentals=TILE * tiles * hidden_width
        ),
        name="expert_chunk",
    )(meta, chunk, x, cot, place, carry, routes, w_router, w_up, w_down, *extra)


def weight_grad_kernel(steps, walk, x_rows, hidden_rows, grad_rows, both_rows, grad_up, grad_down, sum_up, sum_down):
    step = pl.program_id(0)
    number = walk[2 * steps]
    expert = walk[step]

    @pl.when(step < number)
    def _():
        fresh = (step == 0) | (walk[jnp.maximum(step - 1, 0)] != expert)
        up = dot_tn(x_rows[...], both_rows[...])
        down = dot_tn(hidden_rows[...], grad_rows[...])

        @pl.when(fresh)
        def _():
            sum_up[...] = up
            sum_down[...] = down

        @pl.when(jnp.logical_not(fresh))
        def _():
            sum_up[...] += up
            sum_down[...] += down

        done = (step == number - 1) | (walk[jnp.minimum(step + 1, steps - 1)] != expert)

        @pl.when(done)
        def _():
            grad_up[0] = sum_up[...].astype(BF16)
            grad_down[0] = sum_down[...].astype(BF16)


def weight_grads(walk, saved):
    width, hidden_width = saved[0].shape[1], saved[1].shape[1]
    steps = saved[0].shape[0] // TILE
    shape = jax.ShapeDtypeStruct
    rows = lambda columns: pl.BlockSpec((TILE, columns), lambda i, w: (w[steps + i], 0))
    out = lambda *dims: pl.BlockSpec((1, *dims), lambda i, w: (w[i], 0, 0))
    return pl.pallas_call(
        functools.partial(weight_grad_kernel, steps),
        grid_spec=pltpu.PrefetchScalarGridSpec(
            num_scalar_prefetch=1,
            grid=(steps,),
            in_specs=[rows(kept.shape[1]) for kept in saved],
            out_specs=[out(width, 2 * hidden_width), out(hidden_width, width)],
            scratch_shapes=[
                pltpu.VMEM((width, 2 * hidden_width), F32),
                pltpu.VMEM((hidden_width, width), F32),
            ],
        ),
        out_shape=[
            shape((EXP_FFN, width, 2 * hidden_width), BF16),
            shape((EXP_FFN, hidden_width, width), BF16),
        ],
        compiler_params=pltpu.CompilerParams(vmem_limit_bytes=48 * 2**20),
        cost_estimate=pl.CostEstimate(
            flops=12 * 10**9, bytes_accessed=32 * 2**20, transcendentals=0
        ),
        name="weight_grads",
    )(walk, *saved)


def shards(
    dp_size,
    stream,
    cotangent,
    gain_attention,
    w_inputs,
    w_output,
    gain_experts,
    w_router,
    w_carry,
    w_gate_up,
    w_down,
    w_constant,
    constant_vectors,
    previous_logits,
    routes,
    valid,
    prefix,
):
    rows, width = stream.shape
    tokens = routes.shape[0]
    chunks = tokens // rows
    head_columns = w_inputs.shape[2]
    here = lax.axis_index("tensor")
    index = lax.axis_index("dp")
    outer = (here == 0) | (here == chunks - 1)
    bits = list(range(dp_size.bit_length() - 1))
    first_row = here * rows
    valid_all = valid.astype(F32)
    cut = lambda array, at: lax.dynamic_slice_in_dim(array, at, rows, 0)
    valid_here = cut(valid_all, first_row)
    routes_here = cut(routes, first_row)
    previous_here = cut(previous_logits, first_row)

    w_in_rows = w_inputs.transpose(0, 2, 1)
    packed = jnp.concatenate([w_in_rows, w_output[None]], axis=0).reshape(-1, width)
    piece_rows = packed.shape[0] // dp_size
    piece = lax.dynamic_slice_in_dim(packed, index * piece_rows, piece_rows, 0)
    normed_here, inverse_one = norm_forward(stream, gain_attention)
    normed_low = normed_here.astype(BF16)
    normed_other = along_z(normed_low, SIDE)
    piece = along_z(piece, CROSS)
    partner = spread_blocks(piece, bits[::-1], index, dp_size).reshape(4, head_columns, width)
    both_in = jnp.concatenate([w_in_rows, partner[:3]], axis=1)
    both_out = jnp.concatenate([w_output, partner[3]], axis=0)

    cot_low = cotangent.astype(BF16)
    cot_slots = gather_rows(cot_low, outer)

    place, meta, walk = expert_plan(routes, valid, chunks)
    w_up = w_gate_up.reshape(EXP_FFN, width, -1)
    carry = jnp.dot(previous_logits, w_carry, precision=HIGHEST, preferred_element_type=F32)
    columns = carry.shape[1]
    carry_wide = jnp.pad(carry, ((0, 0), (0, LANES - columns))).reshape(chunks, rows, LANES)
    routes_live = jnp.where(valid[:, None] > 0, routes, -1).reshape(chunks, rows, 2)
    router_wide = jnp.pad(w_router, ((0, 0), (0, LANES - columns)))

    offset = (here % 2) * rows
    sequence = here // 2
    scalars = jnp.stack([offset, prefix[sequence]]).astype(I32)
    cosine, sine = rope_tables(offset)
    valid_rows = jnp.concatenate([cut(valid, first_row), cut(valid, (here ^ 1) * rows)])[:, None]
    fixed = (both_in, both_out, cosine, sine, valid_rows)
    part_own, part_other, *saved_attention = attention_forward(
        scalars, normed_low, normed_other, *fixed
    )
    attention = part_own.astype(F32) + along_z(part_other, SIDE).astype(F32)
    middle = stream + attention
    second, inverse_two = norm_forward(middle, gain_experts)
    second_low = second.astype(BF16)
    second_slots = gather_rows(second_low, outer)

    which = slot_chunks(here)
    saved, parts, feeds = None, [], []
    for slot in range(chunks):
        part, feed, *saved = expert_chunk(
            meta,
            which[slot : slot + 1],
            second_slots[slot],
            cot_slots[slot],
            place,
            carry_wide,
            routes_live,
            router_wide,
            w_up,
            w_down,
            saved,
        )
        parts.append(part)
        feeds.append(feed)
    grad_up, grad_down = weight_grads(walk, saved)

    logits = dot(second_low, w_router) + cut(carry, first_row)
    picked = routes_here[:, :, None] == jnp.arange(columns, dtype=I32)[None, None, :]
    chosen = jnp.sum(jnp.where(picked, logits[:, None, :], 0.0), axis=-1)
    gates_here = jax.nn.softmax(chosen, axis=-1)
    live_gates = gates_here * valid_here[:, None]
    copy_gate = jnp.sum(jnp.where(routes_here == EXP_FFN + 1, live_gates, 0.0), axis=-1)
    constant_gates = jnp.stack(
        [
            jnp.sum(jnp.where(routes_here == EXP_FFN + 2 + number, live_gates, 0.0), axis=-1)
            for number in range(2)
        ],
        axis=1,
    )
    alphas = jax.nn.softmax(
        jnp.einsum("td,cad->tca", second, w_constant, precision=HIGHEST, preferred_element_type=F32),
        axis=-1,
    )
    constant_out = (
        alphas[:, :, 0:1] * second[:, None, :] + alphas[:, :, 1:2] * constant_vectors[None, :, :]
    )
    extra = copy_gate[:, None] * second + jnp.sum(
        constant_gates[:, :, None] * constant_out, axis=1
    )
    copy_terms = jnp.sum(cotangent * second, axis=-1)
    constant_terms = jnp.sum(cotangent[:, None, :] * constant_out, axis=-1)
    grad_constant_out = constant_gates[:, :, None] * cotangent[:, None, :]
    grad_vectors = jnp.sum(alphas[:, :, 1:2] * grad_constant_out, axis=0)
    grad_alphas = jnp.stack(
        [
            jnp.sum(grad_constant_out * second[:, None, :], axis=-1),
            jnp.sum(grad_constant_out * constant_vectors[None, :, :], axis=-1),
        ],
        axis=-1,
    )
    grad_mix = alphas * (grad_alphas - jnp.sum(alphas * grad_alphas, axis=-1, keepdims=True))
    grad_constant = jnp.einsum(
        "tca,td->cad", grad_mix, second, precision=HIGHEST, preferred_element_type=F32
    )
    grad_local = (
        copy_gate[:, None] * cotangent
        + jnp.sum(alphas[:, :, 0:1] * grad_constant_out, axis=1)
        + jnp.einsum(
            "tca,cad->td", grad_mix, w_constant, precision=HIGHEST, preferred_element_type=F32
        )
    )

    summed = scatter_rows(parts)
    gate_grads = summed[rows : rows + EXP_FFN, :rows].T
    gate_table = jnp.concatenate(
        [gate_grads, jnp.zeros((rows, 1), F32), copy_terms[:, None], constant_terms], axis=1
    )
    grad_gates = jnp.sum(jnp.where(picked, gate_table[:, None, :], 0.0), axis=-1)
    grad_gates = grad_gates * valid_here[:, None]
    grad_chosen = gates_here * (
        grad_gates - jnp.sum(gates_here * grad_gates, axis=-1, keepdims=True)
    )
    grad_logits = jnp.sum(jnp.where(picked, grad_chosen[:, :, None], 0.0), axis=1)
    grad_router = jnp.dot(
        second_low.astype(F32).T, grad_logits, precision=HIGHEST, preferred_element_type=F32
    )
    grad_carry = jnp.dot(
        previous_here.T, grad_logits, precision=HIGHEST, preferred_element_type=F32
    )
    grad_previous = jnp.dot(
        grad_logits, w_carry.T, precision=HIGHEST, preferred_element_type=F32
    )
    grad_second = (
        summed[:rows]
        + grad_local
        + jnp.dot(
            grad_logits, w_router.astype(F32).T, precision=HIGHEST, preferred_element_type=F32
        )
    )
    grad_gain_experts = jnp.sum(grad_second * middle * inverse_two, axis=0)
    grad_middle = cotangent + norm_backward(middle, inverse_two, gain_experts, grad_second)

    grad_low = grad_middle.astype(BF16)
    grad_other = along_z(grad_low, SIDE)
    part_own, part_other, grad_w, grad_o, gain_rows = attention_backward(
        scalars, normed_low, normed_other, *fixed, grad_low, grad_other, saved_attention
    )
    grad_normed = part_own.astype(F32) + along_z(part_other, SIDE).astype(F32)
    grad_stream = grad_middle + norm_backward(stream, inverse_one, gain_attention, grad_normed)

    feed = scatter_rows(feeds)
    experts = feed + extra
    block_out = middle + experts
    squares = [
        jnp.sum(valid_here[:, None] * part * part) for part in (block_out, attention, experts)
    ]
    squares = jnp.stack([*squares, jnp.sum(valid_here)])

    rotated = [bits[0], *bits[:0:-1]]
    cut_up = jnp.split(grad_up.reshape(-1, grad_up.shape[2]), 2, axis=0)
    cut_down = jnp.split(grad_down.reshape(-1, width), 2, axis=0)
    done = []
    for halves in (cut_up, cut_down):
        both = []
        for half, order in zip(halves, (bits, rotated)):
            reduced = reduce_blocks(half, order, index, dp_size)
            both.append(spread_blocks(reduced, order, index, dp_size))
        done.append(jnp.concatenate(both, axis=0).astype(F32))
    grad_gate_up = done[0].reshape(EXP_FFN, width, 2, -1)
    grad_down = done[1].reshape(EXP_FFN, -1, width)

    own_grads = jnp.concatenate([grad_w[:, :head_columns], grad_o[None, :head_columns]], axis=0)
    far_grads = jnp.concatenate([grad_w[:, head_columns:], grad_o[None, head_columns:]], axis=0)
    order = bits[::-1]
    own_piece = reduce_blocks(own_grads.reshape(-1, width), order, index, dp_size)
    far_piece = reduce_blocks(far_grads.reshape(-1, width), order, index, dp_size)
    own_piece = own_piece + along_z(far_piece, CROSS)
    attention_grads = spread_blocks(own_piece, order, index, dp_size).astype(F32)
    attention_grads = attention_grads.reshape(4, head_columns, width)
    grad_inputs = attention_grads[:3].transpose(0, 2, 1)
    grad_output = attention_grads[3]

    wide = lambda array: jnp.pad(array, ((0, 0), (0, width - array.shape[1])))
    small = jnp.concatenate(
        [
            grad_gain_experts[None],
            grad_router.T,
            wide(grad_carry),
            grad_constant.reshape(-1, width),
            grad_vectors,
            wide(squares[None]),
        ],
        axis=0,
    )
    small = sum_everywhere(small, bits, dp_size)
    gain_row = jnp.sum(gain_rows, axis=0, keepdims=True) / gain_attention[None]
    gain_row = sum_everywhere(gain_row, bits, dp_size)
    at = 1 + 2 * columns
    squares = small[at + 6, :3]
    counted = small[at + 6, 3]
    rms_values = jnp.sqrt(squares / (jnp.maximum(counted, 1.0) * width))
    return (
        block_out,
        grad_stream,
        gain_row[0],
        grad_inputs,
        grad_output,
        small[0],
        small[1 : 1 + columns].T,
        small[1 + columns : at, :columns],
        grad_gate_up,
        grad_down,
        small[at : at + 4].reshape(2, 2, width),
        small[at + 4 : at + 6],
        grad_previous,
        rms_values,
    )


def solution(mesh):
    return jax.shard_map(
        functools.partial(shards, mesh.shape["dp"]),
        mesh=mesh,
        in_specs=(
            P(("dp", "tensor"), None),
            P(("dp", "tensor"), None),
            P(),
            P(None, None, "tensor"),
            P("tensor", None),
            P(),
            P(),
            P(),
            P(None, None, None, "tensor"),
            P(None, "tensor", None),
            P(),
            P(),
            P("dp", None),
            P("dp", None),
            P("dp"),
            P("dp"),
        ),
        out_specs=(
            P(("dp", "tensor"), None),
            P(("dp", "tensor"), None),
            P(),
            P(None, None, "tensor"),
            P("tensor", None),
            P(),
            P(),
            P(),
            P(None, None, None, "tensor"),
            P(None, "tensor", None),
            P(),
            P(),
            P(("dp", "tensor"), None),
            P(),
        ),
        check_vma=False,
    )
```

```python
import functools

import jax
import jax.numpy as jnp
from jax import lax
from jax.experimental import pallas as pl
from jax.experimental.pallas import tpu as pltpu
from jax.sharding import PartitionSpec as P

HEAD_DIM = 64
EXP_FFN = 6
SEQ_LEN = 1024
EPSILON = 1e-05
HIGHEST = lax.Precision.HIGHEST
F32 = jnp.float32
BF16 = jnp.bfloat16
I32 = jnp.int32

LANES = 128
TILE = 128
QUERY_BLOCK = 1024
GROUP = 4
COST_FORWARD, COST_BACKWARD, COST_EXPERT, COST_GRADS, COST_WIDEN, COST_ADD = 20, 32, 20, 11, 3, 3


def lasting(microseconds):
    return pl.CostEstimate(flops=0, bytes_accessed=microseconds * 3 * 10**6, transcendentals=0)


SIDE = ((0, 1), (1, 0), (2, 3), (3, 2))
CROSS = ((0, 2), (1, 3), (2, 0), (3, 1))
MIDDLE = ((1, 2), (2, 1))
OUTWARD = ((1, 0), (2, 3))
INWARD = ((0, 1), (3, 2))


def dot(left, right):
    return jnp.dot(left, right, preferred_element_type=F32)


def dot_nt(left, right):
    return lax.dot_general(left, right, (((1,), (1,)), ((), ())), preferred_element_type=F32)


def dot_tn(left, right):
    return lax.dot_general(left, right, (((0,), (0,)), ((), ())), preferred_element_type=F32)


def norm_forward(values, gain):
    inverse = lax.rsqrt(jnp.mean(values * values, axis=-1, keepdims=True) + EPSILON)
    return (values * inverse * gain, inverse)


def norm_backward(values, inverse, gain, grad):
    scaled = grad * gain
    inner = jnp.mean(scaled * values, axis=-1, keepdims=True)
    return inverse * scaled - values * inverse**3 * inner


def along_z(value, pairs):
    return lax.ppermute(value, "tensor", pairs)


def along_dp(value, bit, size):
    return lax.ppermute(value, "dp", [(i, i ^ (1 << bit)) for i in range(size)])


def behind(value, earlier):
    return lax.optimization_barrier((value, earlier))[0]


def slot_chunks(here):
    table = jnp.array([[0, 1, 2, 3], [1, 0, 2, 3], [2, 3, 1, 0], [3, 2, 1, 0]], I32)
    return lax.dynamic_slice_in_dim(table, here, 1, 0)[0]


def reduce_blocks(value, bits, index, size):
    for bit in bits:
        half = value.shape[0] // 2
        mine = (index >> bit) & 1
        sent = lax.dynamic_slice_in_dim(value, (1 - mine) * half, half, 0)
        kept = lax.dynamic_slice_in_dim(value, mine * half, half, 0)
        value = kept + along_dp(sent, bit, size)
    return value


def spread_blocks(value, bits, index, size):
    for bit in reversed(bits):
        mine = (index >> bit) & 1
        other = along_dp(value, bit, size)
        value = jnp.where(
            mine == 0,
            jnp.concatenate([value, other], axis=0),
            jnp.concatenate([other, value], axis=0),
        )
    return value


def sum_everywhere(value, bits, size):
    for bit in bits:
        value = value + along_dp(value, bit, size)
    value = value + along_z(value, SIDE)
    return value + along_z(value, CROSS)


def piece_place(index, order):
    place = 0
    for bit in order:
        place = 2 * place + ((index >> bit) & 1)
    return place


def rope_tables(offset):
    lane = jnp.arange(LANES, dtype=I32)
    row = jnp.arange(SEQ_LEN, dtype=I32)
    position = jnp.where(row < SEQ_LEN // 2, row + offset, row - offset).astype(F32)
    half = HEAD_DIM // 2
    frequency = 10000.0 ** (-(lane % half).astype(F32) / half)
    angles = position[:, None] * frequency[None, :]
    sign = jnp.where(lane % HEAD_DIM < half, -1.0, 1.0)
    return (jnp.cos(angles), jnp.sin(angles) * sign[None, :])


def swap_halves(value):
    half = HEAD_DIM // 2
    lane = lax.broadcasted_iota(I32, value.shape, 1)
    return jnp.where(
        lane % HEAD_DIM < half,
        pltpu.roll(value, LANES - half, 1),
        pltpu.roll(value, half, 1),
    )


def fill_bias(scalars, valid_ref, bias):
    offset, prefix = scalars[0], scalars[1]
    keys = lax.broadcasted_iota(I32, (SEQ_LEN, 1), 0)
    keys = jnp.where(keys < SEQ_LEN // 2, keys + offset, keys - offset)
    queries = lax.broadcasted_iota(I32, (1, SEQ_LEN), 1)
    queries = jnp.where(queries < SEQ_LEN // 2, queries + offset, queries - offset)
    seen = jnp.where(valid_ref[...] > 0, keys, SEQ_LEN)
    shown = ((seen <= queries) | (seen < prefix)) | (keys == queries)
    bias[...] = jnp.where(shown, 0.0, -1e30)


def head_lanes(value, head):
    lane = lax.broadcasted_iota(I32, value.shape, 1)
    return jnp.where((lane >= head * HEAD_DIM) & (lane < (head + 1) * HEAD_DIM), value, 0)


def attention_kernel(
    scalars, own, other, weights, w_out, cosine, sine, valid, *refs
):
    part_own, part_other, queries, keys, values, mixed, totals = refs[-11:-4]
    bias, key_rows, value_columns, total = refs[-4:]
    step = pl.program_id(0)
    half = SEQ_LEN // 2
    upper, lower = pl.ds(0, half), pl.ds(half, half)

    @pl.when(step == 0)
    def _():
        fill_bias(scalars, valid, bias)
        total[...] = jnp.zeros_like(total)

    for source, rows in ((own, upper), (other, lower)):
        x = source[...]
        for kind, target in ((0, queries), (1, keys), (2, values)):
            y = dot_nt(x, weights[kind])
            if kind < 2:
                y = y * cosine[rows, :] + swap_halves(y) * sine[rows, :]
            target[rows, :] = y.astype(BF16)
    key_rows[...] = keys[...]
    value_columns[...] = values[...].T

    @pl.loop(0, SEQ_LEN // QUERY_BLOCK)
    def _(index):
        columns = pl.ds(pl.multiple_of(index * QUERY_BLOCK, QUERY_BLOCK), QUERY_BLOCK)
        query = queries[columns, :] * 0.125
        outs = []
        for head in range(2):
            scores = dot_nt(key_rows[...], head_lanes(query, head)) + bias[:, columns]
            top = jnp.max(scores, axis=0, keepdims=True)
            raw = jnp.exp(scores - top)
            summed = jnp.sum(raw, axis=0, keepdims=True)
            shares = (raw * (1.0 / summed)).astype(BF16)
            outs.append(dot(value_columns[head * HEAD_DIM : (head + 1) * HEAD_DIM, :], shares))
            totals[0, head : head + 1, columns] = top + jnp.log(summed)
        mixed[columns, :] = jnp.concatenate(outs, axis=0).T.astype(BF16)

    total[...] += dot(mixed[...], w_out[...])

    @pl.when(step == pl.num_programs(0) - 1)
    def _():
        part_own[...] = total[upper, :].astype(BF16)
        part_other[...] = total[lower, :].astype(BF16)


def attention_specs(pairs, width):
    whole = lambda *shape: pl.BlockSpec(shape, lambda p, s: (0,) * len(shape))
    half = SEQ_LEN // 2
    rows = whole(half, width)
    weights = pl.BlockSpec((3, LANES, width), lambda p, s: (0, p, 0))
    w_out = pl.BlockSpec((LANES, width), lambda p, s: (p, 0))
    table = whole(SEQ_LEN, LANES)
    column = pl.BlockSpec((SEQ_LEN, LANES), lambda p, s: (0, p))
    totals = pl.BlockSpec((1, 8, SEQ_LEN), lambda p, s: (p, 0, 0))
    return (rows, weights, w_out, table, whole(SEQ_LEN, 1), column, totals)


def attention_forward(scalars, own, other, weights, w_out, cosine, sine, valid, ready):
    width = own.shape[1]
    pairs = weights.shape[1] // LANES
    rows, spec_w, spec_o, table, spec_v, column, totals = attention_specs(pairs, width)
    half = SEQ_LEN // 2
    shape = jax.ShapeDtypeStruct
    return pl.pallas_call(
        attention_kernel,
        grid_spec=pltpu.PrefetchScalarGridSpec(
            num_scalar_prefetch=1,
            grid=(pairs,),
            in_specs=[rows, rows, spec_w, spec_o, table, table, spec_v]
            + [pl.BlockSpec(memory_space=pl.ANY)] * len(ready),
            out_specs=[rows, rows, column, column, column, column, totals],
            scratch_shapes=[
                pltpu.VMEM((SEQ_LEN, SEQ_LEN), F32),
                pltpu.VMEM((SEQ_LEN, LANES), BF16),
                pltpu.VMEM((LANES, SEQ_LEN), BF16),
                pltpu.VMEM((SEQ_LEN, width), F32),
            ],
        ),
        out_shape=[
            shape((half, width), BF16),
            shape((half, width), BF16),
            *[shape((SEQ_LEN, pairs * LANES), BF16)] * 4,
            shape((pairs, 8, SEQ_LEN), F32),
        ],
        compiler_params=pltpu.CompilerParams(vmem_limit_bytes=48 * 2**20),
        cost_estimate=lasting(COST_FORWARD),
        name="attention_forward",
    )(scalars, own, other, weights, w_out, cosine, sine, valid, *ready)


def attention_back_kernel(
    scalars, own, other, weights, w_out, cosine, sine, valid,
    grad_own, grad_other, queries, keys, values, mixed, totals, *refs
):
    part_own, part_other, grad_w, grad_o, gain_row = refs[-12:-7]
    bias, grad_rows, key_columns, total, grad_q, grad_k, grad_v = refs[-7:]
    step = pl.program_id(0)
    half = SEQ_LEN // 2
    upper, lower = pl.ds(0, half), pl.ds(half, half)

    @pl.when(step == 0)
    def _():
        fill_bias(scalars, valid, bias)
        total[...] = jnp.zeros_like(total)

    grad_rows[upper, :] = dot_nt(grad_own[...], w_out[...]).astype(BF16)
    grad_rows[lower, :] = dot_nt(grad_other[...], w_out[...]).astype(BF16)
    columns_mixed = mixed[...].T
    grad_o[...] = (
        dot(columns_mixed[:, :half], grad_own[...]) + dot(columns_mixed[:, half:], grad_other[...])
    ).astype(BF16)
    key_columns[...] = keys[...].T
    grad_k[...] = jnp.zeros_like(grad_k)
    grad_v[...] = jnp.zeros_like(grad_v)

    @pl.loop(0, SEQ_LEN // QUERY_BLOCK)
    def _(index):
        columns = pl.ds(pl.multiple_of(index * QUERY_BLOCK, QUERY_BLOCK), QUERY_BLOCK)
        query = queries[columns, :] * 0.125
        grad = grad_rows[columns, :]
        outs = []
        for head in range(2):
            query_head = head_lanes(query, head)
            grad_head = head_lanes(grad, head)
            scores = dot_nt(keys[...], query_head) + bias[:, columns]
            shares = jnp.exp(scores - totals[0, head : head + 1, columns])
            grad_shares = dot_nt(values[...], grad_head)
            grad_v[...] += dot(shares.astype(BF16), grad_head)
            product = shares * grad_shares
            inner = jnp.sum(product, axis=0, keepdims=True)
            grad_scores = (product - shares * inner).astype(BF16)
            grad_k[...] += dot(grad_scores, query_head)
            outs.append(dot(key_columns[head * HEAD_DIM : (head + 1) * HEAD_DIM, :], grad_scores))
        grad_q[columns, :] = jnp.concatenate(outs, axis=0).T * 0.125

    for kind, source in ((0, grad_q), (1, grad_k), (2, grad_v)):
        y = source[...]
        if kind < 2:
            y = y * cosine[...] - swap_halves(y) * sine[...]
        y = y.astype(BF16)
        total[...] += dot(y, weights[kind])
        columns_y = y.T
        grad_w[kind] = (
            dot(columns_y[:, :half], own[...]) + dot(columns_y[:, half:], other[...])
        ).astype(BF16)

    @pl.when(step == pl.num_programs(0) - 1)
    def _():
        part_own[...] = total[upper, :].astype(BF16)
        part_other[...] = total[lower, :].astype(BF16)
        product = total[upper, :] * own[...].astype(F32) + total[lower, :] * other[...].astype(F32)
        gain_row[...] = jnp.sum(product.reshape(half // 8, 8, product.shape[1]), axis=0)


def attention_backward(
    scalars, own, other, weights, w_out, cosine, sine, valid, grad_own, grad_other, saved, ready
):
    width = own.shape[1]
    pairs = weights.shape[1] // LANES
    rows, spec_w, spec_o, table, spec_v, column, totals = attention_specs(pairs, width)
    half = SEQ_LEN // 2
    shape = jax.ShapeDtypeStruct
    return pl.pallas_call(
        attention_back_kernel,
        grid_spec=pltpu.PrefetchScalarGridSpec(
            num_scalar_prefetch=1,
            grid=(pairs,),
            in_specs=[
                rows, rows, spec_w, spec_o, table, table, spec_v,
                rows, rows, column, column, column, column, totals,
                *[pl.BlockSpec(memory_space=pl.ANY)] * len(ready),
            ],
            out_specs=[
                rows,
                rows,
                spec_w,
                spec_o,
                pl.BlockSpec((8, width), lambda p, s: (0, 0)),
            ],
            scratch_shapes=[
                pltpu.VMEM((SEQ_LEN, SEQ_LEN), F32),
                pltpu.VMEM((SEQ_LEN, LANES), BF16),
                pltpu.VMEM((LANES, SEQ_LEN), BF16),
                pltpu.VMEM((SEQ_LEN, width), F32),
                *[pltpu.VMEM((SEQ_LEN, LANES), F32)] * 3,
            ],
        ),
        out_shape=[
            shape((half, width), BF16),
            shape((half, width), BF16),
            shape((3, pairs * LANES, width), BF16),
            shape((pairs * LANES, width), BF16),
            shape((8, width), F32),
        ],
        compiler_params=pltpu.CompilerParams(vmem_limit_bytes=48 * 2**20),
        cost_estimate=lasting(COST_BACKWARD),
        name="attention_backward",
    )(
        scalars, own, other, weights, w_out, cosine, sine, valid, grad_own, grad_other, *saved, *ready
    )


def most_tiles(rows):
    return (2 * rows + EXP_FFN * (TILE - 1)) // TILE


def most_groups(tiles, experts):
    return (tiles + experts * (GROUP - 1)) // GROUP


def expert_plan(routes, valid, chunks):
    tokens = routes.shape[0]
    rows = tokens // chunks
    tiles = most_tiles(rows)
    numbers = jnp.arange(8, dtype=I32)[:, None]
    named = ((routes[:, 0][None, :] == numbers) | (routes[:, 1][None, :] == numbers)) & (
        valid[None, :] > 0
    )
    named = (named & (numbers < EXP_FFN)).reshape(8 * chunks, rows)
    before = (jnp.arange(rows)[:, None] < jnp.arange(rows)[None, :]).astype(BF16)
    place = dot(named.astype(BF16), before).astype(I32)
    place = jnp.where(named, place, -1).reshape(8, chunks, rows)
    count = jnp.sum(named.astype(I32), axis=1).reshape(8, chunks)[:EXP_FFN]
    number = (count + TILE - 1) // TILE
    number = jnp.where(jnp.arange(chunks)[None, :] == 0, jnp.maximum(number, 1), number)
    earlier = jnp.arange(EXP_FFN)[:, None] > jnp.arange(EXP_FFN)[None, :]
    first = jnp.sum(jnp.where(earlier[:, :, None], number[None], 0), axis=1)
    total = jnp.sum(number, axis=0)
    slot = jnp.arange(tiles, dtype=I32)
    expert = jnp.sum((first + number)[:, :, None] <= slot, axis=0)
    expert = jnp.minimum(expert, EXP_FFN - 1)
    pick = jnp.arange(EXP_FFN)[:, None, None] == expert[None]
    base = (slot - jnp.sum(jnp.where(pick, first[:, :, None], 0), axis=0)) * TILE
    meta = jnp.concatenate([expert, base, total[:, None]], axis=1).astype(I32)
    return (place.transpose(1, 0, 2), meta.reshape(-1), number, first)


def grad_walk(number, first, tiles, half):
    experts, chunks = number.shape[0] // 2, number.shape[1]
    number = lax.dynamic_slice_in_dim(number, half * experts, experts, 0)
    first = lax.dynamic_slice_in_dim(first, half * experts, experts, 0)
    flat = number.reshape(-1)
    groups = flat.shape[0]
    earlier = jnp.arange(groups)[:, None] > jnp.arange(groups)[None, :]
    start = jnp.sum(jnp.where(earlier, flat[None, :], 0), axis=1)
    held = jnp.sum(number, axis=1)
    held_groups = (held + GROUP - 1) // GROUP
    earlier = jnp.arange(experts)[:, None] > jnp.arange(experts)[None, :]
    held_start = jnp.sum(jnp.where(earlier, held[None, :], 0), axis=1)
    group_start = jnp.sum(jnp.where(earlier, held_groups[None, :], 0), axis=1)
    steps = most_groups(chunks * tiles, experts)
    everything = jnp.sum(held_groups)
    step = jnp.minimum(jnp.arange(steps, dtype=I32), everything - 1)
    owner = jnp.sum((group_start + held_groups)[:, None] <= step[None, :], axis=0)
    pick = jnp.arange(experts)[:, None] == owner[None, :]
    look = lambda values: jnp.sum(jnp.where(pick, values[:, None], 0), axis=0)
    done = (step - look(group_start)) * GROUP
    left = look(held) - done
    place_in = done[:, None] + jnp.minimum(jnp.arange(GROUP)[None, :], left[:, None] - 1)
    spot = (look(held_start)[:, None] + place_in).reshape(-1)
    group = jnp.sum((start + flat)[:, None] <= spot[None, :], axis=0)
    pick = jnp.arange(groups)[:, None] == group[None, :]
    offset = jnp.arange(chunks)[None, :] * tiles + first
    block = jnp.sum(jnp.where(pick, (offset.reshape(-1) - start)[:, None], 0), axis=0) + spot
    return jnp.concatenate([owner, block, left, everything[None]]).astype(I32)


def expert_kernel(tiles, span, meta, chunk, x, cot, place, carry, routes, w_router, w_up, w_down, *refs):
    part, feed, x_rows, hidden_rows, grad_rows, both_rows = refs[-11:-5]
    table, hits, picked, back, total = refs[-5:]
    step = pl.program_id(0)
    width = x.shape[1]
    hidden_width = w_down.shape[1]
    offset = chunk[0] * span
    number = meta[offset + 2 * tiles]
    mine = pl.ds(pl.multiple_of(lax.rem(step, GROUP) * TILE, TILE), TILE)

    @pl.when(step == 0)
    def _():
        logits = dot(x[...], w_router[...]) + carry[0]
        lane = lax.broadcasted_iota(I32, logits.shape, 1)
        one, two = lane == routes[0, :, 0:1], lane == routes[0, :, 1:2]
        score_one = jnp.sum(jnp.where(one, logits, 0.0), axis=1, keepdims=True)
        score_two = jnp.sum(jnp.where(two, logits, 0.0), axis=1, keepdims=True)
        top = jnp.maximum(score_one, score_two)
        score_one, score_two = jnp.exp(score_one - top), jnp.exp(score_two - top)
        both = score_one + score_two
        gates = jnp.where(one, score_one / both, 0.0) + jnp.where(two, score_two / both, 0.0)
        high = gates.astype(BF16).astype(F32)
        low = gates - high
        table[:, :width] = x[...]
        table[:, width : width + LANES] = (high + pltpu.roll(low, LANES // 2, 1)).astype(BF16)
        table[:, width + LANES :] = cot[...]
        total[...] = jnp.zeros_like(total)
        back[...] = jnp.zeros_like(back)

    @pl.when((lax.rem(step, GROUP) == 0) & (step < number))
    def _():
        for at in range(GROUP):
            slot = jnp.minimum(step + at, tiles - 1)
            base = jnp.where(step + at < number, meta[offset + tiles + slot], x.shape[0])
            row = lax.broadcasted_iota(I32, (TILE, x.shape[0]), 0) + base
            hit = place[0, pl.ds(meta[offset + slot], 1), :] == row
            hits[at * TILE : (at + 1) * TILE, :] = jnp.where(hit, 1.0, 0.0).astype(BF16)
        picked[...] = dot(hits[...], table[...]).astype(BF16)

    @pl.when(step < number)
    def _():
        expert = meta[offset + step]
        inputs = picked[mine, :width]
        lane = lax.broadcasted_iota(I32, (TILE, LANES), 1)
        own = (lane == expert) | (lane == expert + LANES // 2)
        scale = jnp.sum(
            jnp.where(own, picked[mine, width : width + LANES].astype(F32), 0.0),
            axis=1,
            keepdims=True,
        )
        upstream = picked[mine, width + LANES :].astype(F32)
        both = dot(inputs, w_up[0])
        gate, up = both[:, :hidden_width], both[:, hidden_width:]
        sigma = 1.0 / (1.0 + jnp.exp(-gate))
        active = gate * sigma
        hidden = (active * up).astype(BF16)
        outputs = dot(hidden, w_down[0])
        gate_term = jnp.sum(upstream * outputs, axis=1, keepdims=True)
        grad_row = (upstream * scale).astype(BF16)
        grad_hidden = dot_nt(grad_row, w_down[0])
        grad_gate = (grad_hidden * up * sigma * (1.0 + gate * (1.0 - sigma))).astype(BF16)
        grad_up = (grad_hidden * active).astype(BF16)
        grad_both = jnp.concatenate([grad_gate, grad_up], axis=1)
        grad_x = dot_nt(grad_both, w_up[0])
        x_rows[...] = inputs
        hidden_rows[...] = hidden
        grad_rows[...] = grad_row
        both_rows[...] = grad_both
        back[mine, :width] = (outputs * scale).astype(BF16)
        back[mine, width : 2 * width] = grad_x.astype(BF16)
        back[mine, 2 * width :] = jnp.where(lane == expert, gate_term, 0.0).astype(BF16)

    @pl.when(
        (step < number) & ((lax.rem(step, GROUP) == GROUP - 1) | (step == number - 1))
    )
    def _():
        total[...] += dot_tn(hits[...], back[...])

    @pl.when(step == pl.num_programs(0) - 1)
    def _():
        rows = x.shape[0]
        feed[...] = total[:, :width].astype(BF16)
        part[:rows, :] = total[:, width : 2 * width].astype(BF16)
        terms = total[:, 2 * width :].T[:16]
        part[rows:, :] = jnp.concatenate(
            [terms, jnp.zeros((16, width - rows), F32)], axis=1
        ).astype(BF16)


def expert_chunk(meta, chunk, x, cot, place, carry, routes, w_router, w_up, w_down, saved):
    rows, width = x.shape
    chunks = place.shape[0]
    hidden_width = w_down.shape[1]
    tiles = most_tiles(rows)
    span = 2 * tiles + 1
    shape = jax.ShapeDtypeStruct
    whole = lambda *dims: pl.BlockSpec(dims, lambda i, m, c: (0,) * len(dims))
    mine = lambda *dims: pl.BlockSpec((1, *dims), lambda i, m, c: (c[0], 0, 0))
    weight = lambda *dims: pl.BlockSpec((1, *dims), lambda i, m, c: (m[c[0] * span + i], 0, 0))

    def kept(columns):
        def index(i, m, c):
            last = jnp.maximum(m[c[0] * span + 2 * tiles] - 1, 0)
            return (c[0] * tiles + jnp.minimum(i, last), 0)

        return pl.BlockSpec((TILE, columns), index)

    columns = (width, hidden_width, width, 2 * hidden_width)
    extra = () if saved is None else tuple(saved)
    return pl.pallas_call(
        functools.partial(expert_kernel, tiles, span),
        grid_spec=pltpu.PrefetchScalarGridSpec(
            num_scalar_prefetch=2,
            grid=(tiles,),
            in_specs=[
                whole(rows, width),
                whole(rows, width),
                mine(8, rows),
                mine(rows, LANES),
                mine(rows, 2),
                whole(width, LANES),
                weight(width, 2 * hidden_width),
                weight(hidden_width, width),
                *[pl.BlockSpec(memory_space=pl.ANY)] * len(extra),
            ],
            out_specs=[
                whole(rows + 16, width),
                whole(rows, width),
                *[kept(c) for c in columns],
            ],
            scratch_shapes=[
                pltpu.VMEM((rows, 2 * width + LANES), BF16),
                pltpu.VMEM((GROUP * TILE, rows), BF16),
                pltpu.VMEM((GROUP * TILE, 2 * width + LANES), BF16),
                pltpu.VMEM((GROUP * TILE, 2 * width + LANES), BF16),
                pltpu.VMEM((rows, 2 * width + LANES), F32),
            ],
        ),
        out_shape=[
            shape((rows + 16, width), BF16),
            shape((rows, width), BF16),
            *[shape((chunks * tiles * TILE, c), BF16) for c in columns],
        ],
        input_output_aliases={10 + k: 2 + k for k in range(len(extra))},
        compiler_params=pltpu.CompilerParams(vmem_limit_bytes=48 * 2**20),
        cost_estimate=lasting(COST_EXPERT),
        name="expert_chunk",
    )(meta, chunk, x, cot, place, carry, routes, w_router, w_up, w_down, *extra)


def weight_grad_kernel(steps, walk, *refs):
    kept, (grad_up, grad_down, sum_up, sum_down) = refs[:-4], refs[-4:]
    step = pl.program_id(0)
    number = walk[(2 + GROUP) * steps]
    expert = walk[step]
    left = walk[(1 + GROUP) * steps + step]

    def joined(kind, live):
        blocks = [kept[kind * GROUP + at][...] for at in range(GROUP)]
        if live:
            blocks = [jnp.where(at < left, block, 0) for at, block in enumerate(blocks)]
        return jnp.concatenate(blocks, axis=0)

    @pl.when(step < number)
    def _():
        fresh = (step == 0) | (walk[jnp.maximum(step - 1, 0)] != expert)

        up = dot_tn(joined(0, True), joined(3, False))
        down = dot_tn(joined(1, True), joined(2, False))

        @pl.when(fresh)
        def _():
            sum_up[...] = up
            sum_down[...] = down

        @pl.when(jnp.logical_not(fresh))
        def _():
            sum_up[...] += up
            sum_down[...] += down

        done = (step == number - 1) | (walk[jnp.minimum(step + 1, steps - 1)] != expert)

        @pl.when(done)
        def _():
            grad_up[...] = sum_up[...].astype(BF16)
            grad_down[...] = sum_down[...].astype(BF16)


def weight_grads(walk, saved):
    width, hidden_width = saved[0].shape[1], saved[1].shape[1]
    experts = EXP_FFN // 2
    steps = most_groups(saved[0].shape[0] // TILE, experts)
    shape = jax.ShapeDtypeStruct

    def rows(columns, at):
        return pl.BlockSpec((TILE, columns), lambda i, w: (w[steps + i * GROUP + at], 0))

    out = lambda *dims: pl.BlockSpec(dims, lambda i, w: (w[i], 0))
    return pl.pallas_call(
        functools.partial(weight_grad_kernel, steps),
        grid_spec=pltpu.PrefetchScalarGridSpec(
            num_scalar_prefetch=1,
            grid=(steps,),
            in_specs=[rows(kept.shape[1], at) for kept in saved for at in range(GROUP)],
            out_specs=[out(width, 2 * hidden_width), out(hidden_width, width)],
            scratch_shapes=[
                pltpu.VMEM((width, 2 * hidden_width), F32),
                pltpu.VMEM((hidden_width, width), F32),
            ],
        ),
        out_shape=[
            shape((experts * width, 2 * hidden_width), BF16),
            shape((experts * hidden_width, width), BF16),
        ],
        compiler_params=pltpu.CompilerParams(vmem_limit_bytes=48 * 2**20),
        cost_estimate=lasting(COST_GRADS),
        name="weight_grads",
    )(walk, *[kept for kept in saved for _ in range(GROUP)])


def combine_kernel(scalars, own_send, far_send, own_keep, far_keep, *refs):
    send, keep = refs[-2:]
    send[...] = own_send[...] + far_send[...]
    keep[...] = own_keep[...] + far_keep[...]


def combine(own, far, bit, start, rows, ready):
    columns = own.shape[1]
    half = rows // 2
    block = min(half, 384)
    number = half // block
    place = lambda side: pl.BlockSpec(
        (block, columns), lambda i, b: (start // block + (b[0] if side else 1 - b[0]) * number + i, 0)
    )
    out = pl.BlockSpec((block, columns), lambda i, b: (i, 0))
    shape = jax.ShapeDtypeStruct((half, columns), own.dtype)
    return pl.pallas_call(
        combine_kernel,
        grid_spec=pltpu.PrefetchScalarGridSpec(
            num_scalar_prefetch=1,
            grid=(number,),
            in_specs=[place(False), place(False), place(True), place(True)]
            + [pl.BlockSpec(memory_space=pl.ANY)] * len(ready),
            out_specs=[out, out],
        ),
        out_shape=[shape, shape],
        compiler_params=pltpu.CompilerParams(vmem_limit_bytes=32 * 2**20),
        cost_estimate=lasting(COST_ADD),
        name="combine",
    )(bit, own, far, own, far, *ready)


def widen_kernel(places, *refs):
    for number, source in enumerate(refs[:-1]):

        @pl.when(pl.program_id(0) == number)
        def _(source=source):
            refs[-1][...] = source[...].astype(F32)


def widen(pieces, places, total, target):
    rows, columns = pieces[0].shape
    extra = () if target is None else (target,)

    def kernel(places, *refs):
        widen_kernel(places, *refs[: len(pieces)], refs[-1])

    return pl.pallas_call(
        kernel,
        grid_spec=pltpu.PrefetchScalarGridSpec(
            num_scalar_prefetch=1,
            grid=(len(pieces),),
            in_specs=[pl.BlockSpec((rows, columns), lambda i, q: (0, 0))] * len(pieces)
            + [pl.BlockSpec(memory_space=pl.ANY)] * len(extra),
            out_specs=pl.BlockSpec((rows, columns), lambda i, q: (q[i], 0)),
        ),
        out_shape=jax.ShapeDtypeStruct((total, columns), F32),
        input_output_aliases={1 + len(pieces): 0} if extra else {},
        compiler_params=pltpu.CompilerParams(vmem_limit_bytes=48 * 2**20),
        cost_estimate=lasting(COST_WIDEN),
        name="widen",
    )(places, *pieces, *extra)


def widen_pairs_kernel(source, *refs):
    target = refs[-1]
    rows, columns = source.shape
    for row in range(columns // LANES):
        at = row % 2 * (columns // 2) + row // 2 * LANES
        target[pl.ds(row, rows, stride=columns // LANES), :] = source[:, at : at + LANES].astype(F32)


def widen_pairs(source, half, target):
    rows, columns = source.shape
    block = 768
    number = rows // block
    extra = () if target is None else (target,)
    split = columns // LANES
    return pl.pallas_call(
        widen_pairs_kernel,
        grid=(number,),
        in_specs=[pl.BlockSpec((block, columns), lambda i: (i, 0))]
        + [pl.BlockSpec(memory_space=pl.ANY)] * len(extra),
        out_specs=pl.BlockSpec((block * split, LANES), lambda i: (half * number + i, 0)),
        out_shape=jax.ShapeDtypeStruct((2 * rows * split, LANES), F32),
        input_output_aliases={1: 0} if extra else {},
        compiler_params=pltpu.CompilerParams(vmem_limit_bytes=48 * 2**20),
        cost_estimate=lasting(COST_WIDEN),
        name="widen_pairs",
    )(source, *extra)


def shards(
    dp_size,
    stream,
    cotangent,
    gain_attention,
    w_inputs,
    w_output,
    gain_experts,
    w_router,
    w_carry,
    w_gate_up,
    w_down,
    w_constant,
    constant_vectors,
    previous_logits,
    routes,
    valid,
    prefix,
):
    rows, width = stream.shape
    tokens = routes.shape[0]
    chunks = tokens // rows
    head_columns = w_inputs.shape[2]
    here = lax.axis_index("tensor")
    index = lax.axis_index("dp")
    outer = (here == 0) | (here == chunks - 1)
    bits = list(range(dp_size.bit_length() - 1))
    first_row = here * rows
    valid_all = valid.astype(F32)
    cut = lambda array, at: lax.dynamic_slice_in_dim(array, at, rows, 0)
    valid_here = cut(valid_all, first_row)
    routes_here = cut(routes, first_row)
    previous_here = cut(previous_logits, first_row)

    w_in_rows = w_inputs.transpose(0, 2, 1)
    packed = jnp.concatenate([w_in_rows, w_output[None]], axis=0).reshape(-1, width)
    piece_rows = packed.shape[0] // dp_size
    position = (index >> 1) | ((index & 1) << (len(bits) - 1))
    piece = lax.dynamic_slice_in_dim(packed, position * piece_rows, piece_rows, 0)
    normed_here, inverse_one = norm_forward(stream, gain_attention)
    normed_low = normed_here.astype(BF16)
    normed_other = along_z(normed_low, SIDE)
    piece = along_z(piece, CROSS)
    cot_low = behind(cotangent, piece).astype(BF16)
    cot_side, cot_middle = along_z(cot_low, SIDE), along_z(cot_low, MIDDLE)
    for level, bit in enumerate([*bits[1:], bits[0]]):
        if level == 0:
            place, meta, number, first = expert_plan(*behind((routes, valid), piece), chunks)
        if level == 1:
            number, first = behind((number, first), piece)
            walks = [grad_walk(number, first, most_tiles(rows), half) for half in range(2)]
        other = along_dp(piece, bit, dp_size)
        piece = jnp.where(
            (index >> bit) & 1 == 0,
            jnp.concatenate([piece, other], axis=0),
            jnp.concatenate([other, piece], axis=0),
        )
    partner = piece.reshape(4, head_columns, width)
    both_in = jnp.concatenate([w_in_rows, partner[:3]], axis=1)
    both_out = jnp.concatenate([w_output, partner[3]], axis=0)

    core = index & 1
    offset = (here % 2) * rows
    sequence = here // 2
    scalars = jnp.stack([offset, prefix[sequence]]).astype(I32)
    cosine, sine = rope_tables(offset)
    valid_rows = jnp.concatenate([cut(valid, first_row), cut(valid, (here ^ 1) * rows)])[:, None]
    fixed = (both_in, both_out, cosine, sine, valid_rows)
    part_own, part_other, *saved_attention = attention_forward(
        scalars, normed_low, normed_other, *fixed, (place, meta, *walks, cot_side, cot_middle)
    )
    attention_other = along_z(part_other, SIDE)

    cot_far, cot_across = along_z(cot_middle, OUTWARD), along_z(cot_side, MIDDLE)
    cot_far, cot_across = behind((cot_far, cot_across), part_own)
    w_up = behind(w_gate_up, (part_own, cot_far, cot_across)).reshape(EXP_FFN, width, -1)
    carry = jnp.dot(behind(previous_logits, part_own), w_carry, precision=HIGHEST, preferred_element_type=F32)
    columns = carry.shape[1]
    carry_wide = jnp.pad(carry, ((0, 0), (0, LANES - columns))).reshape(chunks, rows, LANES)
    routes_live = jnp.where(valid[:, None] > 0, routes, -1).reshape(chunks, rows, 2)
    router_wide = jnp.pad(w_router, ((0, 0), (0, LANES - columns)))

    attention_other = behind(attention_other, w_up)
    attention = part_own.astype(F32) + attention_other.astype(F32)
    middle = stream + attention
    second, inverse_two = norm_forward(middle, gain_experts)
    second_low = second.astype(BF16)

    which = slot_chunks(here)

    def chunk(slot, x, cot, saved):
        return expert_chunk(
            meta,
            which[slot : slot + 1],
            x,
            cot,
            place,
            carry_wide,
            routes_live,
            router_wide,
            w_up,
            w_down,
            saved,
        )

    third_rows = rows // 3 // 16 * 16
    cuts = (0, third_rows, 2 * third_rows, rows)
    cot_pieces = [cot_across[low:high] for low, high in zip(cuts[:-1], cuts[1:])]
    side, middle_rows = along_z(second_low, SIDE), along_z(second_low, MIDDLE)
    cot_last = [along_z(behind(cot_pieces[0], second_low), OUTWARD)]
    part_0, feed_0, *saved = chunk(0, second_low, cot_low, None)
    side, middle_rows, cot_last[0] = behind((side, middle_rows, cot_last[0]), part_0)
    far, across = along_z(middle_rows, OUTWARD), along_z(side, MIDDLE)
    cot_last.append(along_z(behind(cot_pieces[1], part_0), OUTWARD))
    part_1, feed_1, *saved = chunk(1, side, cot_side, saved)
    near = along_z(part_1, INWARD)
    far, across, cot_last[1] = behind((far, across, cot_last[1]), part_1)
    last = along_z(across, OUTWARD)
    cot_last.append(along_z(behind(cot_pieces[2], part_1), OUTWARD))
    part_2, feed_2, *saved = chunk(
        2, jnp.where(outer, far, middle_rows), jnp.where(outer, cot_far, cot_middle), saved
    )
    third = along_z(part_2, INWARD)
    last, cot_last[2] = behind((last, cot_last[2]), part_2)
    part_3, feed_3, *saved = chunk(
        3,
        jnp.where(outer, last, across),
        jnp.where(outer, jnp.concatenate(cot_last, axis=0), cot_across),
        saved,
    )

    inward = along_z(part_3, INWARD)
    up_low, down_low = weight_grads(walks[0], saved)
    inward = part_3 + behind(inward, up_low)
    inward = along_z(inward, MIDDLE)
    third = along_z(part_2 + third, MIDDLE)
    up_high, down_high = weight_grads(walks[1], saved)
    outward_sum = part_1 + behind(inward, up_high)
    outward = along_z(outward_sum, OUTWARD)
    up_low, up_high, down_low, down_high = lax.psum((up_low, up_high, down_low, down_high), "dp")
    summed = part_0.astype(F32) + near.astype(F32) + third.astype(F32) + outward.astype(F32)

    logits = dot(second_low, w_router) + cut(carry, first_row)
    picked = routes_here[:, :, None] == jnp.arange(columns, dtype=I32)[None, None, :]
    chosen = jnp.sum(jnp.where(picked, logits[:, None, :], 0.0), axis=-1)
    gates_here = jax.nn.softmax(chosen, axis=-1)
    live_gates = gates_here * valid_here[:, None]
    copy_gate = jnp.sum(jnp.where(routes_here == EXP_FFN + 1, live_gates, 0.0), axis=-1)
    constant_gates = jnp.stack(
        [
            jnp.sum(jnp.where(routes_here == EXP_FFN + 2 + number, live_gates, 0.0), axis=-1)
            for number in range(2)
        ],
        axis=1,
    )
    alphas = jax.nn.softmax(
        jnp.einsum("td,cad->tca", second, w_constant, precision=HIGHEST, preferred_element_type=F32),
        axis=-1,
    )
    constant_out = (
        alphas[:, :, 0:1] * second[:, None, :] + alphas[:, :, 1:2] * constant_vectors[None, :, :]
    )
    extra = copy_gate[:, None] * second + jnp.sum(
        constant_gates[:, :, None] * constant_out, axis=1
    )
    copy_terms = jnp.sum(cotangent * second, axis=-1)
    constant_terms = jnp.sum(cotangent[:, None, :] * constant_out, axis=-1)
    grad_constant_out = constant_gates[:, :, None] * cotangent[:, None, :]
    grad_vectors = jnp.sum(alphas[:, :, 1:2] * grad_constant_out, axis=0)
    grad_alphas = jnp.stack(
        [
            jnp.sum(grad_constant_out * second[:, None, :], axis=-1),
            jnp.sum(grad_constant_out * constant_vectors[None, :, :], axis=-1),
        ],
        axis=-1,
    )
    grad_mix = alphas * (grad_alphas - jnp.sum(alphas * grad_alphas, axis=-1, keepdims=True))
    grad_constant = jnp.einsum(
        "tca,td->cad", grad_mix, second, precision=HIGHEST, preferred_element_type=F32
    )
    grad_local = (
        copy_gate[:, None] * cotangent
        + jnp.sum(alphas[:, :, 0:1] * grad_constant_out, axis=1)
        + jnp.einsum(
            "tca,cad->td", grad_mix, w_constant, precision=HIGHEST, preferred_element_type=F32
        )
    )

    gate_grads = summed[rows : rows + EXP_FFN, :rows].T
    gate_table = jnp.concatenate(
        [gate_grads, jnp.zeros((rows, 1), F32), copy_terms[:, None], constant_terms], axis=1
    )
    grad_gates = jnp.sum(jnp.where(picked, gate_table[:, None, :], 0.0), axis=-1)
    grad_gates = grad_gates * valid_here[:, None]
    grad_chosen = gates_here * (
        grad_gates - jnp.sum(gates_here * grad_gates, axis=-1, keepdims=True)
    )
    grad_logits = jnp.sum(jnp.where(picked, grad_chosen[:, :, None], 0.0), axis=1)
    grad_router = jnp.dot(
        second_low.astype(F32).T, grad_logits, precision=HIGHEST, preferred_element_type=F32
    )
    grad_carry = jnp.dot(
        previous_here.T, grad_logits, precision=HIGHEST, preferred_element_type=F32
    )
    grad_previous = jnp.dot(
        grad_logits, w_carry.T, precision=HIGHEST, preferred_element_type=F32
    )
    grad_second = (
        summed[:rows]
        + grad_local
        + jnp.dot(
            grad_logits, w_router.astype(F32).T, precision=HIGHEST, preferred_element_type=F32
        )
    )
    grad_gain_experts = jnp.sum(grad_second * middle * inverse_two, axis=0)
    grad_middle = cotangent + norm_backward(middle, inverse_two, gain_experts, grad_second)

    grad_low = grad_middle.astype(BF16)
    grad_other = along_z(grad_low, SIDE)

    part_own, part_other, grad_w, grad_o, gain_rows = attention_backward(
        scalars, normed_low, normed_other, *fixed, grad_low, grad_other, saved_attention, ()
    )
    grad_normed = part_own.astype(F32) + along_z(part_other, SIDE).astype(F32)
    grad_stream = grad_middle + norm_backward(stream, inverse_one, gain_attention, grad_normed)

    feed_1, feed_2, feed_3 = behind((feed_1, feed_2, feed_3), grad_low)
    near = along_z(feed_1, INWARD)
    third = along_z(feed_2 + along_z(feed_2, INWARD), MIDDLE)
    outward = along_z(feed_3 + along_z(feed_3, INWARD), MIDDLE)
    outward = along_z(feed_1 + outward, OUTWARD)
    feed = feed_0.astype(F32) + near.astype(F32) + third.astype(F32) + outward.astype(F32)
    experts = feed + extra
    block_out = middle + experts
    squares = [
        jnp.sum(valid_here[:, None] * part * part) for part in (block_out, attention, experts)
    ]
    squares = jnp.stack([*squares, jnp.sum(valid_here)])

    grad_down = jnp.concatenate([down_low, down_high], axis=0).astype(F32)
    grad_down = grad_down.reshape(EXP_FFN, -1, width)
    grad_gate_up = widen_pairs(up_high, 1, widen_pairs(up_low, 0, None))
    tiles = up_low.shape[1] // (2 * LANES)
    grad_gate_up = grad_gate_up.reshape(EXP_FFN, width, tiles, 2, LANES).transpose(0, 1, 3, 2, 4)
    grad_gate_up = grad_gate_up.reshape(EXP_FFN, width, 2, -1)

    own_grads = jnp.concatenate([grad_w[:, :head_columns], grad_o[None, :head_columns]], axis=0)
    far_grads = jnp.concatenate([grad_w[:, head_columns:], grad_o[None, head_columns:]], axis=0)
    order = bits
    own_piece = reduce_blocks(own_grads.reshape(-1, width), order, index, dp_size)
    far_piece = reduce_blocks(far_grads.reshape(-1, width), order, index, dp_size)
    own_piece = own_piece + along_z(far_piece, CROSS)
    attention_grads = spread_blocks(own_piece, order, index, dp_size).astype(F32)
    attention_grads = attention_grads.reshape(4, head_columns, width)
    grad_inputs = attention_grads[:3].transpose(0, 2, 1)
    grad_output = attention_grads[3]

    wide = lambda array: jnp.pad(array, ((0, 0), (0, width - array.shape[1])))
    small = jnp.concatenate(
        [
            grad_gain_experts[None],
            grad_router.T,
            wide(grad_carry),
            grad_constant.reshape(-1, width),
            grad_vectors,
            wide(squares[None]),
            jnp.sum(gain_rows, axis=0, keepdims=True) / gain_attention[None],
        ],
        axis=0,
    )
    small = sum_everywhere(small, bits, dp_size)
    at = 1 + 2 * columns
    squares = small[at + 6, :3]
    counted = small[at + 6, 3]
    rms_values = jnp.sqrt(squares / (jnp.maximum(counted, 1.0) * width))
    return (
        block_out,
        grad_stream,
        small[at + 7],
        grad_inputs,
        grad_output,
        small[0],
        small[1 : 1 + columns].T,
        small[1 + columns : at, :columns],
        grad_gate_up,
        grad_down,
        small[at : at + 4].reshape(2, 2, width),
        small[at + 4 : at + 6],
        grad_previous,
        rms_values,
    )


def solution(mesh):
    return jax.shard_map(
        functools.partial(shards, mesh.shape["dp"]),
        mesh=mesh,
        in_specs=(
            P(("dp", "tensor"), None),
            P(("dp", "tensor"), None),
            P(),
            P(None, None, "tensor"),
            P("tensor", None),
            P(),
            P(),
            P(),
            P(None, None, None, "tensor"),
            P(None, "tensor", None),
            P(),
            P(),
            P("dp", None),
            P("dp", None),
            P("dp"),
            P("dp"),
        ),
        out_specs=(
            P(("dp", "tensor"), None),
            P(("dp", "tensor"), None),
            P(),
            P(None, None, "tensor"),
            P("tensor", None),
            P(),
            P(),
            P(),
            P(None, None, None, "tensor"),
            P(None, "tensor", None),
            P(),
            P(),
            P(("dp", "tensor"), None),
            P(),
        ),
        check_vma=False,
    )
```

```python
import functools

import jax
import jax.numpy as jnp
from jax import lax
from jax.experimental import pallas as pl
from jax.experimental.pallas import tpu as pltpu
from jax.sharding import PartitionSpec as P

HEAD_DIM = 64
EXP_FFN = 6
SEQ_LEN = 1024
EPSILON = 1e-05
HIGHEST = lax.Precision.HIGHEST
F32 = jnp.float32
BF16 = jnp.bfloat16
I32 = jnp.int32

LANES = 128
TILE = 128
QUERY_BLOCK = 1024
GROUP = 4
GATHER = 3
COST_FORWARD, COST_BACKWARD, COST_EXPERT, COST_GRADS, COST_WIDEN, COST_ADD = 20, 32, 20, 11, 3, 3


def lasting(microseconds):
    return pl.CostEstimate(flops=0, bytes_accessed=microseconds * 3 * 10**6, transcendentals=0)


SIDE = ((0, 1), (1, 0), (2, 3), (3, 2))
CROSS = ((0, 2), (1, 3), (2, 0), (3, 1))
MIDDLE = ((1, 2), (2, 1))
OUTWARD = ((1, 0), (2, 3))
INWARD = ((0, 1), (3, 2))


def dot(left, right):
    return jnp.dot(left, right, preferred_element_type=F32)


def dot_nt(left, right):
    return lax.dot_general(left, right, (((1,), (1,)), ((), ())), preferred_element_type=F32)


def dot_tn(left, right):
    return lax.dot_general(left, right, (((0,), (0,)), ((), ())), preferred_element_type=F32)


def norm_forward(values, gain):
    inverse = lax.rsqrt(jnp.mean(values * values, axis=-1, keepdims=True) + EPSILON)
    return (values * inverse * gain, inverse)


def norm_backward(values, inverse, gain, grad):
    scaled = grad * gain
    inner = jnp.mean(scaled * values, axis=-1, keepdims=True)
    return inverse * scaled - values * inverse**3 * inner


def along_z(value, pairs):
    return lax.ppermute(value, "tensor", pairs)


def along_dp(value, bit, size):
    return lax.ppermute(value, "dp", [(i, i ^ (1 << bit)) for i in range(size)])


def behind(value, earlier):
    return lax.optimization_barrier((value, earlier))[0]


def slot_chunks(here):
    table = jnp.array([[0, 1, 2, 3], [1, 0, 2, 3], [2, 3, 1, 0], [3, 2, 1, 0]], I32)
    return lax.dynamic_slice_in_dim(table, here, 1, 0)[0]


def reduce_blocks(value, bits, index, size):
    for bit in bits:
        half = value.shape[0] // 2
        mine = (index >> bit) & 1
        sent = lax.dynamic_slice_in_dim(value, (1 - mine) * half, half, 0)
        kept = lax.dynamic_slice_in_dim(value, mine * half, half, 0)
        value = kept + along_dp(sent, bit, size)
    return value


def spread_blocks(value, bits, index, size):
    for bit in reversed(bits):
        mine = (index >> bit) & 1
        other = along_dp(value, bit, size)
        value = jnp.where(
            mine == 0,
            jnp.concatenate([value, other], axis=0),
            jnp.concatenate([other, value], axis=0),
        )
    return value


def sum_everywhere(value, bits, size):
    for bit in bits:
        value = value + along_dp(value, bit, size)
    value = value + along_z(value, SIDE)
    return value + along_z(value, CROSS)


def piece_place(index, order):
    place = 0
    for bit in order:
        place = 2 * place + ((index >> bit) & 1)
    return place


def rope_tables(offset):
    lane = jnp.arange(LANES, dtype=I32)
    row = jnp.arange(SEQ_LEN, dtype=I32)
    position = jnp.where(row < SEQ_LEN // 2, row + offset, row - offset).astype(F32)
    half = HEAD_DIM // 2
    frequency = 10000.0 ** (-(lane % half).astype(F32) / half)
    angles = position[:, None] * frequency[None, :]
    sign = jnp.where(lane % HEAD_DIM < half, -1.0, 1.0)
    return (jnp.cos(angles), jnp.sin(angles) * sign[None, :])


def swap_halves(value):
    half = HEAD_DIM // 2
    lane = lax.broadcasted_iota(I32, value.shape, 1)
    return jnp.where(
        lane % HEAD_DIM < half,
        pltpu.roll(value, LANES - half, 1),
        pltpu.roll(value, half, 1),
    )


def fill_bias(scalars, valid_ref, bias):
    offset, prefix = scalars[0], scalars[1]
    keys = lax.broadcasted_iota(I32, (SEQ_LEN, 1), 0)
    keys = jnp.where(keys < SEQ_LEN // 2, keys + offset, keys - offset)
    queries = lax.broadcasted_iota(I32, (1, SEQ_LEN), 1)
    queries = jnp.where(queries < SEQ_LEN // 2, queries + offset, queries - offset)
    seen = jnp.where(valid_ref[...] > 0, keys, SEQ_LEN)
    shown = ((seen <= queries) | (seen < prefix)) | (keys == queries)
    bias[...] = jnp.where(shown, 0.0, -1e30)


def head_lanes(value, head):
    lane = lax.broadcasted_iota(I32, value.shape, 1)
    return jnp.where((lane >= head * HEAD_DIM) & (lane < (head + 1) * HEAD_DIM), value, 0)


def attention_kernel(
    scalars, own, other, weights, w_out, cosine, sine, valid, *refs
):
    part_own, part_other, queries, keys, values, mixed, totals = refs[-11:-4]
    bias, key_rows, value_columns, total = refs[-4:]
    step = pl.program_id(0)
    half = SEQ_LEN // 2
    upper, lower = pl.ds(0, half), pl.ds(half, half)

    @pl.when(step == 0)
    def _():
        fill_bias(scalars, valid, bias)
        total[...] = jnp.zeros_like(total)

    for source, rows in ((own, upper), (other, lower)):
        x = source[...]
        for kind, target in ((0, queries), (1, keys), (2, values)):
            y = dot_nt(x, weights[kind])
            if kind < 2:
                y = y * cosine[rows, :] + swap_halves(y) * sine[rows, :]
            target[rows, :] = y.astype(BF16)
    key_rows[...] = keys[...]
    value_columns[...] = values[...].T

    @pl.loop(0, SEQ_LEN // QUERY_BLOCK)
    def _(index):
        columns = pl.ds(pl.multiple_of(index * QUERY_BLOCK, QUERY_BLOCK), QUERY_BLOCK)
        query = queries[columns, :] * 0.125
        outs = []
        for head in range(2):
            scores = dot_nt(key_rows[...], head_lanes(query, head)) + bias[:, columns]
            top = jnp.max(scores, axis=0, keepdims=True)
            raw = jnp.exp(scores - top)
            summed = jnp.sum(raw, axis=0, keepdims=True)
            shares = (raw * (1.0 / summed)).astype(BF16)
            outs.append(dot(value_columns[head * HEAD_DIM : (head + 1) * HEAD_DIM, :], shares))
            totals[0, head : head + 1, columns] = top + jnp.log(summed)
        mixed[columns, :] = jnp.concatenate(outs, axis=0).T.astype(BF16)

    total[...] += dot(mixed[...], w_out[...])

    @pl.when(step == pl.num_programs(0) - 1)
    def _():
        part_own[...] = total[upper, :].astype(BF16)
        part_other[...] = total[lower, :].astype(BF16)


def attention_specs(pairs, width):
    whole = lambda *shape: pl.BlockSpec(shape, lambda p, s: (0,) * len(shape))
    half = SEQ_LEN // 2
    rows = whole(half, width)
    weights = pl.BlockSpec((3, LANES, width), lambda p, s: (0, p, 0))
    w_out = pl.BlockSpec((LANES, width), lambda p, s: (p, 0))
    table = whole(SEQ_LEN, LANES)
    column = pl.BlockSpec((SEQ_LEN, LANES), lambda p, s: (0, p))
    totals = pl.BlockSpec((1, 8, SEQ_LEN), lambda p, s: (p, 0, 0))
    return (rows, weights, w_out, table, whole(SEQ_LEN, 1), column, totals)


def attention_forward(scalars, own, other, weights, w_out, cosine, sine, valid, ready):
    width = own.shape[1]
    pairs = weights.shape[1] // LANES
    rows, spec_w, spec_o, table, spec_v, column, totals = attention_specs(pairs, width)
    half = SEQ_LEN // 2
    shape = jax.ShapeDtypeStruct
    return pl.pallas_call(
        attention_kernel,
        grid_spec=pltpu.PrefetchScalarGridSpec(
            num_scalar_prefetch=1,
            grid=(pairs,),
            in_specs=[rows, rows, spec_w, spec_o, table, table, spec_v]
            + [pl.BlockSpec(memory_space=pl.ANY)] * len(ready),
            out_specs=[rows, rows, column, column, column, column, totals],
            scratch_shapes=[
                pltpu.VMEM((SEQ_LEN, SEQ_LEN), F32),
                pltpu.VMEM((SEQ_LEN, LANES), BF16),
                pltpu.VMEM((LANES, SEQ_LEN), BF16),
                pltpu.VMEM((SEQ_LEN, width), F32),
            ],
        ),
        out_shape=[
            shape((half, width), BF16),
            pltpu.HBM((half, width), BF16),
            *[pltpu.HBM((SEQ_LEN, pairs * LANES), BF16)] * 4,
            shape((pairs, 8, SEQ_LEN), F32),
        ],
        compiler_params=pltpu.CompilerParams(vmem_limit_bytes=48 * 2**20),
        cost_estimate=lasting(COST_FORWARD),
        name="attention_forward",
    )(scalars, own, other, weights, w_out, cosine, sine, valid, *ready)


def attention_back_kernel(
    scalars, own, other, weights, w_out, cosine, sine, valid,
    grad_own, grad_other, queries, keys, values, mixed, totals, *refs
):
    part_own, part_other, grad_w, grad_o, gain_row = refs[-12:-7]
    bias, grad_rows, key_columns, total, grad_q, grad_k, grad_v = refs[-7:]
    step = pl.program_id(0)
    half = SEQ_LEN // 2
    upper, lower = pl.ds(0, half), pl.ds(half, half)

    @pl.when(step == 0)
    def _():
        fill_bias(scalars, valid, bias)
        total[...] = jnp.zeros_like(total)

    grad_rows[upper, :] = dot_nt(grad_own[...], w_out[...]).astype(BF16)
    grad_rows[lower, :] = dot_nt(grad_other[...], w_out[...]).astype(BF16)
    columns_mixed = mixed[...].T
    grad_o[...] = (
        dot(columns_mixed[:, :half], grad_own[...]) + dot(columns_mixed[:, half:], grad_other[...])
    ).astype(BF16)
    key_columns[...] = keys[...].T
    grad_k[...] = jnp.zeros_like(grad_k)
    grad_v[...] = jnp.zeros_like(grad_v)

    @pl.loop(0, SEQ_LEN // QUERY_BLOCK)
    def _(index):
        columns = pl.ds(pl.multiple_of(index * QUERY_BLOCK, QUERY_BLOCK), QUERY_BLOCK)
        query = queries[columns, :] * 0.125
        grad = grad_rows[columns, :]
        outs = []
        for head in range(2):
            query_head = head_lanes(query, head)
            grad_head = head_lanes(grad, head)
            scores = dot_nt(keys[...], query_head) + bias[:, columns]
            shares = jnp.exp(scores - totals[0, head : head + 1, columns])
            grad_shares = dot_nt(values[...], grad_head)
            grad_v[...] += dot(shares.astype(BF16), grad_head)
            product = shares * grad_shares
            inner = jnp.sum(product, axis=0, keepdims=True)
            grad_scores = (product - shares * inner).astype(BF16)
            grad_k[...] += dot(grad_scores, query_head)
            outs.append(dot(key_columns[head * HEAD_DIM : (head + 1) * HEAD_DIM, :], grad_scores))
        grad_q[columns, :] = jnp.concatenate(outs, axis=0).T * 0.125

    for kind, source in ((0, grad_q), (1, grad_k), (2, grad_v)):
        y = source[...]
        if kind < 2:
            y = y * cosine[...] - swap_halves(y) * sine[...]
        y = y.astype(BF16)
        total[...] += dot(y, weights[kind])
        columns_y = y.T
        grad_w[kind] = (
            dot(columns_y[:, :half], own[...]) + dot(columns_y[:, half:], other[...])
        ).astype(BF16)

    @pl.when(step == pl.num_programs(0) - 1)
    def _():
        part_own[...] = total[upper, :].astype(BF16)
        part_other[...] = total[lower, :].astype(BF16)
        product = total[upper, :] * own[...].astype(F32) + total[lower, :] * other[...].astype(F32)
        gain_row[...] = jnp.sum(product.reshape(half // 8, 8, product.shape[1]), axis=0)


def attention_backward(
    scalars, own, other, weights, w_out, cosine, sine, valid, grad_own, grad_other, saved, ready
):
    width = own.shape[1]
    pairs = weights.shape[1] // LANES
    rows, spec_w, spec_o, table, spec_v, column, totals = attention_specs(pairs, width)
    half = SEQ_LEN // 2
    shape = jax.ShapeDtypeStruct
    return pl.pallas_call(
        attention_back_kernel,
        grid_spec=pltpu.PrefetchScalarGridSpec(
            num_scalar_prefetch=1,
            grid=(pairs,),
            in_specs=[
                rows, rows, spec_w, spec_o, table, table, spec_v,
                rows, rows, column, column, column, column, totals,
                *[pl.BlockSpec(memory_space=pl.ANY)] * len(ready),
            ],
            out_specs=[
                rows,
                rows,
                spec_w,
                spec_o,
                pl.BlockSpec((8, width), lambda p, s: (0, 0)),
            ],
            scratch_shapes=[
                pltpu.VMEM((SEQ_LEN, SEQ_LEN), F32),
                pltpu.VMEM((SEQ_LEN, LANES), BF16),
                pltpu.VMEM((LANES, SEQ_LEN), BF16),
                pltpu.VMEM((SEQ_LEN, width), F32),
                *[pltpu.VMEM((SEQ_LEN, LANES), F32)] * 3,
            ],
        ),
        out_shape=[
            shape((half, width), BF16),
            pltpu.HBM((half, width), BF16),
            shape((3, pairs * LANES, width), BF16),
            shape((pairs * LANES, width), BF16),
            shape((8, width), F32),
        ],
        compiler_params=pltpu.CompilerParams(vmem_limit_bytes=48 * 2**20),
        cost_estimate=lasting(COST_BACKWARD),
        name="attention_backward",
    )(
        scalars, own, other, weights, w_out, cosine, sine, valid, grad_own, grad_other, *saved, *ready
    )


def most_tiles(rows):
    return (2 * rows + EXP_FFN * (TILE - 1)) // TILE


def most_groups(tiles, experts):
    return (tiles + experts * (GROUP - 1)) // GROUP


def expert_plan(routes, valid, chunks):
    tokens = routes.shape[0]
    rows = tokens // chunks
    tiles = most_tiles(rows)
    numbers = jnp.arange(8, dtype=I32)[:, None]
    named = ((routes[:, 0][None, :] == numbers) | (routes[:, 1][None, :] == numbers)) & (
        valid[None, :] > 0
    )
    named = (named & (numbers < EXP_FFN)).reshape(8 * chunks, rows)
    before = (jnp.arange(rows)[:, None] < jnp.arange(rows)[None, :]).astype(BF16)
    place = dot(named.astype(BF16), before).astype(I32)
    place = jnp.where(named, place, -1).reshape(8, chunks, rows)
    count = jnp.sum(named.astype(I32), axis=1).reshape(8, chunks)[:EXP_FFN]
    number = (count + TILE - 1) // TILE
    number = jnp.where(jnp.arange(chunks)[None, :] == 0, jnp.maximum(number, 1), number)
    earlier = jnp.arange(EXP_FFN)[:, None] > jnp.arange(EXP_FFN)[None, :]
    first = jnp.sum(jnp.where(earlier[:, :, None], number[None], 0), axis=1)
    total = jnp.sum(number, axis=0)
    slot = jnp.arange(tiles, dtype=I32)
    expert = jnp.sum((first + number)[:, :, None] <= slot, axis=0)
    expert = jnp.minimum(expert, EXP_FFN - 1)
    pick = jnp.arange(EXP_FFN)[:, None, None] == expert[None]
    base = (slot - jnp.sum(jnp.where(pick, first[:, :, None], 0), axis=0)) * TILE
    meta = jnp.concatenate([expert, base, total[:, None], first.T, number.T], axis=1).astype(I32)
    return (place.transpose(1, 0, 2), meta.reshape(-1), number, first)


def expert_kernel(
    tiles, span, sources, meta, chunk, place, carry, routes, w_router, w_up_all, w_down_all, *refs
):
    taken = refs[: sum(map(len, sources))]
    part, feed, x_out, hidden_out, grad_out, both_out = refs[-18:-12]
    rows = feed.shape[0]
    width = feed.shape[1]
    table, hits, picked, back, total, hidden_rows, grad_rows, both_rows = refs[-12:-4]
    w_up, w_down, load_sems, save_sems = refs[-4:]
    hidden_width = w_down.shape[1]
    offset = chunk[0] * span
    number = meta[offset + 2 * tiles]
    groups = (number + GATHER - 1) // GATHER
    span_rows = GATHER * TILE

    def loads(expert):
        slot = lax.rem(expert, 2)
        return (
            pltpu.make_async_copy(w_up_all.at[expert], w_up.at[slot], load_sems.at[slot, 0]),
            pltpu.make_async_copy(w_down_all.at[expert], w_down.at[slot], load_sems.at[slot, 1]),
        )

    def saves(tile):
        source = pl.ds(pl.multiple_of(tile * TILE, TILE), TILE)
        goal = pl.ds(pl.multiple_of((chunk[0] * tiles + tile) * TILE, TILE), TILE)
        pairs = (
            (picked.at[source, pl.ds(0, width)], x_out),
            (hidden_rows.at[source], hidden_out),
            (grad_rows.at[source], grad_out),
            (both_rows.at[source], both_out),
        )
        return [
            pltpu.make_async_copy(ref, out.at[goal], save_sems.at[tile, k])
            for k, (ref, out) in enumerate(pairs)
        ]

    for copy in loads(0):
        copy.start()

    first = 0
    for option, group in enumerate(sources):
        refs_here = taken[first : first + len(group)]
        first += len(group)

        @pl.when(chunk[1] == option)
        def _(refs_here=refs_here, group=group):
            at = {"x": 0, "cot": 0}
            for ref, kind in zip(refs_here, group):
                columns = pl.ds(0 if kind == "x" else width + LANES, width)
                table[pl.ds(at[kind], ref.shape[0]), columns] = ref[...]
                at[kind] += ref.shape[0]

    logits = dot(table[:, :width], w_router[...]) + carry[0]
    lane = lax.broadcasted_iota(I32, logits.shape, 1)
    one, two = lane == routes[0, :, 0:1], lane == routes[0, :, 1:2]
    score_one = jnp.sum(jnp.where(one, logits, 0.0), axis=1, keepdims=True)
    score_two = jnp.sum(jnp.where(two, logits, 0.0), axis=1, keepdims=True)
    top = jnp.maximum(score_one, score_two)
    score_one, score_two = jnp.exp(score_one - top), jnp.exp(score_two - top)
    both = score_one + score_two
    gates = jnp.where(one, score_one / both, 0.0) + jnp.where(two, score_two / both, 0.0)
    high = gates.astype(BF16).astype(F32)
    low = gates - high
    table[:, width : width + LANES] = (high + pltpu.roll(low, LANES // 2, 1)).astype(BF16)
    total[...] = jnp.zeros_like(total)

    @pl.loop(0, groups)
    def _(group):
        for at in range(GATHER):
            tile = group * GATHER + at
            slot = jnp.minimum(tile, tiles - 1)
            base = jnp.where(tile < number, meta[offset + tiles + slot], rows)
            row = lax.broadcasted_iota(I32, (TILE, rows), 0) + base
            hit = place[0, pl.ds(meta[offset + slot], 1), :] == row
            goal = pl.ds(pl.multiple_of(tile * TILE, TILE), TILE)
            hits[goal, :] = jnp.where(hit, 1.0, 0.0).astype(BF16)

            @pl.when(tile >= number)
            def _():
                back[goal, :] = jnp.zeros((TILE, back.shape[1]), BF16)

        here = pl.ds(pl.multiple_of(group * span_rows, TILE), span_rows)
        picked[here, :] = dot(hits[here, :], table[...]).astype(BF16)

    @pl.loop(0, EXP_FFN)
    def _(expert):
        slot = lax.rem(expert, 2)
        for copy in loads(expert):
            copy.wait()

        @pl.when(expert + 1 < EXP_FFN)
        def _():
            for copy in loads(expert + 1):
                copy.start()

        start = meta[offset + 2 * tiles + 1 + expert]
        amount = meta[offset + 2 * tiles + 1 + EXP_FFN + expert]

        @pl.loop(start, start + amount)
        def _(tile):
            mine = pl.ds(pl.multiple_of(tile * TILE, TILE), TILE)
            inputs = picked[mine, :width]
            lane = lax.broadcasted_iota(I32, (TILE, LANES), 1)
            own = (lane == expert) | (lane == expert + LANES // 2)
            scale = jnp.sum(
                jnp.where(own, picked[mine, width : width + LANES].astype(F32), 0.0),
                axis=1,
                keepdims=True,
            )
            upstream = picked[mine, width + LANES :].astype(F32)
            both = dot(inputs, w_up[slot])
            gate, up = both[:, :hidden_width], both[:, hidden_width:]
            sigma = 1.0 / (1.0 + jnp.exp(-gate))
            active = gate * sigma
            hidden = (active * up).astype(BF16)
            outputs = dot(hidden, w_down[slot])
            gate_term = jnp.sum(upstream * outputs, axis=1, keepdims=True)
            grad_row = (upstream * scale).astype(BF16)
            grad_hidden = dot_nt(grad_row, w_down[slot])
            grad_gate = (grad_hidden * up * sigma * (1.0 + gate * (1.0 - sigma))).astype(BF16)
            grad_up = (grad_hidden * active).astype(BF16)
            grad_both = jnp.concatenate([grad_gate, grad_up], axis=1)
            grad_x = dot_nt(grad_both, w_up[slot])
            hidden_rows[mine, :] = hidden
            grad_rows[mine, :] = grad_row
            both_rows[mine, :] = grad_both
            for copy in saves(tile):
                copy.start()
            back[mine, :width] = (outputs * scale).astype(BF16)
            back[mine, width : 2 * width] = grad_x.astype(BF16)
            back[mine, 2 * width :] = jnp.where(lane == expert, gate_term, 0.0).astype(BF16)

    @pl.loop(0, groups)
    def _(group):
        here = pl.ds(pl.multiple_of(group * span_rows, TILE), span_rows)
        total[...] += dot_tn(hits[here, :], back[here, :])

    feed[...] = total[:, :width].astype(BF16)
    part[:rows, :] = total[:, width : 2 * width].astype(BF16)
    terms = total[:, 2 * width :].T[:16]
    part[rows:, :] = jnp.concatenate([terms, jnp.zeros((16, width - rows), F32)], axis=1).astype(
        BF16
    )

    @pl.loop(0, number)
    def _(tile):
        for copy in saves(tile):
            copy.wait()


def expert_chunk(meta, chunk, options, place, carry, routes, w_router, w_up, w_down, saved):
    rows, width = options[0]["x"][0].shape
    sources = [[kind for kind in ("x", "cot") for _ in option[kind]] for option in options]
    taken = [ref for option in options for kind in ("x", "cot") for ref in option[kind]]
    chunks = place.shape[0]
    hidden_width = w_down.shape[1]
    tiles = most_tiles(rows)
    span = 2 * tiles + 1 + 2 * EXP_FFN
    held = (tiles + GATHER - 1) // GATHER * GATHER * TILE
    shape = jax.ShapeDtypeStruct
    whole = lambda *dims: pl.BlockSpec(dims, lambda i, m, c: (0,) * len(dims))
    mine = lambda *dims: pl.BlockSpec((1, *dims), lambda i, m, c: (c[0], 0, 0))
    stay = pl.BlockSpec(memory_space=pl.ANY)
    columns = (width, hidden_width, width, 2 * hidden_width)
    extra = () if saved is None else tuple(saved)
    return pl.pallas_call(
        functools.partial(expert_kernel, tiles, span, sources),
        grid_spec=pltpu.PrefetchScalarGridSpec(
            num_scalar_prefetch=2,
            grid=(1,),
            in_specs=[
                mine(8, rows),
                mine(rows, LANES),
                mine(rows, 2),
                whole(width, LANES),
                stay,
                stay,
                *[whole(*ref.shape) for ref in taken],
                *[stay] * len(extra),
            ],
            out_specs=[whole(rows + 16, width), whole(rows, width), *[stay] * len(columns)],
            scratch_shapes=[
                pltpu.VMEM((rows, 2 * width + LANES), BF16),
                pltpu.VMEM((held, rows), BF16),
                pltpu.VMEM((held, 2 * width + LANES), BF16),
                pltpu.VMEM((held, 2 * width + LANES), BF16),
                pltpu.VMEM((rows, 2 * width + LANES), F32),
                *[pltpu.VMEM((held, c), BF16) for c in columns[1:]],
                pltpu.VMEM((2, width, 2 * hidden_width), BF16),
                pltpu.VMEM((2, hidden_width, width), BF16),
                pltpu.SemaphoreType.DMA((2, 2)),
                pltpu.SemaphoreType.DMA((tiles, len(columns))),
            ],
        ),
        out_shape=[
            pltpu.HBM((rows + 16, width), BF16),
            pltpu.HBM((rows, width), BF16),
            *[shape((chunks * tiles * TILE, c), BF16) for c in columns],
        ],
        input_output_aliases={8 + len(taken) + k: 2 + k for k in range(len(extra))},
        compiler_params=pltpu.CompilerParams(vmem_limit_bytes=52 * 2**20),
        cost_estimate=lasting(COST_EXPERT),
        name="expert_chunk",
    )(meta, chunk, place, carry, routes, w_router, w_up, w_down, *taken, *extra)


def grad_walk(number, first, tiles, half):
    experts, chunks = number.shape[0] // 2, number.shape[1]
    number = lax.dynamic_slice_in_dim(number, half * experts, experts, 0)
    first = lax.dynamic_slice_in_dim(first, half * experts, experts, 0)
    flat = number.reshape(-1)
    groups = flat.shape[0]
    earlier = jnp.arange(groups)[:, None] > jnp.arange(groups)[None, :]
    start = jnp.sum(jnp.where(earlier, flat[None, :], 0), axis=1)
    held = jnp.sum(number, axis=1)
    held_groups = (held + GROUP - 1) // GROUP
    earlier = jnp.arange(experts)[:, None] > jnp.arange(experts)[None, :]
    held_start = jnp.sum(jnp.where(earlier, held[None, :], 0), axis=1)
    group_start = jnp.sum(jnp.where(earlier, held_groups[None, :], 0), axis=1)
    steps = most_groups(chunks * tiles, experts)
    everything = jnp.sum(held_groups)
    step = jnp.minimum(jnp.arange(steps, dtype=I32), everything - 1)
    owner = jnp.sum((group_start + held_groups)[:, None] <= step[None, :], axis=0)
    pick = jnp.arange(experts)[:, None] == owner[None, :]
    look = lambda values: jnp.sum(jnp.where(pick, values[:, None], 0), axis=0)
    done = (step - look(group_start)) * GROUP
    left = look(held) - done
    place_in = done[:, None] + jnp.minimum(jnp.arange(GROUP)[None, :], left[:, None] - 1)
    spot = (look(held_start)[:, None] + place_in).reshape(-1)
    group = jnp.sum((start + flat)[:, None] <= spot[None, :], axis=0)
    pick = jnp.arange(groups)[:, None] == group[None, :]
    offset = jnp.arange(chunks)[None, :] * tiles + first
    block = jnp.sum(jnp.where(pick, (offset.reshape(-1) - start)[:, None], 0), axis=0) + spot
    return jnp.concatenate([owner, block, left, everything[None]]).astype(I32)


def weight_grad_kernel(steps, walk, *refs):
    kept, (grad_up, grad_down) = refs[:4], refs[4:6]
    rows, (sum_up, sum_down, out_up, out_down, load_sems, save_sems) = refs[6:10], refs[10:]
    number = walk[(2 + GROUP) * steps]
    width, hidden_width = sum_up.shape[0], sum_down.shape[0]

    def loads(step):
        slot = lax.rem(step, 2)
        copies = []
        for at in range(GROUP):
            block = walk[steps + step * GROUP + at]
            source = pl.ds(pl.multiple_of(block * TILE, TILE), TILE)
            for kind in range(4):
                copies.append(
                    pltpu.make_async_copy(
                        kept[kind].at[source],
                        rows[kind].at[slot, pl.ds(at * TILE, TILE)],
                        load_sems.at[slot, at, kind],
                    )
                )
        return copies

    def saves(expert):
        slot = lax.rem(expert, 2)
        up_rows = pl.ds(pl.multiple_of(expert * width, width), width)
        down_rows = pl.ds(pl.multiple_of(expert * hidden_width, hidden_width), hidden_width)
        return (
            pltpu.make_async_copy(out_up.at[slot], grad_up.at[up_rows], save_sems.at[slot, 0]),
            pltpu.make_async_copy(out_down.at[slot], grad_down.at[down_rows], save_sems.at[slot, 1]),
        )

    for copy in loads(0):
        copy.start()

    @pl.loop(0, number)
    def _(step):
        slot = lax.rem(step, 2)
        expert = walk[step]
        left = walk[(1 + GROUP) * steps + step]
        for copy in loads(step):
            copy.wait()

        @pl.when(step + 1 < number)
        def _():
            for copy in loads(step + 1):
                copy.start()

        row = lax.broadcasted_iota(I32, (GROUP * TILE, 1), 0)
        live = row < left * TILE
        side = lax.rem(expert, 2)

        def products():
            return (
                dot_tn(jnp.where(live, rows[0][slot], 0), rows[3][slot]),
                dot_tn(jnp.where(live, rows[1][slot], 0), rows[2][slot]),
            )

        fresh = (step == 0) | (walk[jnp.maximum(step - 1, 0)] != expert)
        done = (step == number - 1) | (walk[jnp.minimum(step + 1, steps - 1)] != expert)

        @pl.when(done & (expert >= 2))
        def _():
            for copy in saves(expert - 2):
                copy.wait()

        @pl.when(fresh & done)
        def _():
            up, down = products()
            out_up[side], out_down[side] = up.astype(BF16), down.astype(BF16)

        @pl.when(fresh & jnp.logical_not(done))
        def _():
            sum_up[...], sum_down[...] = products()

        @pl.when(jnp.logical_not(fresh | done))
        def _():
            up, down = products()
            sum_up[...] += up
            sum_down[...] += down

        @pl.when(jnp.logical_not(fresh) & done)
        def _():
            up, down = products()
            out_up[side] = (sum_up[...] + up).astype(BF16)
            out_down[side] = (sum_down[...] + down).astype(BF16)

        @pl.when(done)
        def _():
            for copy in saves(expert):
                copy.start()

    for expert in (EXP_FFN // 2 - 2, EXP_FFN // 2 - 1):
        for copy in saves(expert):
            copy.wait()


def weight_grads(walk, saved):
    width, hidden_width = saved[0].shape[1], saved[1].shape[1]
    experts = EXP_FFN // 2
    steps = most_groups(saved[0].shape[0] // TILE, experts)
    shape = jax.ShapeDtypeStruct
    stay = pl.BlockSpec(memory_space=pl.ANY)
    return pl.pallas_call(
        functools.partial(weight_grad_kernel, steps),
        grid_spec=pltpu.PrefetchScalarGridSpec(
            num_scalar_prefetch=1,
            grid=(1,),
            in_specs=[stay] * 4,
            out_specs=[stay] * 2,
            scratch_shapes=[
                *[pltpu.VMEM((2, GROUP * TILE, kept.shape[1]), BF16) for kept in saved],
                pltpu.VMEM((width, 2 * hidden_width), F32),
                pltpu.VMEM((hidden_width, width), F32),
                pltpu.VMEM((2, width, 2 * hidden_width), BF16),
                pltpu.VMEM((2, hidden_width, width), BF16),
                pltpu.SemaphoreType.DMA((2, GROUP, 4)),
                pltpu.SemaphoreType.DMA((2, 2)),
            ],
        ),
        out_shape=[
            shape((experts * width, 2 * hidden_width), BF16),
            shape((experts * hidden_width, width), BF16),
        ],
        compiler_params=pltpu.CompilerParams(vmem_limit_bytes=48 * 2**20),
        cost_estimate=lasting(COST_GRADS),
        name="weight_grads",
    )(walk, *saved)


def combine_kernel(scalars, own_send, far_send, own_keep, far_keep, *refs):
    send, keep = refs[-2:]
    send[...] = own_send[...] + far_send[...]
    keep[...] = own_keep[...] + far_keep[...]


def combine(own, far, bit, start, rows, ready):
    columns = own.shape[1]
    half = rows // 2
    block = min(half, 384)
    number = half // block
    place = lambda side: pl.BlockSpec(
        (block, columns), lambda i, b: (start // block + (b[0] if side else 1 - b[0]) * number + i, 0)
    )
    out = pl.BlockSpec((block, columns), lambda i, b: (i, 0))
    shape = jax.ShapeDtypeStruct((half, columns), own.dtype)
    return pl.pallas_call(
        combine_kernel,
        grid_spec=pltpu.PrefetchScalarGridSpec(
            num_scalar_prefetch=1,
            grid=(number,),
            in_specs=[place(False), place(False), place(True), place(True)]
            + [pl.BlockSpec(memory_space=pl.ANY)] * len(ready),
            out_specs=[out, out],
        ),
        out_shape=[shape, shape],
        compiler_params=pltpu.CompilerParams(vmem_limit_bytes=32 * 2**20),
        cost_estimate=lasting(COST_ADD),
        name="combine",
    )(bit, own, far, own, far, *ready)


def widen_kernel(source, *refs):
    refs[-1][...] = source[...].astype(F32)


def widen(source, half, target):
    rows, columns = source.shape
    block = 768
    number = rows // block
    extra = () if target is None else (target,)
    return pl.pallas_call(
        widen_kernel,
        grid=(number,),
        in_specs=[pl.BlockSpec((block, columns), lambda i: (i, 0))]
        + [pl.BlockSpec(memory_space=pl.ANY)] * len(extra),
        out_specs=pl.BlockSpec((block, columns), lambda i: (half * number + i, 0)),
        out_shape=jax.ShapeDtypeStruct((2 * rows, columns), F32),
        input_output_aliases={1: 0} if extra else {},
        compiler_params=pltpu.CompilerParams(vmem_limit_bytes=48 * 2**20),
        cost_estimate=lasting(COST_WIDEN),
        name="widen",
    )(source, *extra)


def widen_pairs_kernel(source, *refs):
    target = refs[-1]
    rows, columns = source.shape
    for row in range(columns // LANES):
        at = row % 2 * (columns // 2) + row // 2 * LANES
        target[pl.ds(row, rows, stride=columns // LANES), :] = source[:, at : at + LANES].astype(F32)


def widen_pairs(source, half, target):
    rows, columns = source.shape
    block = 768
    number = rows // block
    extra = () if target is None else (target,)
    split = columns // LANES
    return pl.pallas_call(
        widen_pairs_kernel,
        grid=(number,),
        in_specs=[pl.BlockSpec((block, columns), lambda i: (i, 0))]
        + [pl.BlockSpec(memory_space=pl.ANY)] * len(extra),
        out_specs=pl.BlockSpec((block * split, LANES), lambda i: (half * number + i, 0)),
        out_shape=jax.ShapeDtypeStruct((2 * rows * split, LANES), F32),
        input_output_aliases={1: 0} if extra else {},
        compiler_params=pltpu.CompilerParams(vmem_limit_bytes=48 * 2**20),
        cost_estimate=lasting(COST_WIDEN),
        name="widen_pairs",
    )(source, *extra)


def shards(
    dp_size,
    stream,
    cotangent,
    gain_attention,
    w_inputs,
    w_output,
    gain_experts,
    w_router,
    w_carry,
    w_gate_up,
    w_down,
    w_constant,
    constant_vectors,
    previous_logits,
    routes,
    valid,
    prefix,
):
    rows, width = stream.shape
    tokens = routes.shape[0]
    chunks = tokens // rows
    head_columns = w_inputs.shape[2]
    here = lax.axis_index("tensor")
    index = lax.axis_index("dp")
    outer = (here == 0) | (here == chunks - 1)
    bits = list(range(dp_size.bit_length() - 1))
    first_row = here * rows
    valid_all = valid.astype(F32)
    cut = lambda array, at: lax.dynamic_slice_in_dim(array, at, rows, 0)
    valid_here = cut(valid_all, first_row)
    routes_here = cut(routes, first_row)
    previous_here = cut(previous_logits, first_row)

    w_in_rows = w_inputs.transpose(0, 2, 1)
    packed = jnp.concatenate([w_in_rows, w_output[None]], axis=0).reshape(-1, width)
    piece_rows = packed.shape[0] // dp_size
    position = (index >> 1) | ((index & 1) << (len(bits) - 1))
    piece = lax.dynamic_slice_in_dim(packed, position * piece_rows, piece_rows, 0)
    normed_here, inverse_one = norm_forward(stream, gain_attention)
    normed_low = normed_here.astype(BF16)
    normed_other = along_z(normed_low, SIDE)
    piece = along_z(piece, CROSS)
    cot_low = behind(cotangent, piece).astype(BF16)
    cot_side, cot_middle = along_z(cot_low, SIDE), along_z(cot_low, MIDDLE)
    for level, bit in enumerate([*bits[1:], bits[0]]):
        if level == 0:
            place, meta, number, first = expert_plan(*behind((routes, valid), piece), chunks)
        if level == 1:
            number, first = behind((number, first), piece)
            walks = [grad_walk(number, first, most_tiles(rows), half) for half in range(2)]
        other = along_dp(piece, bit, dp_size)
        piece = jnp.where(
            (index >> bit) & 1 == 0,
            jnp.concatenate([piece, other], axis=0),
            jnp.concatenate([other, piece], axis=0),
        )
    carry = jnp.dot(behind(previous_logits, place), w_carry, precision=HIGHEST, preferred_element_type=F32)
    columns = carry.shape[1]
    carry_wide = jnp.pad(carry, ((0, 0), (0, LANES - columns))).reshape(chunks, rows, LANES)
    routes_live = jnp.where(valid[:, None] > 0, routes, -1).reshape(chunks, rows, 2)
    router_wide = jnp.pad(w_router, ((0, 0), (0, LANES - columns)))
    partner = piece.reshape(4, head_columns, width)
    both_in = jnp.concatenate([w_in_rows, partner[:3]], axis=1)
    both_out = jnp.concatenate([w_output, partner[3]], axis=0)

    core = index & 1
    offset = (here % 2) * rows
    sequence = here // 2
    scalars = jnp.stack([offset, prefix[sequence]]).astype(I32)
    cosine, sine = rope_tables(offset)
    valid_rows = jnp.concatenate([cut(valid, first_row), cut(valid, (here ^ 1) * rows)])[:, None]
    fixed = (both_in, both_out, cosine, sine, valid_rows)
    ready = (place, meta, *walks, cot_side, cot_middle, carry_wide, routes_live, router_wide)
    part_own, part_other, *saved_attention = attention_forward(
        scalars, normed_low, normed_other, *fixed, ready
    )
    attention_other = along_z(part_other, SIDE)

    cot_far, cot_across = along_z(cot_middle, OUTWARD), along_z(cot_side, MIDDLE)
    cot_far, cot_across = behind((cot_far, cot_across), part_own)
    w_up = behind(w_gate_up, (part_own, cot_far, cot_across)).reshape(EXP_FFN, width, -1)
    attention_other = behind(attention_other, w_up)
    attention = part_own.astype(F32) + attention_other.astype(F32)
    middle = stream + attention
    second, inverse_two = norm_forward(middle, gain_experts)
    second_low = second.astype(BF16)

    which = slot_chunks(here)

    def chunk(slot, options, saved):
        choice = outer.astype(I32) * (len(options) - 1)
        return expert_chunk(
            meta,
            jnp.stack([which[slot], choice]),
            options,
            place,
            carry_wide,
            routes_live,
            router_wide,
            w_up,
            w_down,
            saved,
        )

    third_rows = rows // 3 // 16 * 16
    cuts = (0, third_rows, 2 * third_rows, rows)
    cot_pieces = [cot_across[low:high] for low, high in zip(cuts[:-1], cuts[1:])]
    side, middle_rows = along_z(second_low, SIDE), along_z(second_low, MIDDLE)
    cot_last = [along_z(behind(cot_pieces[0], second_low), OUTWARD)]
    part_0, feed_0, *saved = chunk(0, [{"x": [second_low], "cot": [cot_low]}], None)
    side, middle_rows, cot_last[0] = behind((side, middle_rows, cot_last[0]), part_0)
    far, across = along_z(middle_rows, OUTWARD), along_z(side, MIDDLE)
    cot_last.append(along_z(behind(cot_pieces[1], part_0), OUTWARD))
    part_1, feed_1, *saved = chunk(1, [{"x": [side], "cot": [cot_side]}], saved)
    near = along_z(part_1, INWARD)
    far, across, cot_last[1] = behind((far, across, cot_last[1]), part_1)
    last = along_z(across, OUTWARD)
    cot_last.append(along_z(behind(cot_pieces[2], part_1), OUTWARD))
    part_2, feed_2, *saved = chunk(
        2, [{"x": [middle_rows], "cot": [cot_middle]}, {"x": [far], "cot": [cot_far]}], saved
    )
    third = along_z(part_2, INWARD)
    last, cot_last[2] = behind((last, cot_last[2]), part_2)
    part_3, feed_3, *saved = chunk(
        3,
        [{"x": [across], "cot": [cot_across]}, {"x": [last], "cot": cot_last}],
        saved,
    )

    inward = along_z(part_3, INWARD)
    up_low, down_low = weight_grads(walks[0], saved)
    inward = part_3 + behind(inward, up_low)
    inward = along_z(inward, MIDDLE)
    third = along_z(part_2 + third, MIDDLE)
    up_high, down_high = weight_grads(walks[1], saved)
    outward_sum = part_1 + behind(inward, up_high)
    outward = along_z(outward_sum, OUTWARD)
    up_low, up_high, down_low, down_high = lax.psum((up_low, up_high, down_low, down_high), "dp")
    summed = part_0.astype(F32) + near.astype(F32) + third.astype(F32) + outward.astype(F32)

    logits = dot(second_low, w_router) + cut(carry, first_row)
    picked = routes_here[:, :, None] == jnp.arange(columns, dtype=I32)[None, None, :]
    chosen = jnp.sum(jnp.where(picked, logits[:, None, :], 0.0), axis=-1)
    gates_here = jax.nn.softmax(chosen, axis=-1)
    live_gates = gates_here * valid_here[:, None]
    copy_gate = jnp.sum(jnp.where(routes_here == EXP_FFN + 1, live_gates, 0.0), axis=-1)
    constant_gates = jnp.stack(
        [
            jnp.sum(jnp.where(routes_here == EXP_FFN + 2 + number, live_gates, 0.0), axis=-1)
            for number in range(2)
        ],
        axis=1,
    )
    alphas = jax.nn.softmax(
        jnp.einsum("td,cad->tca", second, w_constant, precision=HIGHEST, preferred_element_type=F32),
        axis=-1,
    )
    constant_out = (
        alphas[:, :, 0:1] * second[:, None, :] + alphas[:, :, 1:2] * constant_vectors[None, :, :]
    )
    extra = copy_gate[:, None] * second + jnp.sum(
        constant_gates[:, :, None] * constant_out, axis=1
    )
    copy_terms = jnp.sum(cotangent * second, axis=-1)
    constant_terms = jnp.sum(cotangent[:, None, :] * constant_out, axis=-1)
    grad_constant_out = constant_gates[:, :, None] * cotangent[:, None, :]
    grad_vectors = jnp.sum(alphas[:, :, 1:2] * grad_constant_out, axis=0)
    grad_alphas = jnp.stack(
        [
            jnp.sum(grad_constant_out * second[:, None, :], axis=-1),
            jnp.sum(grad_constant_out * constant_vectors[None, :, :], axis=-1),
        ],
        axis=-1,
    )
    grad_mix = alphas * (grad_alphas - jnp.sum(alphas * grad_alphas, axis=-1, keepdims=True))
    grad_constant = jnp.einsum(
        "tca,td->cad", grad_mix, second, precision=HIGHEST, preferred_element_type=F32
    )
    grad_local = (
        copy_gate[:, None] * cotangent
        + jnp.sum(alphas[:, :, 0:1] * grad_constant_out, axis=1)
        + jnp.einsum(
            "tca,cad->td", grad_mix, w_constant, precision=HIGHEST, preferred_element_type=F32
        )
    )

    gate_grads = summed[rows : rows + EXP_FFN, :rows].T
    gate_table = jnp.concatenate(
        [gate_grads, jnp.zeros((rows, 1), F32), copy_terms[:, None], constant_terms], axis=1
    )
    grad_gates = jnp.sum(jnp.where(picked, gate_table[:, None, :], 0.0), axis=-1)
    grad_gates = grad_gates * valid_here[:, None]
    grad_chosen = gates_here * (
        grad_gates - jnp.sum(gates_here * grad_gates, axis=-1, keepdims=True)
    )
    grad_logits = jnp.sum(jnp.where(picked, grad_chosen[:, :, None], 0.0), axis=1)
    grad_router = jnp.dot(
        second_low.astype(F32).T, grad_logits, precision=HIGHEST, preferred_element_type=F32
    )
    grad_carry = jnp.dot(
        previous_here.T, grad_logits, precision=HIGHEST, preferred_element_type=F32
    )
    grad_previous = jnp.dot(
        grad_logits, w_carry.T, precision=HIGHEST, preferred_element_type=F32
    )
    grad_second = (
        summed[:rows]
        + grad_local
        + jnp.dot(
            grad_logits, w_router.astype(F32).T, precision=HIGHEST, preferred_element_type=F32
        )
    )
    grad_gain_experts = jnp.sum(grad_second * middle * inverse_two, axis=0)
    grad_middle = cotangent + norm_backward(middle, inverse_two, gain_experts, grad_second)

    grad_low = grad_middle.astype(BF16)
    grad_other = along_z(grad_low, SIDE)

    part_own, part_other, grad_w, grad_o, gain_rows = attention_backward(
        scalars, normed_low, normed_other, *fixed, grad_low, grad_other, saved_attention, ()
    )
    grad_normed = part_own.astype(F32) + along_z(part_other, SIDE).astype(F32)
    grad_stream = grad_middle + norm_backward(stream, inverse_one, gain_attention, grad_normed)

    feed_1, feed_2, feed_3 = behind((feed_1, feed_2, feed_3), grad_low)
    near = along_z(feed_1, INWARD)
    third = along_z(feed_2 + along_z(feed_2, INWARD), MIDDLE)
    outward = along_z(feed_3 + along_z(feed_3, INWARD), MIDDLE)
    outward = along_z(feed_1 + outward, OUTWARD)
    feed = feed_0.astype(F32) + near.astype(F32) + third.astype(F32) + outward.astype(F32)
    experts = feed + extra
    block_out = middle + experts
    squares = [
        jnp.sum(valid_here[:, None] * part * part) for part in (block_out, attention, experts)
    ]
    squares = jnp.stack([*squares, jnp.sum(valid_here)])

    grad_down = widen(down_high, 1, widen(down_low, 0, None))
    grad_down = grad_down.reshape(EXP_FFN, -1, width)
    grad_gate_up = widen_pairs(up_high, 1, widen_pairs(up_low, 0, None))
    tiles = up_low.shape[1] // (2 * LANES)
    grad_gate_up = grad_gate_up.reshape(EXP_FFN, width, tiles, 2, LANES).transpose(0, 1, 3, 2, 4)
    grad_gate_up = grad_gate_up.reshape(EXP_FFN, width, 2, -1)

    own_grads = jnp.concatenate([grad_w[:, :head_columns], grad_o[None, :head_columns]], axis=0)
    far_grads = jnp.concatenate([grad_w[:, head_columns:], grad_o[None, head_columns:]], axis=0)
    order = bits
    own_piece = reduce_blocks(own_grads.reshape(-1, width), order, index, dp_size)
    far_piece = reduce_blocks(far_grads.reshape(-1, width), order, index, dp_size)
    own_piece = own_piece + along_z(far_piece, CROSS)
    attention_grads = spread_blocks(own_piece, order, index, dp_size).astype(F32)
    attention_grads = attention_grads.reshape(4, head_columns, width)
    grad_inputs = attention_grads[:3].transpose(0, 2, 1)
    grad_output = attention_grads[3]

    wide = lambda array: jnp.pad(array, ((0, 0), (0, width - array.shape[1])))
    small = jnp.concatenate(
        [
            grad_gain_experts[None],
            grad_router.T,
            wide(grad_carry),
            grad_constant.reshape(-1, width),
            grad_vectors,
            wide(squares[None]),
            jnp.sum(gain_rows, axis=0, keepdims=True) / gain_attention[None],
        ],
        axis=0,
    )
    small = sum_everywhere(small, bits, dp_size)
    at = 1 + 2 * columns
    squares = small[at + 6, :3]
    counted = small[at + 6, 3]
    rms_values = jnp.sqrt(squares / (jnp.maximum(counted, 1.0) * width))
    return (
        block_out,
        grad_stream,
        small[at + 7],
        grad_inputs,
        grad_output,
        small[0],
        small[1 : 1 + columns].T,
        small[1 + columns : at, :columns],
        grad_gate_up,
        grad_down,
        small[at : at + 4].reshape(2, 2, width),
        small[at + 4 : at + 6],
        grad_previous,
        rms_values,
    )


def solution(mesh):
    return jax.shard_map(
        functools.partial(shards, mesh.shape["dp"]),
        mesh=mesh,
        in_specs=(
            P(("dp", "tensor"), None),
            P(("dp", "tensor"), None),
            P(),
            P(None, None, "tensor"),
            P("tensor", None),
            P(),
            P(),
            P(),
            P(None, None, None, "tensor"),
            P(None, "tensor", None),
            P(),
            P(),
            P("dp", None),
            P("dp", None),
            P("dp"),
            P("dp"),
        ),
        out_specs=(
            P(("dp", "tensor"), None),
            P(("dp", "tensor"), None),
            P(),
            P(None, None, "tensor"),
            P("tensor", None),
            P(),
            P(),
            P(),
            P(None, None, None, "tensor"),
            P(None, "tensor", None),
            P(),
            P(),
            P(("dp", "tensor"), None),
            P(),
        ),
        check_vma=False,
    )
```

```python
import functools

import jax
import jax.numpy as jnp
from jax import lax
from jax.experimental import pallas as pl
from jax.experimental.pallas import tpu as pltpu
from jax.sharding import PartitionSpec as P

HEAD_DIM = 64
EXP_FFN = 6
SEQ_LEN = 1024
EPSILON = 1e-05
HIGHEST = lax.Precision.HIGHEST
F32 = jnp.float32
BF16 = jnp.bfloat16
I32 = jnp.int32

LANES = 128
TILE = 128
QUERY_BLOCK = 1024
GROUP = 4
GATHER = 3
COST_FORWARD, COST_BACKWARD, COST_EXPERT, COST_GRADS, COST_WIDEN, COST_ADD = 20, 32, 20, 11, 3, 3


def lasting(microseconds):
    return pl.CostEstimate(flops=0, bytes_accessed=microseconds * 3 * 10**6, transcendentals=0)


SIDE = ((0, 1), (1, 0), (2, 3), (3, 2))
CROSS = ((0, 2), (1, 3), (2, 0), (3, 1))
MIDDLE = ((1, 2), (2, 1))
OUTWARD = ((1, 0), (2, 3))
INWARD = ((0, 1), (3, 2))


def dot(left, right):
    return jnp.dot(left, right, preferred_element_type=F32)


def dot_nt(left, right):
    return lax.dot_general(left, right, (((1,), (1,)), ((), ())), preferred_element_type=F32)


def dot_tn(left, right):
    return lax.dot_general(left, right, (((0,), (0,)), ((), ())), preferred_element_type=F32)


def norm_forward(values, gain):
    inverse = lax.rsqrt(jnp.mean(values * values, axis=-1, keepdims=True) + EPSILON)
    return (values * inverse * gain, inverse)


def norm_backward(values, inverse, gain, grad):
    scaled = grad * gain
    inner = jnp.mean(scaled * values, axis=-1, keepdims=True)
    return inverse * scaled - values * inverse**3 * inner


def along_z(value, pairs):
    return lax.ppermute(value, "tensor", pairs)


def along_dp(value, bit, size):
    return lax.ppermute(value, "dp", [(i, i ^ (1 << bit)) for i in range(size)])


def behind(value, earlier):
    return lax.optimization_barrier((value, earlier))[0]


def slot_chunks(here):
    table = jnp.array([[0, 1, 2, 3], [1, 0, 2, 3], [2, 3, 1, 0], [3, 2, 1, 0]], I32)
    return lax.dynamic_slice_in_dim(table, here, 1, 0)[0]


def reduce_blocks(value, bits, index, size):
    for bit in bits:
        half = value.shape[0] // 2
        mine = (index >> bit) & 1
        sent = lax.dynamic_slice_in_dim(value, (1 - mine) * half, half, 0)
        kept = lax.dynamic_slice_in_dim(value, mine * half, half, 0)
        value = kept + along_dp(sent, bit, size)
    return value


def spread_blocks(value, bits, index, size):
    for bit in reversed(bits):
        mine = (index >> bit) & 1
        other = along_dp(value, bit, size)
        value = jnp.where(
            mine == 0,
            jnp.concatenate([value, other], axis=0),
            jnp.concatenate([other, value], axis=0),
        )
    return value


def sum_everywhere(value, bits, size, beside):
    value = value + along_z(value, SIDE)
    value = value + along_z(value, CROSS)
    for bit in bits[1:]:
        value = value + along_dp(value, bit, size)
    return value + behind(along_dp(value, bits[0], size), beside)


def rope_tables(offset):
    lane = jnp.arange(LANES, dtype=I32)
    row = jnp.arange(SEQ_LEN, dtype=I32)
    position = jnp.where(row < SEQ_LEN // 2, row + offset, row - offset).astype(F32)
    half = HEAD_DIM // 2
    frequency = 10000.0 ** (-(lane % half).astype(F32) / half)
    angles = position[:, None] * frequency[None, :]
    sign = jnp.where(lane % HEAD_DIM < half, -1.0, 1.0)
    return (jnp.cos(angles), jnp.sin(angles) * sign[None, :])


def swap_halves(value):
    half = HEAD_DIM // 2
    lane = lax.broadcasted_iota(I32, value.shape, 1)
    return jnp.where(
        lane % HEAD_DIM < half,
        pltpu.roll(value, LANES - half, 1),
        pltpu.roll(value, half, 1),
    )


def fill_bias(scalars, valid_ref, bias):
    offset, prefix = scalars[0], scalars[1]
    keys = lax.broadcasted_iota(I32, (SEQ_LEN, 1), 0)
    keys = jnp.where(keys < SEQ_LEN // 2, keys + offset, keys - offset)
    queries = lax.broadcasted_iota(I32, (1, SEQ_LEN), 1)
    queries = jnp.where(queries < SEQ_LEN // 2, queries + offset, queries - offset)
    seen = jnp.where(valid_ref[...] > 0, keys, SEQ_LEN)
    shown = ((seen <= queries) | (seen < prefix)) | (keys == queries)
    bias[...] = jnp.where(shown, 0.0, -1e30)


def head_lanes(value, head):
    lane = lax.broadcasted_iota(I32, value.shape, 1)
    return jnp.where((lane >= head * HEAD_DIM) & (lane < (head + 1) * HEAD_DIM), value, 0)


def attention_kernel(
    scalars, own, other, weights, w_out, cosine, sine, valid, *refs
):
    part_own, part_other, queries, keys, values, mixed, totals = refs[-11:-4]
    bias, key_rows, value_columns, total = refs[-4:]
    step = pl.program_id(0)
    half = SEQ_LEN // 2
    upper, lower = pl.ds(0, half), pl.ds(half, half)

    @pl.when(step == 0)
    def _():
        fill_bias(scalars, valid, bias)
        total[...] = jnp.zeros_like(total)

    for source, rows in ((own, upper), (other, lower)):
        x = source[...]
        for kind, target in ((0, queries), (1, keys), (2, values)):
            y = dot_nt(x, weights[kind])
            if kind < 2:
                y = y * cosine[rows, :] + swap_halves(y) * sine[rows, :]
            target[rows, :] = y.astype(BF16)
    key_rows[...] = keys[...]
    value_columns[...] = values[...].T

    @pl.loop(0, SEQ_LEN // QUERY_BLOCK)
    def _(index):
        columns = pl.ds(pl.multiple_of(index * QUERY_BLOCK, QUERY_BLOCK), QUERY_BLOCK)
        query = queries[columns, :] * 0.125
        outs = []
        for head in range(2):
            scores = dot_nt(key_rows[...], head_lanes(query, head)) + bias[:, columns]
            top = jnp.max(scores, axis=0, keepdims=True)
            raw = jnp.exp(scores - top)
            summed = jnp.sum(raw, axis=0, keepdims=True)
            shares = (raw * (1.0 / summed)).astype(BF16)
            outs.append(dot(value_columns[head * HEAD_DIM : (head + 1) * HEAD_DIM, :], shares))
            totals[0, head : head + 1, columns] = top + jnp.log(summed)
        mixed[columns, :] = jnp.concatenate(outs, axis=0).T.astype(BF16)

    total[...] += dot(mixed[...], w_out[...])

    @pl.when(step == pl.num_programs(0) - 1)
    def _():
        part_own[...] = total[upper, :].astype(BF16)
        part_other[...] = total[lower, :].astype(BF16)


def attention_specs(pairs, width):
    whole = lambda *shape: pl.BlockSpec(shape, lambda p, s: (0,) * len(shape))
    half = SEQ_LEN // 2
    rows = whole(half, width)
    weights = pl.BlockSpec((3, LANES, width), lambda p, s: (0, p, 0))
    w_out = pl.BlockSpec((LANES, width), lambda p, s: (p, 0))
    table = whole(SEQ_LEN, LANES)
    column = pl.BlockSpec((SEQ_LEN, LANES), lambda p, s: (0, p))
    totals = pl.BlockSpec((1, 8, SEQ_LEN), lambda p, s: (p, 0, 0))
    return (rows, weights, w_out, table, whole(SEQ_LEN, 1), column, totals)


def attention_forward(scalars, own, other, weights, w_out, cosine, sine, valid, ready):
    width = own.shape[1]
    pairs = weights.shape[1] // LANES
    rows, spec_w, spec_o, table, spec_v, column, totals = attention_specs(pairs, width)
    half = SEQ_LEN // 2
    shape = jax.ShapeDtypeStruct
    return pl.pallas_call(
        attention_kernel,
        grid_spec=pltpu.PrefetchScalarGridSpec(
            num_scalar_prefetch=1,
            grid=(pairs,),
            in_specs=[rows, rows, spec_w, spec_o, table, table, spec_v]
            + [pl.BlockSpec(memory_space=pl.ANY)] * len(ready),
            out_specs=[rows, rows, column, column, column, column, totals],
            scratch_shapes=[
                pltpu.VMEM((SEQ_LEN, SEQ_LEN), F32),
                pltpu.VMEM((SEQ_LEN, LANES), BF16),
                pltpu.VMEM((LANES, SEQ_LEN), BF16),
                pltpu.VMEM((SEQ_LEN, width), F32),
            ],
        ),
        out_shape=[
            shape((half, width), BF16),
            pltpu.HBM((half, width), BF16),
            *[pltpu.HBM((SEQ_LEN, pairs * LANES), BF16)] * 4,
            shape((pairs, 8, SEQ_LEN), F32),
        ],
        compiler_params=pltpu.CompilerParams(vmem_limit_bytes=48 * 2**20),
        cost_estimate=lasting(COST_FORWARD),
        name="attention_forward",
    )(scalars, own, other, weights, w_out, cosine, sine, valid, *ready)


def attention_back_kernel(
    scalars, own, other, weights, w_out, cosine, sine, valid,
    grad_own, grad_other, queries, keys, values, mixed, totals, *refs
):
    part_own, part_other, grad_w, grad_o, gain_row = refs[-12:-7]
    bias, grad_rows, key_columns, total, grad_q, grad_k, grad_v = refs[-7:]
    step = pl.program_id(0)
    half = SEQ_LEN // 2
    upper, lower = pl.ds(0, half), pl.ds(half, half)

    @pl.when(step == 0)
    def _():
        fill_bias(scalars, valid, bias)
        total[...] = jnp.zeros_like(total)

    grad_rows[upper, :] = dot_nt(grad_own[...], w_out[...]).astype(BF16)
    grad_rows[lower, :] = dot_nt(grad_other[...], w_out[...]).astype(BF16)
    columns_mixed = mixed[...].T
    grad_o[...] = (
        dot(columns_mixed[:, :half], grad_own[...]) + dot(columns_mixed[:, half:], grad_other[...])
    ).astype(BF16)
    key_columns[...] = keys[...].T
    grad_k[...] = jnp.zeros_like(grad_k)
    grad_v[...] = jnp.zeros_like(grad_v)

    @pl.loop(0, SEQ_LEN // QUERY_BLOCK)
    def _(index):
        columns = pl.ds(pl.multiple_of(index * QUERY_BLOCK, QUERY_BLOCK), QUERY_BLOCK)
        query = queries[columns, :] * 0.125
        grad = grad_rows[columns, :]
        outs = []
        for head in range(2):
            query_head = head_lanes(query, head)
            grad_head = head_lanes(grad, head)
            scores = dot_nt(keys[...], query_head) + bias[:, columns]
            shares = jnp.exp(scores - totals[0, head : head + 1, columns])
            grad_shares = dot_nt(values[...], grad_head)
            grad_v[...] += dot(shares.astype(BF16), grad_head)
            product = shares * grad_shares
            inner = jnp.sum(product, axis=0, keepdims=True)
            grad_scores = (product - shares * inner).astype(BF16)
            grad_k[...] += dot(grad_scores, query_head)
            outs.append(dot(key_columns[head * HEAD_DIM : (head + 1) * HEAD_DIM, :], grad_scores))
        grad_q[columns, :] = jnp.concatenate(outs, axis=0).T * 0.125

    for kind, source in ((0, grad_q), (1, grad_k), (2, grad_v)):
        y = source[...]
        if kind < 2:
            y = y * cosine[...] - swap_halves(y) * sine[...]
        y = y.astype(BF16)
        total[...] += dot(y, weights[kind])
        columns_y = y.T
        grad_w[kind] = (
            dot(columns_y[:, :half], own[...]) + dot(columns_y[:, half:], other[...])
        ).astype(BF16)

    @pl.when(step == pl.num_programs(0) - 1)
    def _():
        part_own[...] = total[upper, :].astype(BF16)
        part_other[...] = total[lower, :].astype(BF16)
        product = total[upper, :] * own[...].astype(F32) + total[lower, :] * other[...].astype(F32)
        gain_row[...] = jnp.sum(product.reshape(half // 8, 8, product.shape[1]), axis=0)


def attention_backward(
    scalars, own, other, weights, w_out, cosine, sine, valid, grad_own, grad_other, saved, ready
):
    width = own.shape[1]
    pairs = weights.shape[1] // LANES
    rows, spec_w, spec_o, table, spec_v, column, totals = attention_specs(pairs, width)
    half = SEQ_LEN // 2
    shape = jax.ShapeDtypeStruct
    return pl.pallas_call(
        attention_back_kernel,
        grid_spec=pltpu.PrefetchScalarGridSpec(
            num_scalar_prefetch=1,
            grid=(pairs,),
            in_specs=[
                rows, rows, spec_w, spec_o, table, table, spec_v,
                rows, rows, column, column, column, column, totals,
                *[pl.BlockSpec(memory_space=pl.ANY)] * len(ready),
            ],
            out_specs=[
                rows,
                rows,
                spec_w,
                spec_o,
                pl.BlockSpec((8, width), lambda p, s: (0, 0)),
            ],
            scratch_shapes=[
                pltpu.VMEM((SEQ_LEN, SEQ_LEN), F32),
                pltpu.VMEM((SEQ_LEN, LANES), BF16),
                pltpu.VMEM((LANES, SEQ_LEN), BF16),
                pltpu.VMEM((SEQ_LEN, width), F32),
                *[pltpu.VMEM((SEQ_LEN, LANES), F32)] * 3,
            ],
        ),
        out_shape=[
            shape((half, width), BF16),
            pltpu.HBM((half, width), BF16),
            shape((3, pairs * LANES, width), BF16),
            shape((pairs * LANES, width), BF16),
            shape((8, width), F32),
        ],
        compiler_params=pltpu.CompilerParams(vmem_limit_bytes=48 * 2**20),
        cost_estimate=lasting(COST_BACKWARD),
        name="attention_backward",
    )(
        scalars, own, other, weights, w_out, cosine, sine, valid, grad_own, grad_other, *saved, *ready
    )


def most_tiles(rows):
    return (2 * rows + EXP_FFN * (TILE - 1)) // TILE


def most_groups(tiles, experts):
    return (tiles + experts * (GROUP - 1)) // GROUP


def expert_plan(routes, valid, chunks):
    tokens = routes.shape[0]
    rows = tokens // chunks
    tiles = most_tiles(rows)
    numbers = jnp.arange(8, dtype=I32)[:, None]
    named = ((routes[:, 0][None, :] == numbers) | (routes[:, 1][None, :] == numbers)) & (
        valid[None, :] > 0
    )
    named = (named & (numbers < EXP_FFN)).reshape(8 * chunks, rows)
    before = (jnp.arange(rows)[:, None] < jnp.arange(rows)[None, :]).astype(BF16)
    place = dot(named.astype(BF16), before).astype(I32)
    place = jnp.where(named, place, -1).reshape(8, chunks, rows)
    count = jnp.sum(named.astype(I32), axis=1).reshape(8, chunks)[:EXP_FFN]
    number = (count + TILE - 1) // TILE
    number = jnp.where(jnp.arange(chunks)[None, :] == 0, jnp.maximum(number, 1), number)
    earlier = jnp.arange(EXP_FFN)[:, None] > jnp.arange(EXP_FFN)[None, :]
    first = jnp.sum(jnp.where(earlier[:, :, None], number[None], 0), axis=1)
    total = jnp.sum(number, axis=0)
    slot = jnp.arange(tiles, dtype=I32)
    expert = jnp.sum((first + number)[:, :, None] <= slot, axis=0)
    expert = jnp.minimum(expert, EXP_FFN - 1)
    pick = jnp.arange(EXP_FFN)[:, None, None] == expert[None]
    base = (slot - jnp.sum(jnp.where(pick, first[:, :, None], 0), axis=0)) * TILE
    meta = jnp.concatenate([expert, base, total[:, None], first.T, number.T], axis=1).astype(I32)
    return (place.transpose(1, 0, 2), meta.reshape(-1), number, first)


def expert_kernel(
    tiles, span, sources, meta, chunk, place, carry, routes, w_router, w_up_all, w_down_all, *refs
):
    taken = refs[: sum(map(len, sources))]
    part, feed, x_out, hidden_out, grad_out, both_out = refs[-18:-12]
    rows = feed.shape[0]
    width = feed.shape[1]
    table, hits, picked, back, total, hidden_rows, grad_rows, both_rows = refs[-12:-4]
    w_up, w_down, load_sems, save_sems = refs[-4:]
    hidden_width = w_down.shape[1]
    offset = chunk[0] * span
    number = meta[offset + 2 * tiles]
    groups = (number + GATHER - 1) // GATHER
    span_rows = GATHER * TILE

    def loads(expert):
        slot = lax.rem(expert, 2)
        return (
            pltpu.make_async_copy(w_up_all.at[expert], w_up.at[slot], load_sems.at[slot, 0]),
            pltpu.make_async_copy(w_down_all.at[expert], w_down.at[slot], load_sems.at[slot, 1]),
        )

    def saves(tile):
        source = pl.ds(pl.multiple_of(tile * TILE, TILE), TILE)
        goal = pl.ds(pl.multiple_of((chunk[0] * tiles + tile) * TILE, TILE), TILE)
        pairs = (
            (picked.at[source, pl.ds(0, width)], x_out),
            (hidden_rows.at[source], hidden_out),
            (grad_rows.at[source], grad_out),
            (both_rows.at[source], both_out),
        )
        return [
            pltpu.make_async_copy(ref, out.at[goal], save_sems.at[tile, k])
            for k, (ref, out) in enumerate(pairs)
        ]

    for copy in loads(0):
        copy.start()

    first = 0
    for option, group in enumerate(sources):
        refs_here = taken[first : first + len(group)]
        first += len(group)

        @pl.when(chunk[1] == option)
        def _(refs_here=refs_here, group=group):
            at = {"x": 0, "cot": 0}
            for ref, kind in zip(refs_here, group):
                columns = pl.ds(0 if kind == "x" else width + LANES, width)
                table[pl.ds(at[kind], ref.shape[0]), columns] = ref[...]
                at[kind] += ref.shape[0]

    logits = dot(table[:, :width], w_router[...]) + carry[0]
    lane = lax.broadcasted_iota(I32, logits.shape, 1)
    one, two = lane == routes[0, :, 0:1], lane == routes[0, :, 1:2]
    score_one = jnp.sum(jnp.where(one, logits, 0.0), axis=1, keepdims=True)
    score_two = jnp.sum(jnp.where(two, logits, 0.0), axis=1, keepdims=True)
    top = jnp.maximum(score_one, score_two)
    score_one, score_two = jnp.exp(score_one - top), jnp.exp(score_two - top)
    both = score_one + score_two
    gates = jnp.where(one, score_one / both, 0.0) + jnp.where(two, score_two / both, 0.0)
    high = gates.astype(BF16).astype(F32)
    low = gates - high
    table[:, width : width + LANES] = (high + pltpu.roll(low, LANES // 2, 1)).astype(BF16)
    total[...] = jnp.zeros_like(total)

    @pl.loop(0, groups)
    def _(group):
        for at in range(GATHER):
            tile = group * GATHER + at
            slot = jnp.minimum(tile, tiles - 1)
            base = jnp.where(tile < number, meta[offset + tiles + slot], rows)
            row = lax.broadcasted_iota(I32, (TILE, rows), 0) + base
            hit = place[0, pl.ds(meta[offset + slot], 1), :] == row
            goal = pl.ds(pl.multiple_of(tile * TILE, TILE), TILE)
            hits[goal, :] = jnp.where(hit, 1.0, 0.0).astype(BF16)

            @pl.when(tile >= number)
            def _():
                back[goal, :] = jnp.zeros((TILE, back.shape[1]), BF16)

        here = pl.ds(pl.multiple_of(group * span_rows, TILE), span_rows)
        picked[here, :] = dot(hits[here, :], table[...]).astype(BF16)

    @pl.loop(0, EXP_FFN)
    def _(expert):
        slot = lax.rem(expert, 2)
        for copy in loads(expert):
            copy.wait()

        @pl.when(expert + 1 < EXP_FFN)
        def _():
            for copy in loads(expert + 1):
                copy.start()

        start = meta[offset + 2 * tiles + 1 + expert]
        amount = meta[offset + 2 * tiles + 1 + EXP_FFN + expert]

        @pl.loop(start, start + amount)
        def _(tile):
            mine = pl.ds(pl.multiple_of(tile * TILE, TILE), TILE)
            inputs = picked[mine, :width]
            lane = lax.broadcasted_iota(I32, (TILE, LANES), 1)
            own = (lane == expert) | (lane == expert + LANES // 2)
            scale = jnp.sum(
                jnp.where(own, picked[mine, width : width + LANES].astype(F32), 0.0),
                axis=1,
                keepdims=True,
            )
            upstream = picked[mine, width + LANES :].astype(F32)
            both = dot(inputs, w_up[slot])
            gate, up = both[:, :hidden_width], both[:, hidden_width:]
            sigma = 1.0 / (1.0 + jnp.exp(-gate))
            active = gate * sigma
            hidden = (active * up).astype(BF16)
            outputs = dot(hidden, w_down[slot])
            gate_term = jnp.sum(upstream * outputs, axis=1, keepdims=True)
            grad_row = (upstream * scale).astype(BF16)
            grad_hidden = dot_nt(grad_row, w_down[slot])
            grad_gate = (grad_hidden * up * sigma * (1.0 + gate * (1.0 - sigma))).astype(BF16)
            grad_up = (grad_hidden * active).astype(BF16)
            grad_both = jnp.concatenate([grad_gate, grad_up], axis=1)
            grad_x = dot_nt(grad_both, w_up[slot])
            hidden_rows[mine, :] = hidden
            grad_rows[mine, :] = grad_row
            both_rows[mine, :] = grad_both
            for copy in saves(tile):
                copy.start()
            back[mine, :width] = (outputs * scale).astype(BF16)
            back[mine, width : 2 * width] = grad_x.astype(BF16)
            back[mine, 2 * width :] = jnp.where(lane == expert, gate_term, 0.0).astype(BF16)

    @pl.loop(0, groups)
    def _(group):
        here = pl.ds(pl.multiple_of(group * span_rows, TILE), span_rows)
        total[...] += dot_tn(hits[here, :], back[here, :])

    feed[...] = total[:, :width].astype(BF16)
    part[:rows, :] = total[:, width : 2 * width].astype(BF16)
    terms = total[:, 2 * width :].T[:16]
    part[rows:, :] = jnp.concatenate([terms, jnp.zeros((16, width - rows), F32)], axis=1).astype(
        BF16
    )

    @pl.loop(0, number)
    def _(tile):
        for copy in saves(tile):
            copy.wait()


def expert_chunk(meta, chunk, options, place, carry, routes, w_router, w_up, w_down, saved):
    rows, width = options[0]["x"][0].shape
    sources = [[kind for kind in ("x", "cot") for _ in option[kind]] for option in options]
    taken = [ref for option in options for kind in ("x", "cot") for ref in option[kind]]
    chunks = place.shape[0]
    hidden_width = w_down.shape[1]
    tiles = most_tiles(rows)
    span = 2 * tiles + 1 + 2 * EXP_FFN
    held = (tiles + GATHER - 1) // GATHER * GATHER * TILE
    shape = jax.ShapeDtypeStruct
    whole = lambda *dims: pl.BlockSpec(dims, lambda i, m, c: (0,) * len(dims))
    mine = lambda *dims: pl.BlockSpec((1, *dims), lambda i, m, c: (c[0], 0, 0))
    stay = pl.BlockSpec(memory_space=pl.ANY)
    columns = (width, hidden_width, width, 2 * hidden_width)
    extra = () if saved is None else tuple(saved)
    return pl.pallas_call(
        functools.partial(expert_kernel, tiles, span, sources),
        grid_spec=pltpu.PrefetchScalarGridSpec(
            num_scalar_prefetch=2,
            grid=(1,),
            in_specs=[
                mine(8, rows),
                mine(rows, LANES),
                mine(rows, 2),
                whole(width, LANES),
                stay,
                stay,
                *[whole(*ref.shape) for ref in taken],
                *[stay] * len(extra),
            ],
            out_specs=[whole(rows + 16, width), whole(rows, width), *[stay] * len(columns)],
            scratch_shapes=[
                pltpu.VMEM((rows, 2 * width + LANES), BF16),
                pltpu.VMEM((held, rows), BF16),
                pltpu.VMEM((held, 2 * width + LANES), BF16),
                pltpu.VMEM((held, 2 * width + LANES), BF16),
                pltpu.VMEM((rows, 2 * width + LANES), F32),
                *[pltpu.VMEM((held, c), BF16) for c in columns[1:]],
                pltpu.VMEM((2, width, 2 * hidden_width), BF16),
                pltpu.VMEM((2, hidden_width, width), BF16),
                pltpu.SemaphoreType.DMA((2, 2)),
                pltpu.SemaphoreType.DMA((tiles, len(columns))),
            ],
        ),
        out_shape=[
            pltpu.HBM((rows + 16, width), BF16),
            pltpu.HBM((rows, width), BF16),
            *[shape((chunks * tiles * TILE, c), BF16) for c in columns],
        ],
        input_output_aliases={8 + len(taken) + k: 2 + k for k in range(len(extra))},
        compiler_params=pltpu.CompilerParams(vmem_limit_bytes=52 * 2**20),
        cost_estimate=lasting(COST_EXPERT),
        name="expert_chunk",
    )(meta, chunk, place, carry, routes, w_router, w_up, w_down, *taken, *extra)


def grad_walk(number, first, tiles):
    experts, chunks = number.shape
    flat = number.reshape(-1)
    groups = flat.shape[0]
    earlier = jnp.arange(groups)[:, None] > jnp.arange(groups)[None, :]
    start = jnp.sum(jnp.where(earlier, flat[None, :], 0), axis=1)
    held = jnp.sum(number, axis=1)
    held_groups = (held + GROUP - 1) // GROUP
    earlier = jnp.arange(experts)[:, None] > jnp.arange(experts)[None, :]
    held_start = jnp.sum(jnp.where(earlier, held[None, :], 0), axis=1)
    group_start = jnp.sum(jnp.where(earlier, held_groups[None, :], 0), axis=1)
    steps = most_groups(chunks * tiles, experts)
    everything = jnp.sum(held_groups)
    step = jnp.minimum(jnp.arange(steps, dtype=I32), everything - 1)
    owner = jnp.sum((group_start + held_groups)[:, None] <= step[None, :], axis=0)
    pick = jnp.arange(experts)[:, None] == owner[None, :]
    look = lambda values: jnp.sum(jnp.where(pick, values[:, None], 0), axis=0)
    done = (step - look(group_start)) * GROUP
    left = look(held) - done
    place_in = done[:, None] + jnp.minimum(jnp.arange(GROUP)[None, :], left[:, None] - 1)
    spot = (look(held_start)[:, None] + place_in).reshape(-1)
    group = jnp.sum((start + flat)[:, None] <= spot[None, :], axis=0)
    pick = jnp.arange(groups)[:, None] == group[None, :]
    offset = jnp.arange(chunks)[None, :] * tiles + first
    block = jnp.sum(jnp.where(pick, (offset.reshape(-1) - start)[:, None], 0), axis=0) + spot
    return jnp.concatenate([owner, block, left, everything[None]]).astype(I32)


def packing(width, hidden_width):
    columns = 2 * hidden_width
    spare = columns - width
    height = hidden_width * width // columns
    pieces = [(slice(width, width + height), slice(0, width), slice(0, height), slice(0, width))]
    short = hidden_width - height
    for at in range(width // spare):
        pieces.append(
            (
                slice(width + at * short, width + (at + 1) * short),
                slice(width, columns),
                slice(height, hidden_width),
                slice(at * spare, (at + 1) * spare),
            )
        )
    return pieces


def packed_height(width, hidden_width):
    return width + width // 2


def weight_grad_kernel(steps, walk, *refs):
    kept, packed = refs[:4], refs[4]
    rows, (sum_up, sum_down, out, load_sems, save_sems) = refs[5:9], refs[9:]
    number = walk[(2 + GROUP) * steps]
    width, hidden_width = sum_up.shape[0], sum_down.shape[0]

    def loads(step):
        slot = lax.rem(step, 2)
        copies = []
        for at in range(GROUP):
            block = walk[steps + step * GROUP + at]
            source = pl.ds(pl.multiple_of(block * TILE, TILE), TILE)
            for kind in range(4):
                copies.append(
                    pltpu.make_async_copy(
                        kept[kind].at[source],
                        rows[kind].at[slot, pl.ds(at * TILE, TILE)],
                        load_sems.at[slot, at, kind],
                    )
                )
        return copies

    def save(expert):
        slot, height = lax.rem(expert, 2), out.shape[1]
        goal = pl.ds(pl.multiple_of(expert * height, height), height)
        return pltpu.make_async_copy(out.at[slot], packed.at[goal], save_sems.at[slot])

    def store(side, up, down):
        out[side, :width] = up.astype(BF16)
        for goal, columns, source, taken in packing(width, hidden_width):
            out[side, goal, columns] = down[source, taken].astype(BF16)

    for copy in loads(0):
        copy.start()

    @pl.loop(0, number)
    def _(step):
        slot = lax.rem(step, 2)
        expert = walk[step]
        left = walk[(1 + GROUP) * steps + step]
        for copy in loads(step):
            copy.wait()

        @pl.when(step + 1 < number)
        def _():
            for copy in loads(step + 1):
                copy.start()

        row = lax.broadcasted_iota(I32, (GROUP * TILE, 1), 0)
        live = row < left * TILE
        side = lax.rem(expert, 2)

        def products():
            return (
                dot_tn(jnp.where(live, rows[0][slot], 0), rows[3][slot]),
                dot_tn(jnp.where(live, rows[1][slot], 0), rows[2][slot]),
            )

        fresh = (step == 0) | (walk[jnp.maximum(step - 1, 0)] != expert)
        done = (step == number - 1) | (walk[jnp.minimum(step + 1, steps - 1)] != expert)

        @pl.when(done & (expert >= 2))
        def _():
            save(expert - 2).wait()

        @pl.when(fresh & done)
        def _():
            store(side, *products())

        @pl.when(fresh & jnp.logical_not(done))
        def _():
            sum_up[...], sum_down[...] = products()

        @pl.when(jnp.logical_not(fresh | done))
        def _():
            up, down = products()
            sum_up[...] += up
            sum_down[...] += down

        @pl.when(jnp.logical_not(fresh) & done)
        def _():
            up, down = products()
            store(side, sum_up[...] + up, sum_down[...] + down)

        @pl.when(done)
        def _():
            save(expert).start()

    for expert in (EXP_FFN - 2, EXP_FFN - 1):
        save(expert).wait()


def weight_grads(walk, saved):
    width, hidden_width = saved[0].shape[1], saved[1].shape[1]
    height = packed_height(width, hidden_width)
    steps = most_groups(saved[0].shape[0] // TILE, EXP_FFN)
    shape = jax.ShapeDtypeStruct
    stay = pl.BlockSpec(memory_space=pl.ANY)
    return pl.pallas_call(
        functools.partial(weight_grad_kernel, steps),
        grid_spec=pltpu.PrefetchScalarGridSpec(
            num_scalar_prefetch=1,
            grid=(1,),
            in_specs=[stay] * 4,
            out_specs=stay,
            scratch_shapes=[
                *[pltpu.VMEM((2, GROUP * TILE, kept.shape[1]), BF16) for kept in saved],
                pltpu.VMEM((width, 2 * hidden_width), F32),
                pltpu.VMEM((hidden_width, width), F32),
                pltpu.VMEM((2, height, 2 * hidden_width), BF16),
                pltpu.SemaphoreType.DMA((2, GROUP, 4)),
                pltpu.SemaphoreType.DMA((2,)),
            ],
        ),
        out_shape=shape((EXP_FFN * height, 2 * hidden_width), BF16),
        compiler_params=pltpu.CompilerParams(vmem_limit_bytes=48 * 2**20),
        cost_estimate=lasting(COST_GRADS),
        name="weight_grads",
    )(walk, *saved)


def widen_kernel(source, up, down):
    width = down.shape[1]
    split = source.shape[1] // LANES
    for row in range(split):
        at = row % 2 * (source.shape[1] // 2) + row // 2 * LANES
        up[pl.ds(row, width, stride=split), :] = source[:width, at : at + LANES].astype(F32)
    for place, columns, goal, taken in packing(width, down.shape[0]):
        down[goal, taken] = source[place, columns].astype(F32)


def widen(packed, width, hidden_width):
    height = packed_height(width, hidden_width)
    rows = width * packed.shape[1] // LANES
    shape = jax.ShapeDtypeStruct
    return pl.pallas_call(
        widen_kernel,
        grid=(EXP_FFN,),
        in_specs=[pl.BlockSpec((height, packed.shape[1]), lambda i: (i, 0))],
        out_specs=[
            pl.BlockSpec((rows, LANES), lambda i: (i, 0)),
            pl.BlockSpec((hidden_width, width), lambda i: (i, 0)),
        ],
        out_shape=[
            shape((EXP_FFN * rows, LANES), F32),
            shape((EXP_FFN * hidden_width, width), F32),
        ],
        compiler_params=pltpu.CompilerParams(vmem_limit_bytes=60 * 2**20),
        cost_estimate=lasting(COST_WIDEN),
        name="widen",
    )(packed)


def shards(
    dp_size,
    stream,
    cotangent,
    gain_attention,
    w_inputs,
    w_output,
    gain_experts,
    w_router,
    w_carry,
    w_gate_up,
    w_down,
    w_constant,
    constant_vectors,
    previous_logits,
    routes,
    valid,
    prefix,
):
    rows, width = stream.shape
    tokens = routes.shape[0]
    chunks = tokens // rows
    head_columns = w_inputs.shape[2]
    here = lax.axis_index("tensor")
    index = lax.axis_index("dp")
    outer = (here == 0) | (here == chunks - 1)
    bits = list(range(dp_size.bit_length() - 1))
    first_row = here * rows
    valid_all = valid.astype(F32)
    cut = lambda array, at: lax.dynamic_slice_in_dim(array, at, rows, 0)
    valid_here = cut(valid_all, first_row)
    routes_here = cut(routes, first_row)
    previous_here = cut(previous_logits, first_row)

    w_in_rows = w_inputs.transpose(0, 2, 1)
    packed = jnp.concatenate([w_in_rows, w_output[None]], axis=0).reshape(-1, width)
    piece_rows = packed.shape[0] // dp_size
    position = (index >> 1) | ((index & 1) << (len(bits) - 1))
    piece = lax.dynamic_slice_in_dim(packed, position * piece_rows, piece_rows, 0)
    normed_here, inverse_one = norm_forward(stream, gain_attention)
    normed_low = normed_here.astype(BF16)
    normed_other = along_z(normed_low, SIDE)
    piece = along_z(piece, CROSS)
    cot_low = behind(cotangent, piece).astype(BF16)
    cot_side, cot_middle = along_z(cot_low, SIDE), along_z(cot_low, MIDDLE)
    for level, bit in enumerate([*bits[1:], bits[0]]):
        if level == 0:
            place, meta, number, first = expert_plan(*behind((routes, valid), piece), chunks)
        if level == 1:
            number, first = behind((number, first), piece)
            walk = grad_walk(number, first, most_tiles(rows))
        other = along_dp(piece, bit, dp_size)
        piece = jnp.where(
            (index >> bit) & 1 == 0,
            jnp.concatenate([piece, other], axis=0),
            jnp.concatenate([other, piece], axis=0),
        )
    carry = jnp.dot(behind(previous_logits, place), w_carry, precision=HIGHEST, preferred_element_type=F32)
    columns = carry.shape[1]
    carry_wide = jnp.pad(carry, ((0, 0), (0, LANES - columns))).reshape(chunks, rows, LANES)
    routes_live = jnp.where(valid[:, None] > 0, routes, -1).reshape(chunks, rows, 2)
    router_wide = jnp.pad(w_router, ((0, 0), (0, LANES - columns)))
    partner = piece.reshape(4, head_columns, width)
    both_in = jnp.concatenate([w_in_rows, partner[:3]], axis=1)
    both_out = jnp.concatenate([w_output, partner[3]], axis=0)

    core = index & 1
    offset = (here % 2) * rows
    sequence = here // 2
    scalars = jnp.stack([offset, prefix[sequence]]).astype(I32)
    cosine, sine = rope_tables(offset)
    valid_rows = jnp.concatenate([cut(valid, first_row), cut(valid, (here ^ 1) * rows)])[:, None]
    fixed = (both_in, both_out, cosine, sine, valid_rows)
    ready = (place, meta, walk, cot_side, cot_middle, carry_wide, routes_live, router_wide)
    part_own, part_other, *saved_attention = attention_forward(
        scalars, normed_low, normed_other, *fixed, ready
    )
    attention_other = along_z(part_other, SIDE)

    cot_far, cot_across = along_z(cot_middle, OUTWARD), along_z(cot_side, MIDDLE)
    cot_far, cot_across = behind((cot_far, cot_across), part_own)
    w_up = behind(w_gate_up, (part_own, cot_far, cot_across)).reshape(EXP_FFN, width, -1)
    attention_other = behind(attention_other, w_up)
    attention = part_own.astype(F32) + attention_other.astype(F32)
    middle = stream + attention
    second, inverse_two = norm_forward(middle, gain_experts)
    second_low = second.astype(BF16)

    which = slot_chunks(here)

    def chunk(slot, options, saved):
        choice = outer.astype(I32) * (len(options) - 1)
        return expert_chunk(
            meta,
            jnp.stack([which[slot], choice]),
            options,
            place,
            carry_wide,
            routes_live,
            router_wide,
            w_up,
            w_down,
            saved,
        )

    third_rows = rows // 3 // 16 * 16
    cuts = (0, third_rows, 2 * third_rows, rows)
    cot_pieces = [cot_across[low:high] for low, high in zip(cuts[:-1], cuts[1:])]
    side, middle_rows = along_z(second_low, SIDE), along_z(second_low, MIDDLE)
    cot_last = [along_z(behind(cot_pieces[0], second_low), OUTWARD)]
    part_0, feed_0, *saved = chunk(0, [{"x": [second_low], "cot": [cot_low]}], None)
    side, middle_rows, cot_last[0] = behind((side, middle_rows, cot_last[0]), part_0)
    far, across = along_z(middle_rows, OUTWARD), along_z(side, MIDDLE)
    cot_last.append(along_z(behind(cot_pieces[1], part_0), OUTWARD))
    part_1, feed_1, *saved = chunk(1, [{"x": [side], "cot": [cot_side]}], saved)
    near, feed_near = along_z(part_1, INWARD), along_z(feed_1, INWARD)
    far, across, cot_last[1] = behind((far, across, cot_last[1]), part_1)
    last = along_z(across, OUTWARD)
    cot_last.append(along_z(behind(cot_pieces[2], part_1), OUTWARD))
    part_2, feed_2, *saved = chunk(
        2, [{"x": [middle_rows], "cot": [cot_middle]}, {"x": [far], "cot": [cot_far]}], saved
    )
    third = along_z(part_2, INWARD)
    last, cot_last[2] = behind((last, cot_last[2]), part_2)
    part_3, feed_3, *saved = chunk(
        3,
        [{"x": [across], "cot": [cot_across]}, {"x": [last], "cot": cot_last}],
        saved,
    )

    inward = along_z(part_3, INWARD)
    packed = weight_grads(walk, saved)
    inward, packed = lax.optimization_barrier((inward, packed))
    packed = lax.psum_scatter(packed, "dp", scatter_dimension=0, tiled=True)
    feed_outward = along_z(behind(feed_3, inward), INWARD)
    inward = part_3 + inward
    inward, feed_outward = lax.optimization_barrier((along_z(inward, MIDDLE), feed_outward))
    third = along_z(part_2 + third, MIDDLE)
    outward = along_z(part_1 + inward, OUTWARD)
    summed = part_0.astype(F32) + near.astype(F32) + third.astype(F32) + outward.astype(F32)

    logits = dot(second_low, w_router) + cut(carry, first_row)
    picked = routes_here[:, :, None] == jnp.arange(columns, dtype=I32)[None, None, :]
    chosen = jnp.sum(jnp.where(picked, logits[:, None, :], 0.0), axis=-1)
    gates_here = jax.nn.softmax(chosen, axis=-1)
    live_gates = gates_here * valid_here[:, None]
    copy_gate = jnp.sum(jnp.where(routes_here == EXP_FFN + 1, live_gates, 0.0), axis=-1)
    constant_gates = jnp.stack(
        [
            jnp.sum(jnp.where(routes_here == EXP_FFN + 2 + number, live_gates, 0.0), axis=-1)
            for number in range(2)
        ],
        axis=1,
    )
    alphas = jax.nn.softmax(
        jnp.einsum("td,cad->tca", second, w_constant, precision=HIGHEST, preferred_element_type=F32),
        axis=-1,
    )
    constant_out = (
        alphas[:, :, 0:1] * second[:, None, :] + alphas[:, :, 1:2] * constant_vectors[None, :, :]
    )
    extra = copy_gate[:, None] * second + jnp.sum(
        constant_gates[:, :, None] * constant_out, axis=1
    )
    copy_terms = jnp.sum(cotangent * second, axis=-1)
    constant_terms = jnp.sum(cotangent[:, None, :] * constant_out, axis=-1)
    grad_constant_out = constant_gates[:, :, None] * cotangent[:, None, :]
    grad_vectors = jnp.sum(alphas[:, :, 1:2] * grad_constant_out, axis=0)
    grad_alphas = jnp.stack(
        [
            jnp.sum(grad_constant_out * second[:, None, :], axis=-1),
            jnp.sum(grad_constant_out * constant_vectors[None, :, :], axis=-1),
        ],
        axis=-1,
    )
    grad_mix = alphas * (grad_alphas - jnp.sum(alphas * grad_alphas, axis=-1, keepdims=True))
    grad_constant = jnp.einsum(
        "tca,td->cad", grad_mix, second, precision=HIGHEST, preferred_element_type=F32
    )
    grad_local = (
        copy_gate[:, None] * cotangent
        + jnp.sum(alphas[:, :, 0:1] * grad_constant_out, axis=1)
        + jnp.einsum(
            "tca,cad->td", grad_mix, w_constant, precision=HIGHEST, preferred_element_type=F32
        )
    )

    gate_grads = summed[rows : rows + EXP_FFN, :rows].T
    gate_table = jnp.concatenate(
        [gate_grads, jnp.zeros((rows, 1), F32), copy_terms[:, None], constant_terms], axis=1
    )
    grad_gates = jnp.sum(jnp.where(picked, gate_table[:, None, :], 0.0), axis=-1)
    grad_gates = grad_gates * valid_here[:, None]
    grad_chosen = gates_here * (
        grad_gates - jnp.sum(gates_here * grad_gates, axis=-1, keepdims=True)
    )
    grad_logits = jnp.sum(jnp.where(picked, grad_chosen[:, :, None], 0.0), axis=1)
    grad_router = jnp.dot(
        second_low.astype(F32).T, grad_logits, precision=HIGHEST, preferred_element_type=F32
    )
    grad_carry = jnp.dot(
        previous_here.T, grad_logits, precision=HIGHEST, preferred_element_type=F32
    )
    grad_previous = jnp.dot(
        grad_logits, w_carry.T, precision=HIGHEST, preferred_element_type=F32
    )
    grad_second = (
        summed[:rows]
        + grad_local
        + jnp.dot(
            grad_logits, w_router.astype(F32).T, precision=HIGHEST, preferred_element_type=F32
        )
    )
    grad_gain_experts = jnp.sum(grad_second * middle * inverse_two, axis=0)
    grad_middle = cotangent + norm_backward(middle, inverse_two, gain_experts, grad_second)

    grad_low = grad_middle.astype(BF16)
    grad_other = along_z(grad_low, SIDE)
    feed_outward = feed_3 + feed_outward

    part_own, part_other, grad_w, grad_o, gain_rows = attention_backward(
        scalars, normed_low, normed_other, *fixed, grad_low, grad_other, saved_attention, ()
    )
    grad_normed = part_own.astype(F32) + along_z(part_other, SIDE).astype(F32)
    grad_stream = grad_middle + norm_backward(stream, inverse_one, gain_attention, grad_normed)

    feed_2, feed_outward = behind((feed_2, feed_outward), part_own)
    feed_third, feed_outward = along_z(feed_2, INWARD), along_z(feed_outward, MIDDLE)
    feed_third = along_z(feed_2 + feed_third, MIDDLE)
    feed_outward = along_z(feed_1 + feed_outward, OUTWARD)
    feed = feed_0.astype(F32) + feed_near.astype(F32)
    feed = feed + feed_third.astype(F32) + feed_outward.astype(F32)
    experts = feed + extra
    block_out = middle + experts
    squares = [
        jnp.sum(valid_here[:, None] * part * part) for part in (block_out, attention, experts)
    ]
    squares = jnp.stack([*squares, jnp.sum(valid_here)])

    own_grads = jnp.concatenate([grad_w[:, :head_columns], grad_o[None, :head_columns]], axis=0)
    far_grads = jnp.concatenate([grad_w[:, head_columns:], grad_o[None, head_columns:]], axis=0)
    order = bits
    own_piece = reduce_blocks(own_grads.reshape(-1, width), order[:1], index, dp_size)
    far_piece = reduce_blocks(far_grads.reshape(-1, width), order[:1], index, dp_size)
    packed = lax.all_gather(behind(packed, own_piece), "dp", axis=0, tiled=True)
    own_piece = reduce_blocks(own_piece, order[1:], index, dp_size)
    far_piece = reduce_blocks(far_piece, order[1:], index, dp_size)
    own_piece = own_piece + along_z(far_piece, CROSS)
    grad_gate_up, grad_down = widen(packed, width, w_down.shape[1])
    grad_gate_up = grad_gate_up.reshape(EXP_FFN, width, -1, 2, LANES).transpose(0, 1, 3, 2, 4)
    grad_gate_up = grad_gate_up.reshape(EXP_FFN, width, 2, -1)
    grad_down = grad_down.reshape(EXP_FFN, -1, width)

    attention_grads = spread_blocks(own_piece, order, index, dp_size).astype(F32)
    attention_grads = attention_grads.reshape(4, head_columns, width)
    grad_inputs = attention_grads[:3].transpose(0, 2, 1)
    grad_output = attention_grads[3]

    wide = lambda array: jnp.pad(array, ((0, 0), (0, width - array.shape[1])))
    small = jnp.concatenate(
        [
            grad_gain_experts[None],
            grad_router.T,
            wide(grad_carry),
            grad_constant.reshape(-1, width),
            grad_vectors,
            wide(squares[None]),
            jnp.sum(gain_rows, axis=0, keepdims=True) / gain_attention[None],
        ],
        axis=0,
    )
    small = sum_everywhere(small, bits, dp_size, grad_down)
    at = 1 + 2 * columns
    squares = small[at + 6, :3]
    counted = small[at + 6, 3]
    rms_values = jnp.sqrt(squares / (jnp.maximum(counted, 1.0) * width))
    return (
        block_out,
        grad_stream,
        small[at + 7],
        grad_inputs,
        grad_output,
        small[0],
        small[1 : 1 + columns].T,
        small[1 + columns : at, :columns],
        grad_gate_up,
        grad_down,
        small[at : at + 4].reshape(2, 2, width),
        small[at + 4 : at + 6],
        grad_previous,
        rms_values,
    )


def solution(mesh):
    return jax.shard_map(
        functools.partial(shards, mesh.shape["dp"]),
        mesh=mesh,
        in_specs=(
            P(("dp", "tensor"), None),
            P(("dp", "tensor"), None),
            P(),
            P(None, None, "tensor"),
            P("tensor", None),
            P(),
            P(),
            P(),
            P(None, None, None, "tensor"),
            P(None, "tensor", None),
            P(),
            P(),
            P("dp", None),
            P("dp", None),
            P("dp"),
            P("dp"),
        ),
        out_specs=(
            P(("dp", "tensor"), None),
            P(("dp", "tensor"), None),
            P(),
            P(None, None, "tensor"),
            P("tensor", None),
            P(),
            P(),
            P(),
            P(None, None, None, "tensor"),
            P(None, "tensor", None),
            P(),
            P(),
            P(("dp", "tensor"), None),
            P(),
        ),
        check_vma=False,
    )
```

```python
import functools

import jax
import jax.numpy as jnp
from jax import lax
from jax.experimental import pallas as pl
from jax.experimental.pallas import tpu as pltpu
from jax.sharding import PartitionSpec as P

HEAD_DIM = 64
EXP_FFN = 6
SEQ_LEN = 1024
EPSILON = 1e-05
HIGHEST = lax.Precision.HIGHEST
F32 = jnp.float32
BF16 = jnp.bfloat16
I32 = jnp.int32

LANES = 128
TILE = 128
QUERY_BLOCK = 1024
GROUP = 4
GATHER = 3
COST_FORWARD, COST_BACKWARD, COST_EXPERT, COST_GRADS, COST_WIDEN, COST_ADD = 20, 32, 20, 11, 3, 3


def lasting(microseconds):
    return pl.CostEstimate(flops=0, bytes_accessed=microseconds * 3 * 10**6, transcendentals=0)


SIDE = ((0, 1), (1, 0), (2, 3), (3, 2))
CROSS = ((0, 2), (1, 3), (2, 0), (3, 1))
MIDDLE = ((1, 2), (2, 1))
OUTWARD = ((1, 0), (2, 3))
INWARD = ((0, 1), (3, 2))


def dot(left, right):
    return jnp.dot(left, right, preferred_element_type=F32)


def dot_nt(left, right):
    return lax.dot_general(left, right, (((1,), (1,)), ((), ())), preferred_element_type=F32)


def dot_tn(left, right):
    return lax.dot_general(left, right, (((0,), (0,)), ((), ())), preferred_element_type=F32)


def norm_forward(values, gain):
    inverse = lax.rsqrt(jnp.mean(values * values, axis=-1, keepdims=True) + EPSILON)
    return (values * inverse * gain, inverse)


def norm_backward(values, inverse, gain, grad):
    scaled = grad * gain
    inner = jnp.mean(scaled * values, axis=-1, keepdims=True)
    return inverse * scaled - values * inverse**3 * inner


def along_z(value, pairs):
    return lax.ppermute(value, "tensor", pairs)


def along_dp(value, bit, size):
    return lax.ppermute(value, "dp", [(i, i ^ (1 << bit)) for i in range(size)])


def behind(value, earlier):
    return lax.optimization_barrier((value, earlier))[0]


def slot_chunks(here):
    table = jnp.array([[0, 1, 2, 3], [1, 0, 2, 3], [2, 3, 1, 0], [3, 2, 1, 0]], I32)
    return lax.dynamic_slice_in_dim(table, here, 1, 0)[0]


def reduce_blocks(value, bits, index, size):
    for bit in bits:
        half = value.shape[0] // 2
        mine = (index >> bit) & 1
        sent = lax.dynamic_slice_in_dim(value, (1 - mine) * half, half, 0)
        kept = lax.dynamic_slice_in_dim(value, mine * half, half, 0)
        value = kept + along_dp(sent, bit, size)
    return value


def spread_blocks(value, bits, index, size):
    for bit in reversed(bits):
        mine = (index >> bit) & 1
        other = along_dp(value, bit, size)
        value = jnp.where(
            mine == 0,
            jnp.concatenate([value, other], axis=0),
            jnp.concatenate([other, value], axis=0),
        )
    return value


def sum_everywhere(value, bits, size, beside):
    value = value + along_z(value, SIDE)
    value = value + along_z(value, CROSS)
    for bit in bits[1:]:
        value = value + along_dp(value, bit, size)
    return value + behind(along_dp(value, bits[0], size), beside)


def rope_tables(offset):
    lane = jnp.arange(LANES, dtype=I32)
    row = jnp.arange(SEQ_LEN, dtype=I32)
    position = jnp.where(row < SEQ_LEN // 2, row + offset, row - offset).astype(F32)
    half = HEAD_DIM // 2
    frequency = 10000.0 ** (-(lane % half).astype(F32) / half)
    angles = position[:, None] * frequency[None, :]
    sign = jnp.where(lane % HEAD_DIM < half, -1.0, 1.0)
    return (jnp.cos(angles), jnp.sin(angles) * sign[None, :])


def swap_halves(value):
    half = HEAD_DIM // 2
    lane = lax.broadcasted_iota(I32, value.shape, 1)
    return jnp.where(
        lane % HEAD_DIM < half,
        pltpu.roll(value, LANES - half, 1),
        pltpu.roll(value, half, 1),
    )


def fill_bias(scalars, valid_ref, bias):
    offset, prefix = scalars[0], scalars[1]
    keys = lax.broadcasted_iota(I32, (SEQ_LEN, 1), 0)
    keys = jnp.where(keys < SEQ_LEN // 2, keys + offset, keys - offset)
    queries = lax.broadcasted_iota(I32, (1, SEQ_LEN), 1)
    queries = jnp.where(queries < SEQ_LEN // 2, queries + offset, queries - offset)
    seen = jnp.where(valid_ref[...] > 0, keys, SEQ_LEN)
    shown = ((seen <= queries) | (seen < prefix)) | (keys == queries)
    bias[...] = jnp.where(shown, 0.0, -1e30)


def head_lanes(value, head):
    lane = lax.broadcasted_iota(I32, value.shape, 1)
    return jnp.where((lane >= head * HEAD_DIM) & (lane < (head + 1) * HEAD_DIM), value, 0)


def attention_kernel(
    scalars, own, other, weights, w_out, cosine, sine, valid, *refs
):
    part_own, part_other, queries, keys, values, mixed, totals = refs[-11:-4]
    bias, key_rows, value_columns, total = refs[-4:]
    step = pl.program_id(0)
    half = SEQ_LEN // 2
    upper, lower = pl.ds(0, half), pl.ds(half, half)

    @pl.when(step == 0)
    def _():
        fill_bias(scalars, valid, bias)
        total[...] = jnp.zeros_like(total)

    for source, rows in ((own, upper), (other, lower)):
        x = source[...]
        for kind, target in ((0, queries), (1, keys), (2, values)):
            y = dot_nt(x, weights[kind])
            if kind < 2:
                y = y * cosine[rows, :] + swap_halves(y) * sine[rows, :]
            target[rows, :] = y.astype(BF16)
    key_rows[...] = keys[...]
    value_columns[...] = values[...].T

    @pl.loop(0, SEQ_LEN // QUERY_BLOCK)
    def _(index):
        columns = pl.ds(pl.multiple_of(index * QUERY_BLOCK, QUERY_BLOCK), QUERY_BLOCK)
        query = queries[columns, :] * 0.125
        outs = []
        for head in range(2):
            scores = dot_nt(key_rows[...], head_lanes(query, head)) + bias[:, columns]
            top = jnp.max(scores, axis=0, keepdims=True)
            raw = jnp.exp(scores - top)
            summed = jnp.sum(raw, axis=0, keepdims=True)
            shares = (raw * (1.0 / summed)).astype(BF16)
            outs.append(dot(value_columns[head * HEAD_DIM : (head + 1) * HEAD_DIM, :], shares))
            totals[0, head : head + 1, columns] = top + jnp.log(summed)
        mixed[columns, :] = jnp.concatenate(outs, axis=0).T.astype(BF16)

    total[...] += dot(mixed[...], w_out[...])

    @pl.when(step == pl.num_programs(0) - 1)
    def _():
        part_own[...] = total[upper, :].astype(BF16)
        part_other[...] = total[lower, :].astype(BF16)


def attention_specs(pairs, width):
    whole = lambda *shape: pl.BlockSpec(shape, lambda p, s: (0,) * len(shape))
    half = SEQ_LEN // 2
    rows = whole(half, width)
    weights = pl.BlockSpec((3, LANES, width), lambda p, s: (0, p, 0))
    w_out = pl.BlockSpec((LANES, width), lambda p, s: (p, 0))
    table = whole(SEQ_LEN, LANES)
    column = pl.BlockSpec((SEQ_LEN, LANES), lambda p, s: (0, p))
    totals = pl.BlockSpec((1, 8, SEQ_LEN), lambda p, s: (p, 0, 0))
    return (rows, weights, w_out, table, whole(SEQ_LEN, 1), column, totals)


def attention_forward(scalars, own, other, weights, w_out, cosine, sine, valid, ready):
    width = own.shape[1]
    pairs = weights.shape[1] // LANES
    rows, spec_w, spec_o, table, spec_v, column, totals = attention_specs(pairs, width)
    half = SEQ_LEN // 2
    shape = jax.ShapeDtypeStruct
    return pl.pallas_call(
        attention_kernel,
        grid_spec=pltpu.PrefetchScalarGridSpec(
            num_scalar_prefetch=1,
            grid=(pairs,),
            in_specs=[rows, rows, spec_w, spec_o, table, table, spec_v]
            + [pl.BlockSpec(memory_space=pl.ANY)] * len(ready),
            out_specs=[rows, rows, column, column, column, column, totals],
            scratch_shapes=[
                pltpu.VMEM((SEQ_LEN, SEQ_LEN), F32),
                pltpu.VMEM((SEQ_LEN, LANES), BF16),
                pltpu.VMEM((LANES, SEQ_LEN), BF16),
                pltpu.VMEM((SEQ_LEN, width), F32),
            ],
        ),
        out_shape=[
            shape((half, width), BF16),
            pltpu.HBM((half, width), BF16),
            *[pltpu.HBM((SEQ_LEN, pairs * LANES), BF16)] * 4,
            shape((pairs, 8, SEQ_LEN), F32),
        ],
        compiler_params=pltpu.CompilerParams(vmem_limit_bytes=48 * 2**20),
        cost_estimate=lasting(COST_FORWARD),
        name="attention_forward",
    )(scalars, own, other, weights, w_out, cosine, sine, valid, *ready)


def attention_back_kernel(
    scalars, own, other, weights, w_out, cosine, sine, valid,
    grad_own, grad_other, queries, keys, values, mixed, totals, *refs
):
    part_own, part_other, grad_w, grad_o, gain_row = refs[-12:-7]
    bias, grad_rows, key_columns, total, grad_q, grad_k, grad_v = refs[-7:]
    step = pl.program_id(0)
    half = SEQ_LEN // 2
    upper, lower = pl.ds(0, half), pl.ds(half, half)

    @pl.when(step == 0)
    def _():
        fill_bias(scalars, valid, bias)
        total[...] = jnp.zeros_like(total)

    grad_rows[upper, :] = dot_nt(grad_own[...], w_out[...]).astype(BF16)
    grad_rows[lower, :] = dot_nt(grad_other[...], w_out[...]).astype(BF16)
    columns_mixed = mixed[...].T
    grad_o[...] = (
        dot(columns_mixed[:, :half], grad_own[...]) + dot(columns_mixed[:, half:], grad_other[...])
    ).astype(BF16)
    key_columns[...] = keys[...].T
    grad_k[...] = jnp.zeros_like(grad_k)
    grad_v[...] = jnp.zeros_like(grad_v)

    @pl.loop(0, SEQ_LEN // QUERY_BLOCK)
    def _(index):
        columns = pl.ds(pl.multiple_of(index * QUERY_BLOCK, QUERY_BLOCK), QUERY_BLOCK)
        query = queries[columns, :] * 0.125
        grad = grad_rows[columns, :]
        outs = []
        for head in range(2):
            query_head = head_lanes(query, head)
            grad_head = head_lanes(grad, head)
            scores = dot_nt(keys[...], query_head) + bias[:, columns]
            shares = jnp.exp(scores - totals[0, head : head + 1, columns])
            grad_shares = dot_nt(values[...], grad_head)
            grad_v[...] += dot(shares.astype(BF16), grad_head)
            product = shares * grad_shares
            inner = jnp.sum(product, axis=0, keepdims=True)
            grad_scores = (product - shares * inner).astype(BF16)
            grad_k[...] += dot(grad_scores, query_head)
            outs.append(dot(key_columns[head * HEAD_DIM : (head + 1) * HEAD_DIM, :], grad_scores))
        grad_q[columns, :] = jnp.concatenate(outs, axis=0).T * 0.125

    for kind, source in ((0, grad_q), (1, grad_k), (2, grad_v)):
        y = source[...]
        if kind < 2:
            y = y * cosine[...] - swap_halves(y) * sine[...]
        y = y.astype(BF16)
        total[...] += dot(y, weights[kind])
        columns_y = y.T
        grad_w[kind] = (
            dot(columns_y[:, :half], own[...]) + dot(columns_y[:, half:], other[...])
        ).astype(BF16)

    @pl.when(step == pl.num_programs(0) - 1)
    def _():
        part_own[...] = total[upper, :].astype(BF16)
        part_other[...] = total[lower, :].astype(BF16)
        product = total[upper, :] * own[...].astype(F32) + total[lower, :] * other[...].astype(F32)
        gain_row[...] = jnp.sum(product.reshape(half // 8, 8, product.shape[1]), axis=0)


def attention_backward(
    scalars, own, other, weights, w_out, cosine, sine, valid, grad_own, grad_other, saved, ready
):
    width = own.shape[1]
    pairs = weights.shape[1] // LANES
    rows, spec_w, spec_o, table, spec_v, column, totals = attention_specs(pairs, width)
    half = SEQ_LEN // 2
    shape = jax.ShapeDtypeStruct
    return pl.pallas_call(
        attention_back_kernel,
        grid_spec=pltpu.PrefetchScalarGridSpec(
            num_scalar_prefetch=1,
            grid=(pairs,),
            in_specs=[
                rows, rows, spec_w, spec_o, table, table, spec_v,
                rows, rows, column, column, column, column, totals,
                *[pl.BlockSpec(memory_space=pl.ANY)] * len(ready),
            ],
            out_specs=[
                rows,
                rows,
                spec_w,
                spec_o,
                pl.BlockSpec((8, width), lambda p, s: (0, 0)),
            ],
            scratch_shapes=[
                pltpu.VMEM((SEQ_LEN, SEQ_LEN), F32),
                pltpu.VMEM((SEQ_LEN, LANES), BF16),
                pltpu.VMEM((LANES, SEQ_LEN), BF16),
                pltpu.VMEM((SEQ_LEN, width), F32),
                *[pltpu.VMEM((SEQ_LEN, LANES), F32)] * 3,
            ],
        ),
        out_shape=[
            shape((half, width), BF16),
            pltpu.HBM((half, width), BF16),
            shape((3, pairs * LANES, width), BF16),
            shape((pairs * LANES, width), BF16),
            shape((8, width), F32),
        ],
        compiler_params=pltpu.CompilerParams(vmem_limit_bytes=48 * 2**20),
        cost_estimate=lasting(COST_BACKWARD),
        name="attention_backward",
    )(
        scalars, own, other, weights, w_out, cosine, sine, valid, grad_own, grad_other, *saved, *ready
    )


def most_tiles(rows):
    return (2 * rows + EXP_FFN * (TILE - 1)) // TILE


def most_groups(tiles, experts):
    return (tiles + experts * (GROUP - 1)) // GROUP


def expert_plan(routes, valid, chunks):
    tokens = routes.shape[0]
    rows = tokens // chunks
    tiles = most_tiles(rows)
    numbers = jnp.arange(8, dtype=I32)[:, None]
    named = ((routes[:, 0][None, :] == numbers) | (routes[:, 1][None, :] == numbers)) & (
        valid[None, :] > 0
    )
    named = (named & (numbers < EXP_FFN)).reshape(8 * chunks, rows)
    before = (jnp.arange(rows)[:, None] < jnp.arange(rows)[None, :]).astype(BF16)
    place = dot(named.astype(BF16), before).astype(I32)
    place = jnp.where(named, place, -1).reshape(8, chunks, rows)
    count = jnp.sum(named.astype(I32), axis=1).reshape(8, chunks)[:EXP_FFN]
    number = (count + TILE - 1) // TILE
    number = jnp.where(jnp.arange(chunks)[None, :] == 0, jnp.maximum(number, 1), number)
    earlier = jnp.arange(EXP_FFN)[:, None] > jnp.arange(EXP_FFN)[None, :]
    first = jnp.sum(jnp.where(earlier[:, :, None], number[None], 0), axis=1)
    total = jnp.sum(number, axis=0)
    slot = jnp.arange(tiles, dtype=I32)
    expert = jnp.sum((first + number)[:, :, None] <= slot, axis=0)
    expert = jnp.minimum(expert, EXP_FFN - 1)
    pick = jnp.arange(EXP_FFN)[:, None, None] == expert[None]
    base = (slot - jnp.sum(jnp.where(pick, first[:, :, None], 0), axis=0)) * TILE
    meta = jnp.concatenate([expert, base, total[:, None], first.T, number.T], axis=1).astype(I32)
    return (place.transpose(1, 0, 2), meta.reshape(-1), number, first)


def expert_kernel(
    tiles, span, sources, meta, chunk, place, carry, routes, w_router, w_up_all, w_down_all, *refs
):
    taken = refs[: sum(map(len, sources))]
    part, feed, x_out, hidden_out, grad_out, both_out = refs[-18:-12]
    rows = feed.shape[0]
    width = feed.shape[1]
    table, hits, picked, back, total, hidden_rows, grad_rows, both_rows = refs[-12:-4]
    w_up, w_down, load_sems, save_sems = refs[-4:]
    hidden_width = w_down.shape[1]
    offset = chunk[0] * span
    number = meta[offset + 2 * tiles]
    groups = (number + GATHER - 1) // GATHER
    span_rows = GATHER * TILE

    def loads(expert):
        slot = lax.rem(expert, 2)
        return (
            pltpu.make_async_copy(w_up_all.at[expert], w_up.at[slot], load_sems.at[slot, 0]),
            pltpu.make_async_copy(w_down_all.at[expert], w_down.at[slot], load_sems.at[slot, 1]),
        )

    def saves(tile):
        source = pl.ds(pl.multiple_of(tile * TILE, TILE), TILE)
        goal = pl.ds(pl.multiple_of((chunk[0] * tiles + tile) * TILE, TILE), TILE)
        pairs = (
            (picked.at[source, pl.ds(0, width)], x_out),
            (hidden_rows.at[source], hidden_out),
            (grad_rows.at[source], grad_out),
            (both_rows.at[source], both_out),
        )
        return [
            pltpu.make_async_copy(ref, out.at[goal], save_sems.at[tile, k])
            for k, (ref, out) in enumerate(pairs)
        ]

    for copy in loads(0):
        copy.start()

    first = 0
    for option, group in enumerate(sources):
        refs_here = taken[first : first + len(group)]
        first += len(group)

        @pl.when(chunk[1] == option)
        def _(refs_here=refs_here, group=group):
            at = {"x": 0, "cot": 0}
            for ref, kind in zip(refs_here, group):
                columns = pl.ds(0 if kind == "x" else width + LANES, width)
                table[pl.ds(at[kind], ref.shape[0]), columns] = ref[...]
                at[kind] += ref.shape[0]

    logits = dot(table[:, :width], w_router[...]) + carry[0]
    lane = lax.broadcasted_iota(I32, logits.shape, 1)
    one, two = lane == routes[0, :, 0:1], lane == routes[0, :, 1:2]
    score_one = jnp.sum(jnp.where(one, logits, 0.0), axis=1, keepdims=True)
    score_two = jnp.sum(jnp.where(two, logits, 0.0), axis=1, keepdims=True)
    top = jnp.maximum(score_one, score_two)
    score_one, score_two = jnp.exp(score_one - top), jnp.exp(score_two - top)
    both = score_one + score_two
    gates = jnp.where(one, score_one / both, 0.0) + jnp.where(two, score_two / both, 0.0)
    high = gates.astype(BF16).astype(F32)
    low = gates - high
    table[:, width : width + LANES] = (high + pltpu.roll(low, LANES // 2, 1)).astype(BF16)
    total[...] = jnp.zeros_like(total)

    @pl.loop(0, groups)
    def _(group):
        for at in range(GATHER):
            tile = group * GATHER + at
            slot = jnp.minimum(tile, tiles - 1)
            base = jnp.where(tile < number, meta[offset + tiles + slot], rows)
            row = lax.broadcasted_iota(I32, (TILE, rows), 0) + base
            hit = place[0, pl.ds(meta[offset + slot], 1), :] == row
            goal = pl.ds(pl.multiple_of(tile * TILE, TILE), TILE)
            hits[goal, :] = jnp.where(hit, 1.0, 0.0).astype(BF16)

            @pl.when(tile >= number)
            def _():
                back[goal, :] = jnp.zeros((TILE, back.shape[1]), BF16)

        here = pl.ds(pl.multiple_of(group * span_rows, TILE), span_rows)
        picked[here, :] = dot(hits[here, :], table[...]).astype(BF16)

    @pl.loop(0, EXP_FFN)
    def _(expert):
        slot = lax.rem(expert, 2)
        for copy in loads(expert):
            copy.wait()

        @pl.when(expert + 1 < EXP_FFN)
        def _():
            for copy in loads(expert + 1):
                copy.start()

        start = meta[offset + 2 * tiles + 1 + expert]
        amount = meta[offset + 2 * tiles + 1 + EXP_FFN + expert]

        @pl.loop(start, start + amount)
        def _(tile):
            mine = pl.ds(pl.multiple_of(tile * TILE, TILE), TILE)
            inputs = picked[mine, :width]
            lane = lax.broadcasted_iota(I32, (TILE, LANES), 1)
            own = (lane == expert) | (lane == expert + LANES // 2)
            scale = jnp.sum(
                jnp.where(own, picked[mine, width : width + LANES].astype(F32), 0.0),
                axis=1,
                keepdims=True,
            )
            upstream = picked[mine, width + LANES :].astype(F32)
            both = dot(inputs, w_up[slot])
            gate, up = both[:, :hidden_width], both[:, hidden_width:]
            sigma = 1.0 / (1.0 + jnp.exp(-gate))
            active = gate * sigma
            hidden = (active * up).astype(BF16)
            outputs = dot(hidden, w_down[slot])
            gate_term = jnp.sum(upstream * outputs, axis=1, keepdims=True)
            grad_row = (upstream * scale).astype(BF16)
            grad_hidden = dot_nt(grad_row, w_down[slot])
            grad_gate = (grad_hidden * up * sigma * (1.0 + gate * (1.0 - sigma))).astype(BF16)
            grad_up = (grad_hidden * active).astype(BF16)
            grad_both = jnp.concatenate([grad_gate, grad_up], axis=1)
            grad_x = dot_nt(grad_both, w_up[slot])
            hidden_rows[mine, :] = hidden
            grad_rows[mine, :] = grad_row
            both_rows[mine, :] = grad_both
            for copy in saves(tile):
                copy.start()
            back[mine, :width] = (outputs * scale).astype(BF16)
            back[mine, width : 2 * width] = grad_x.astype(BF16)
            back[mine, 2 * width :] = jnp.where(lane == expert, gate_term, 0.0).astype(BF16)

    @pl.loop(0, groups)
    def _(group):
        here = pl.ds(pl.multiple_of(group * span_rows, TILE), span_rows)
        total[...] += dot_tn(hits[here, :], back[here, :])

    feed[...] = total[:, :width].astype(BF16)
    part[:rows, :] = total[:, width : 2 * width].astype(BF16)
    terms = total[:, 2 * width :].T[:16]
    part[rows:, :] = jnp.concatenate([terms, jnp.zeros((16, width - rows), F32)], axis=1).astype(
        BF16
    )

    @pl.loop(0, number)
    def _(tile):
        for copy in saves(tile):
            copy.wait()


def expert_chunk(meta, chunk, options, place, carry, routes, w_router, w_up, w_down, saved):
    rows, width = options[0]["x"][0].shape
    sources = [[kind for kind in ("x", "cot") for _ in option[kind]] for option in options]
    taken = [ref for option in options for kind in ("x", "cot") for ref in option[kind]]
    chunks = place.shape[0]
    hidden_width = w_down.shape[1]
    tiles = most_tiles(rows)
    span = 2 * tiles + 1 + 2 * EXP_FFN
    held = (tiles + GATHER - 1) // GATHER * GATHER * TILE
    shape = jax.ShapeDtypeStruct
    whole = lambda *dims: pl.BlockSpec(dims, lambda i, m, c: (0,) * len(dims))
    mine = lambda *dims: pl.BlockSpec((1, *dims), lambda i, m, c: (c[0], 0, 0))
    stay = pl.BlockSpec(memory_space=pl.ANY)
    columns = (width, hidden_width, width, 2 * hidden_width)
    extra = () if saved is None else tuple(saved)
    return pl.pallas_call(
        functools.partial(expert_kernel, tiles, span, sources),
        grid_spec=pltpu.PrefetchScalarGridSpec(
            num_scalar_prefetch=2,
            grid=(1,),
            in_specs=[
                mine(8, rows),
                mine(rows, LANES),
                mine(rows, 2),
                whole(width, LANES),
                stay,
                stay,
                *[whole(*ref.shape) for ref in taken],
                *[stay] * len(extra),
            ],
            out_specs=[whole(rows + 16, width), whole(rows, width), *[stay] * len(columns)],
            scratch_shapes=[
                pltpu.VMEM((rows, 2 * width + LANES), BF16),
                pltpu.VMEM((held, rows), BF16),
                pltpu.VMEM((held, 2 * width + LANES), BF16),
                pltpu.VMEM((held, 2 * width + LANES), BF16),
                pltpu.VMEM((rows, 2 * width + LANES), F32),
                *[pltpu.VMEM((held, c), BF16) for c in columns[1:]],
                pltpu.VMEM((2, width, 2 * hidden_width), BF16),
                pltpu.VMEM((2, hidden_width, width), BF16),
                pltpu.SemaphoreType.DMA((2, 2)),
                pltpu.SemaphoreType.DMA((tiles, len(columns))),
            ],
        ),
        out_shape=[
            pltpu.HBM((rows + 16, width), BF16),
            pltpu.HBM((rows, width), BF16),
            *[shape((chunks * tiles * TILE, c), BF16) for c in columns],
        ],
        input_output_aliases={8 + len(taken) + k: 2 + k for k in range(len(extra))},
        compiler_params=pltpu.CompilerParams(vmem_limit_bytes=52 * 2**20),
        cost_estimate=lasting(COST_EXPERT),
        name="expert_chunk",
    )(meta, chunk, place, carry, routes, w_router, w_up, w_down, *taken, *extra)


def grad_walk(number, first, tiles):
    experts, chunks = number.shape
    flat = number.reshape(-1)
    groups = flat.shape[0]
    earlier = jnp.arange(groups)[:, None] > jnp.arange(groups)[None, :]
    start = jnp.sum(jnp.where(earlier, flat[None, :], 0), axis=1)
    held = jnp.sum(number, axis=1)
    held_groups = (held + GROUP - 1) // GROUP
    earlier = jnp.arange(experts)[:, None] > jnp.arange(experts)[None, :]
    held_start = jnp.sum(jnp.where(earlier, held[None, :], 0), axis=1)
    group_start = jnp.sum(jnp.where(earlier, held_groups[None, :], 0), axis=1)
    steps = most_groups(chunks * tiles, experts)
    everything = jnp.sum(held_groups)
    step = jnp.minimum(jnp.arange(steps, dtype=I32), everything - 1)
    owner = jnp.sum((group_start + held_groups)[:, None] <= step[None, :], axis=0)
    pick = jnp.arange(experts)[:, None] == owner[None, :]
    look = lambda values: jnp.sum(jnp.where(pick, values[:, None], 0), axis=0)
    done = (step - look(group_start)) * GROUP
    left = look(held) - done
    place_in = done[:, None] + jnp.minimum(jnp.arange(GROUP)[None, :], left[:, None] - 1)
    spot = (look(held_start)[:, None] + place_in).reshape(-1)
    group = jnp.sum((start + flat)[:, None] <= spot[None, :], axis=0)
    pick = jnp.arange(groups)[:, None] == group[None, :]
    offset = jnp.arange(chunks)[None, :] * tiles + first
    block = jnp.sum(jnp.where(pick, (offset.reshape(-1) - start)[:, None], 0), axis=0) + spot
    return jnp.concatenate([owner, block, left, everything[None]]).astype(I32)


def packing(width, hidden_width):
    columns = 2 * hidden_width
    spare = columns - width
    height = hidden_width * width // columns
    pieces = [(slice(width, width + height), slice(0, width), slice(0, height), slice(0, width))]
    short = hidden_width - height
    for at in range(width // spare):
        pieces.append(
            (
                slice(width + at * short, width + (at + 1) * short),
                slice(width, columns),
                slice(height, hidden_width),
                slice(at * spare, (at + 1) * spare),
            )
        )
    return pieces


def packed_height(width, hidden_width):
    return width + width // 2


def weight_grad_kernel(steps, walk, *refs):
    kept, packed = refs[:4], refs[4]
    rows, (sum_up, sum_down, out, load_sems, save_sems) = refs[5:9], refs[9:]
    number = walk[(2 + GROUP) * steps]
    width, hidden_width = sum_up.shape[0], sum_down.shape[0]

    def loads(step):
        slot = lax.rem(step, 2)
        copies = []
        for at in range(GROUP):
            block = walk[steps + step * GROUP + at]
            source = pl.ds(pl.multiple_of(block * TILE, TILE), TILE)
            for kind in range(4):
                copies.append(
                    pltpu.make_async_copy(
                        kept[kind].at[source],
                        rows[kind].at[slot, pl.ds(at * TILE, TILE)],
                        load_sems.at[slot, at, kind],
                    )
                )
        return copies

    def save(expert):
        slot, height = lax.rem(expert, 2), out.shape[1]
        goal = pl.ds(pl.multiple_of(expert * height, height), height)
        return pltpu.make_async_copy(out.at[slot], packed.at[goal], save_sems.at[slot])

    def store(side, up, down):
        out[side, :width] = up.astype(BF16)
        for goal, columns, source, taken in packing(width, hidden_width):
            out[side, goal, columns] = down[source, taken].astype(BF16)

    for copy in loads(0):
        copy.start()

    @pl.loop(0, number)
    def _(step):
        slot = lax.rem(step, 2)
        expert = walk[step]
        left = walk[(1 + GROUP) * steps + step]
        for copy in loads(step):
            copy.wait()

        @pl.when(step + 1 < number)
        def _():
            for copy in loads(step + 1):
                copy.start()

        row = lax.broadcasted_iota(I32, (GROUP * TILE, 1), 0)
        live = row < left * TILE
        side = lax.rem(expert, 2)

        def products():
            return (
                dot_tn(jnp.where(live, rows[0][slot], 0), rows[3][slot]),
                dot_tn(jnp.where(live, rows[1][slot], 0), rows[2][slot]),
            )

        fresh = (step == 0) | (walk[jnp.maximum(step - 1, 0)] != expert)
        done = (step == number - 1) | (walk[jnp.minimum(step + 1, steps - 1)] != expert)

        @pl.when(done & (expert >= 2))
        def _():
            save(expert - 2).wait()

        @pl.when(fresh & done)
        def _():
            store(side, *products())

        @pl.when(fresh & jnp.logical_not(done))
        def _():
            sum_up[...], sum_down[...] = products()

        @pl.when(jnp.logical_not(fresh | done))
        def _():
            up, down = products()
            sum_up[...] += up
            sum_down[...] += down

        @pl.when(jnp.logical_not(fresh) & done)
        def _():
            up, down = products()
            store(side, sum_up[...] + up, sum_down[...] + down)

        @pl.when(done)
        def _():
            save(expert).start()

    for expert in (EXP_FFN - 2, EXP_FFN - 1):
        save(expert).wait()


def weight_grads(walk, saved):
    width, hidden_width = saved[0].shape[1], saved[1].shape[1]
    height = packed_height(width, hidden_width)
    steps = most_groups(saved[0].shape[0] // TILE, EXP_FFN)
    shape = jax.ShapeDtypeStruct
    stay = pl.BlockSpec(memory_space=pl.ANY)
    return pl.pallas_call(
        functools.partial(weight_grad_kernel, steps),
        grid_spec=pltpu.PrefetchScalarGridSpec(
            num_scalar_prefetch=1,
            grid=(1,),
            in_specs=[stay] * 4,
            out_specs=stay,
            scratch_shapes=[
                *[pltpu.VMEM((2, GROUP * TILE, kept.shape[1]), BF16) for kept in saved],
                pltpu.VMEM((width, 2 * hidden_width), F32),
                pltpu.VMEM((hidden_width, width), F32),
                pltpu.VMEM((2, height, 2 * hidden_width), BF16),
                pltpu.SemaphoreType.DMA((2, GROUP, 4)),
                pltpu.SemaphoreType.DMA((2,)),
            ],
        ),
        out_shape=shape((EXP_FFN * height, 2 * hidden_width), BF16),
        compiler_params=pltpu.CompilerParams(vmem_limit_bytes=48 * 2**20),
        cost_estimate=lasting(COST_GRADS),
        name="weight_grads",
    )(walk, *saved)


def widen_kernel(source, up, down):
    width = down.shape[1]
    split = source.shape[1] // LANES
    for row in range(split):
        at = row % 2 * (source.shape[1] // 2) + row // 2 * LANES
        up[pl.ds(row, width, stride=split), :] = source[:width, at : at + LANES].astype(F32)
    for place, columns, goal, taken in packing(width, down.shape[0]):
        down[goal, taken] = source[place, columns].astype(F32)


def widen(packed, width, hidden_width):
    height = packed_height(width, hidden_width)
    rows = width * packed.shape[1] // LANES
    shape = jax.ShapeDtypeStruct
    return pl.pallas_call(
        widen_kernel,
        grid=(EXP_FFN,),
        in_specs=[pl.BlockSpec((height, packed.shape[1]), lambda i: (i, 0))],
        out_specs=[
            pl.BlockSpec((rows, LANES), lambda i: (i, 0)),
            pl.BlockSpec((hidden_width, width), lambda i: (i, 0)),
        ],
        out_shape=[
            shape((EXP_FFN * rows, LANES), F32),
            shape((EXP_FFN * hidden_width, width), F32),
        ],
        compiler_params=pltpu.CompilerParams(vmem_limit_bytes=60 * 2**20),
        cost_estimate=lasting(COST_WIDEN),
        name="widen",
    )(packed)


def shards(
    dp_size,
    stream,
    cotangent,
    gain_attention,
    w_inputs,
    w_output,
    gain_experts,
    w_router,
    w_carry,
    w_gate_up,
    w_down,
    w_constant,
    constant_vectors,
    previous_logits,
    routes,
    valid,
    prefix,
):
    rows, width = stream.shape
    tokens = routes.shape[0]
    chunks = tokens // rows
    head_columns = w_inputs.shape[2]
    here = lax.axis_index("tensor")
    index = lax.axis_index("dp")
    outer = (here == 0) | (here == chunks - 1)
    bits = list(range(dp_size.bit_length() - 1))
    first_row = here * rows
    valid_all = valid.astype(F32)
    cut = lambda array, at: lax.dynamic_slice_in_dim(array, at, rows, 0)
    valid_here = cut(valid_all, first_row)
    routes_here = cut(routes, first_row)
    previous_here = cut(previous_logits, first_row)

    w_in_rows = w_inputs.transpose(0, 2, 1)
    packed = jnp.concatenate([w_in_rows, w_output[None]], axis=0).reshape(-1, width)
    piece_rows = packed.shape[0] // dp_size
    position = (index >> 1) | ((index & 1) << (len(bits) - 1))
    piece = lax.dynamic_slice_in_dim(packed, position * piece_rows, piece_rows, 0)
    normed_here, inverse_one = norm_forward(stream, gain_attention)
    normed_low = normed_here.astype(BF16)
    normed_other = along_z(normed_low, SIDE)
    piece = along_z(piece, CROSS)
    cot_low = behind(cotangent, piece).astype(BF16)
    cot_side, cot_middle = along_z(cot_low, SIDE), along_z(cot_low, MIDDLE)
    for level, bit in enumerate([*bits[1:], bits[0]]):
        if level == 0:
            place, meta, number, first = expert_plan(*behind((routes, valid), piece), chunks)
        if level == 1:
            number, first = behind((number, first), piece)
            walk = grad_walk(number, first, most_tiles(rows))
        other = along_dp(piece, bit, dp_size)
        piece = jnp.where(
            (index >> bit) & 1 == 0,
            jnp.concatenate([piece, other], axis=0),
            jnp.concatenate([other, piece], axis=0),
        )
    carry = jnp.dot(behind(previous_logits, place), w_carry, precision=HIGHEST, preferred_element_type=F32)
    columns = carry.shape[1]
    carry_wide = jnp.pad(carry, ((0, 0), (0, LANES - columns))).reshape(chunks, rows, LANES)
    routes_live = jnp.where(valid[:, None] > 0, routes, -1).reshape(chunks, rows, 2)
    router_wide = jnp.pad(w_router, ((0, 0), (0, LANES - columns)))
    partner = piece.reshape(4, head_columns, width)
    both_in = jnp.concatenate([w_in_rows, partner[:3]], axis=1)
    both_out = jnp.concatenate([w_output, partner[3]], axis=0)

    core = index & 1
    offset = (here % 2) * rows
    sequence = here // 2
    scalars = jnp.stack([offset, prefix[sequence]]).astype(I32)
    cosine, sine = rope_tables(offset)
    valid_rows = jnp.concatenate([cut(valid, first_row), cut(valid, (here ^ 1) * rows)])[:, None]
    fixed = (both_in, both_out, cosine, sine, valid_rows)
    ready = (place, meta, walk, cot_side, cot_middle, carry_wide, routes_live, router_wide)
    part_own, part_other, *saved_attention = attention_forward(
        scalars, normed_low, normed_other, *fixed, ready
    )
    attention_other = along_z(part_other, SIDE)

    cot_far, cot_across = along_z(cot_middle, OUTWARD), along_z(cot_side, MIDDLE)
    cot_far, cot_across = behind((cot_far, cot_across), part_own)
    w_up = behind(w_gate_up, (part_own, cot_far, cot_across)).reshape(EXP_FFN, width, -1)
    attention_other = behind(attention_other, w_up)
    attention = part_own.astype(F32) + attention_other.astype(F32)
    middle = stream + attention
    second, inverse_two = norm_forward(middle, gain_experts)
    second_low = second.astype(BF16)

    which = slot_chunks(here)

    def chunk(slot, options, saved):
        choice = outer.astype(I32) * (len(options) - 1)
        return expert_chunk(
            meta,
            jnp.stack([which[slot], choice]),
            options,
            place,
            carry_wide,
            routes_live,
            router_wide,
            w_up,
            w_down,
            saved,
        )

    third_rows = rows // 3 // 16 * 16
    cuts = (0, third_rows, 2 * third_rows, rows)
    cot_pieces = [cot_across[low:high] for low, high in zip(cuts[:-1], cuts[1:])]
    side, middle_rows = along_z(second_low, SIDE), along_z(second_low, MIDDLE)
    cot_last = [along_z(behind(cot_pieces[0], second_low), OUTWARD)]
    part_0, feed_0, *saved = chunk(0, [{"x": [second_low], "cot": [cot_low]}], None)
    side, middle_rows, cot_last[0] = behind((side, middle_rows, cot_last[0]), part_0)
    far, across = along_z(middle_rows, OUTWARD), along_z(side, MIDDLE)
    cot_last.append(along_z(behind(cot_pieces[1], part_0), OUTWARD))
    part_1, feed_1, *saved = chunk(1, [{"x": [side], "cot": [cot_side]}], saved)
    near, feed_near = along_z(part_1, INWARD), along_z(feed_1, INWARD)
    far, across, cot_last[1] = behind((far, across, cot_last[1]), part_1)
    last = along_z(across, OUTWARD)
    cot_last.append(along_z(behind(cot_pieces[2], part_1), OUTWARD))
    part_2, feed_2, *saved = chunk(
        2, [{"x": [middle_rows], "cot": [cot_middle]}, {"x": [far], "cot": [cot_far]}], saved
    )
    third = along_z(part_2, INWARD)
    last, cot_last[2] = behind((last, cot_last[2]), part_2)
    part_3, feed_3, *saved = chunk(
        3,
        [{"x": [across], "cot": [cot_across]}, {"x": [last], "cot": cot_last}],
        saved,
    )

    inward = along_z(part_3, INWARD)
    packed = weight_grads(walk, saved)
    inward, packed = lax.optimization_barrier((inward, packed))
    packed = lax.psum_scatter(packed, "dp", scatter_dimension=0, tiled=True)
    feed_outward = along_z(behind(feed_3, inward), INWARD)
    inward = part_3 + inward
    inward, feed_outward = lax.optimization_barrier((along_z(inward, MIDDLE), feed_outward))
    third = along_z(part_2 + third, MIDDLE)
    outward = along_z(part_1 + inward, OUTWARD)
    summed = part_0.astype(F32) + near.astype(F32) + third.astype(F32) + outward.astype(F32)

    logits = dot(second_low, w_router) + cut(carry, first_row)
    picked = routes_here[:, :, None] == jnp.arange(columns, dtype=I32)[None, None, :]
    chosen = jnp.sum(jnp.where(picked, logits[:, None, :], 0.0), axis=-1)
    gates_here = jax.nn.softmax(chosen, axis=-1)
    live_gates = gates_here * valid_here[:, None]
    copy_gate = jnp.sum(jnp.where(routes_here == EXP_FFN + 1, live_gates, 0.0), axis=-1)
    constant_gates = jnp.stack(
        [
            jnp.sum(jnp.where(routes_here == EXP_FFN + 2 + number, live_gates, 0.0), axis=-1)
            for number in range(2)
        ],
        axis=1,
    )
    alphas = jax.nn.softmax(
        jnp.einsum("td,cad->tca", second, w_constant, precision=HIGHEST, preferred_element_type=F32),
        axis=-1,
    )
    constant_out = (
        alphas[:, :, 0:1] * second[:, None, :] + alphas[:, :, 1:2] * constant_vectors[None, :, :]
    )
    extra = copy_gate[:, None] * second + jnp.sum(
        constant_gates[:, :, None] * constant_out, axis=1
    )
    copy_terms = jnp.sum(cotangent * second, axis=-1)
    constant_terms = jnp.sum(cotangent[:, None, :] * constant_out, axis=-1)
    grad_constant_out = constant_gates[:, :, None] * cotangent[:, None, :]
    grad_vectors = jnp.sum(alphas[:, :, 1:2] * grad_constant_out, axis=0)
    grad_alphas = jnp.stack(
        [
            jnp.sum(grad_constant_out * second[:, None, :], axis=-1),
            jnp.sum(grad_constant_out * constant_vectors[None, :, :], axis=-1),
        ],
        axis=-1,
    )
    grad_mix = alphas * (grad_alphas - jnp.sum(alphas * grad_alphas, axis=-1, keepdims=True))
    grad_constant = jnp.einsum(
        "tca,td->cad", grad_mix, second, precision=HIGHEST, preferred_element_type=F32
    )
    grad_local = (
        copy_gate[:, None] * cotangent
        + jnp.sum(alphas[:, :, 0:1] * grad_constant_out, axis=1)
        + jnp.einsum(
            "tca,cad->td", grad_mix, w_constant, precision=HIGHEST, preferred_element_type=F32
        )
    )

    gate_grads = summed[rows : rows + EXP_FFN, :rows].T
    gate_table = jnp.concatenate(
        [gate_grads, jnp.zeros((rows, 1), F32), copy_terms[:, None], constant_terms], axis=1
    )
    grad_gates = jnp.sum(jnp.where(picked, gate_table[:, None, :], 0.0), axis=-1)
    grad_gates = grad_gates * valid_here[:, None]
    grad_chosen = gates_here * (
        grad_gates - jnp.sum(gates_here * grad_gates, axis=-1, keepdims=True)
    )
    grad_logits = jnp.sum(jnp.where(picked, grad_chosen[:, :, None], 0.0), axis=1)
    grad_router = jnp.dot(
        second_low.astype(F32).T, grad_logits, precision=HIGHEST, preferred_element_type=F32
    )
    grad_carry = jnp.dot(
        previous_here.T, grad_logits, precision=HIGHEST, preferred_element_type=F32
    )
    grad_previous = jnp.dot(
        grad_logits, w_carry.T, precision=HIGHEST, preferred_element_type=F32
    )
    grad_second = (
        summed[:rows]
        + grad_local
        + jnp.dot(
            grad_logits, w_router.astype(F32).T, precision=HIGHEST, preferred_element_type=F32
        )
    )
    grad_gain_experts = jnp.sum(grad_second * middle * inverse_two, axis=0)
    grad_middle = cotangent + norm_backward(middle, inverse_two, gain_experts, grad_second)

    grad_low = grad_middle.astype(BF16)
    grad_other = along_z(grad_low, SIDE)
    feed_outward = feed_3 + feed_outward

    part_own, part_other, grad_w, grad_o, gain_rows = attention_backward(
        scalars, normed_low, normed_other, *fixed, grad_low, grad_other, saved_attention, ()
    )
    grad_normed = part_own.astype(F32) + along_z(part_other, SIDE).astype(F32)
    grad_stream = grad_middle + norm_backward(stream, inverse_one, gain_attention, grad_normed)

    feed_2, feed_outward = behind((feed_2, feed_outward), part_own)
    feed_third, feed_outward = along_z(feed_2, INWARD), along_z(feed_outward, MIDDLE)
    feed_third = along_z(feed_2 + feed_third, MIDDLE)
    feed_outward = along_z(feed_1 + feed_outward, OUTWARD)
    feed = feed_0.astype(F32) + feed_near.astype(F32)
    feed = feed + feed_third.astype(F32) + feed_outward.astype(F32)
    experts = feed + extra
    block_out = middle + experts
    squares = [
        jnp.sum(valid_here[:, None] * part * part) for part in (block_out, attention, experts)
    ]
    squares = jnp.stack([*squares, jnp.sum(valid_here)])

    own_grads = jnp.concatenate([grad_w[:, :head_columns], grad_o[None, :head_columns]], axis=0)
    far_grads = jnp.concatenate([grad_w[:, head_columns:], grad_o[None, head_columns:]], axis=0)
    order = bits
    own_piece = reduce_blocks(own_grads.reshape(-1, width), order[:1], index, dp_size)
    far_piece = reduce_blocks(far_grads.reshape(-1, width), order[:1], index, dp_size)
    packed = lax.all_gather(behind(packed, part_own), "dp", axis=0, tiled=True)
    own_piece = reduce_blocks(own_piece, order[1:], index, dp_size)
    far_piece = reduce_blocks(far_piece, order[1:], index, dp_size)
    own_piece = own_piece + along_z(far_piece, CROSS)
    grad_gate_up, grad_down = widen(packed, width, w_down.shape[1])
    grad_gate_up = grad_gate_up.reshape(EXP_FFN, width, -1, 2, LANES).transpose(0, 1, 3, 2, 4)
    grad_gate_up = grad_gate_up.reshape(EXP_FFN, width, 2, -1)
    grad_down = grad_down.reshape(EXP_FFN, -1, width)

    attention_grads = spread_blocks(own_piece, order, index, dp_size).astype(F32)
    attention_grads = attention_grads.reshape(4, head_columns, width)
    grad_inputs = attention_grads[:3].transpose(0, 2, 1)
    grad_output = attention_grads[3]

    wide = lambda array: jnp.pad(array, ((0, 0), (0, width - array.shape[1])))
    small = jnp.concatenate(
        [
            grad_gain_experts[None],
            grad_router.T,
            wide(grad_carry),
            grad_constant.reshape(-1, width),
            grad_vectors,
            wide(squares[None]),
            jnp.sum(gain_rows, axis=0, keepdims=True) / gain_attention[None],
        ],
        axis=0,
    )
    small = sum_everywhere(small, bits, dp_size, grad_down)
    at = 1 + 2 * columns
    squares = small[at + 6, :3]
    counted = small[at + 6, 3]
    rms_values = jnp.sqrt(squares / (jnp.maximum(counted, 1.0) * width))
    return (
        block_out,
        grad_stream,
        small[at + 7],
        grad_inputs,
        grad_output,
        small[0],
        small[1 : 1 + columns].T,
        small[1 + columns : at, :columns],
        grad_gate_up,
        grad_down,
        small[at : at + 4].reshape(2, 2, width),
        small[at + 4 : at + 6],
        grad_previous,
        rms_values,
    )


def solution(mesh):
    return jax.shard_map(
        functools.partial(shards, mesh.shape["dp"]),
        mesh=mesh,
        in_specs=(
            P(("dp", "tensor"), None),
            P(("dp", "tensor"), None),
            P(),
            P(None, None, "tensor"),
            P("tensor", None),
            P(),
            P(),
            P(),
            P(None, None, None, "tensor"),
            P(None, "tensor", None),
            P(),
            P(),
            P("dp", None),
            P("dp", None),
            P("dp"),
            P("dp"),
        ),
        out_specs=(
            P(("dp", "tensor"), None),
            P(("dp", "tensor"), None),
            P(),
            P(None, None, "tensor"),
            P("tensor", None),
            P(),
            P(),
            P(),
            P(None, None, None, "tensor"),
            P(None, "tensor", None),
            P(),
            P(),
            P(("dp", "tensor"), None),
            P(),
        ),
        check_vma=False,
    )
```

```python
import functools

import jax
import jax.numpy as jnp
from jax import lax
from jax.experimental import pallas as pl
from jax.experimental.pallas import tpu as pltpu
from jax.sharding import PartitionSpec as P

HEAD_DIM = 64
EXP_FFN = 6
SEQ_LEN = 1024
EPSILON = 1e-05
HIGHEST = lax.Precision.HIGHEST
F32 = jnp.float32
BF16 = jnp.bfloat16
I32 = jnp.int32

LANES = 128
TILE = 128
QUERY_BLOCK = 1024
GROUP = 4
GATHER = 2
COST_FORWARD, COST_BACKWARD, COST_EXPERT, COST_GRADS, COST_WIDEN, COST_ADD = 20, 32, 20, 11, 3, 3


def lasting(microseconds):
    return pl.CostEstimate(flops=0, bytes_accessed=microseconds * 3 * 10**6, transcendentals=0)


SIDE = ((0, 1), (1, 0), (2, 3), (3, 2))
CROSS = ((0, 2), (1, 3), (2, 0), (3, 1))
MIDDLE = ((1, 2), (2, 1))
OUTWARD = ((1, 0), (2, 3))
INWARD = ((0, 1), (3, 2))


def dot(left, right):
    return jnp.dot(left, right, preferred_element_type=F32)


def dot_nt(left, right):
    return lax.dot_general(left, right, (((1,), (1,)), ((), ())), preferred_element_type=F32)


def dot_tn(left, right):
    return lax.dot_general(left, right, (((0,), (0,)), ((), ())), preferred_element_type=F32)


def norm_forward(values, gain):
    inverse = lax.rsqrt(jnp.mean(values * values, axis=-1, keepdims=True) + EPSILON)
    return (values * inverse * gain, inverse)


def norm_backward(values, inverse, gain, grad):
    scaled = grad * gain
    inner = jnp.mean(scaled * values, axis=-1, keepdims=True)
    return inverse * scaled - values * inverse**3 * inner


def along_z(value, pairs):
    return lax.ppermute(value, "tensor", pairs)


def along_dp(value, bit, size):
    return lax.ppermute(value, "dp", [(i, i ^ (1 << bit)) for i in range(size)])


def behind(value, earlier):
    return lax.optimization_barrier((value, earlier))[0]


def slot_chunks(here):
    table = jnp.array([[0, 1, 2, 3], [1, 0, 2, 3], [2, 3, 1, 0], [3, 2, 1, 0]], I32)
    return lax.dynamic_slice_in_dim(table, here, 1, 0)[0]


def reduce_blocks(value, bits, index, size):
    for bit in bits:
        half = value.shape[0] // 2
        mine = (index >> bit) & 1
        sent = lax.dynamic_slice_in_dim(value, (1 - mine) * half, half, 0)
        kept = lax.dynamic_slice_in_dim(value, mine * half, half, 0)
        value = kept + along_dp(sent, bit, size)
    return value


def spread_blocks(value, bits, index, size):
    for bit in reversed(bits):
        mine = (index >> bit) & 1
        other = along_dp(value, bit, size)
        value = jnp.where(
            mine == 0,
            jnp.concatenate([value, other], axis=0),
            jnp.concatenate([other, value], axis=0),
        )
    return value


def sum_everywhere(value, bits, size, beside):
    value = value + along_z(value, SIDE)
    value = value + along_z(value, CROSS)
    for bit in bits[1:]:
        value = value + along_dp(value, bit, size)
    return value + behind(along_dp(value, bits[0], size), beside)


def rope_tables(offset):
    lane = jnp.arange(LANES, dtype=I32)
    row = jnp.arange(SEQ_LEN, dtype=I32)
    position = jnp.where(row < SEQ_LEN // 2, row + offset, row - offset).astype(F32)
    half = HEAD_DIM // 2
    frequency = 10000.0 ** (-(lane % half).astype(F32) / half)
    angles = position[:, None] * frequency[None, :]
    sign = jnp.where(lane % HEAD_DIM < half, -1.0, 1.0)
    return (jnp.cos(angles), jnp.sin(angles) * sign[None, :])


def swap_halves(value):
    half = HEAD_DIM // 2
    lane = lax.broadcasted_iota(I32, value.shape, 1)
    return jnp.where(
        lane % HEAD_DIM < half,
        pltpu.roll(value, LANES - half, 1),
        pltpu.roll(value, half, 1),
    )


def fill_bias(scalars, valid_ref, bias):
    offset, prefix = scalars[0], scalars[1]
    keys = lax.broadcasted_iota(I32, (SEQ_LEN, 1), 0)
    keys = jnp.where(keys < SEQ_LEN // 2, keys + offset, keys - offset)
    queries = lax.broadcasted_iota(I32, (1, SEQ_LEN), 1)
    queries = jnp.where(queries < SEQ_LEN // 2, queries + offset, queries - offset)
    seen = jnp.where(valid_ref[...] > 0, keys, SEQ_LEN)
    shown = ((seen <= queries) | (seen < prefix)) | (keys == queries)
    bias[...] = jnp.where(shown, 0.0, -1e30)


def head_lanes(value, head):
    lane = lax.broadcasted_iota(I32, value.shape, 1)
    return jnp.where((lane >= head * HEAD_DIM) & (lane < (head + 1) * HEAD_DIM), value, 0)


def attention_kernel(
    scalars, own, other, weights, w_out, cosine, sine, valid, *refs
):
    part_own, part_other, queries, keys, values, mixed, totals = refs[-11:-4]
    bias, key_rows, value_columns, total = refs[-4:]
    step = pl.program_id(0)
    half = SEQ_LEN // 2
    upper, lower = pl.ds(0, half), pl.ds(half, half)

    @pl.when(step == 0)
    def _():
        fill_bias(scalars, valid, bias)
        total[...] = jnp.zeros_like(total)

    for source, rows in ((own, upper), (other, lower)):
        x = source[...]
        for kind, target in ((0, queries), (1, keys), (2, values)):
            y = dot_nt(x, weights[kind])
            if kind < 2:
                y = y * cosine[rows, :] + swap_halves(y) * sine[rows, :]
            target[rows, :] = y.astype(BF16)
    key_rows[...] = keys[...]
    value_columns[...] = values[...].T

    @pl.loop(0, SEQ_LEN // QUERY_BLOCK)
    def _(index):
        columns = pl.ds(pl.multiple_of(index * QUERY_BLOCK, QUERY_BLOCK), QUERY_BLOCK)
        query = queries[columns, :] * 0.125
        outs = []
        for head in range(2):
            scores = dot_nt(key_rows[...], head_lanes(query, head)) + bias[:, columns]
            top = jnp.max(scores, axis=0, keepdims=True)
            raw = jnp.exp(scores - top)
            summed = jnp.sum(raw, axis=0, keepdims=True)
            shares = (raw * (1.0 / summed)).astype(BF16)
            outs.append(dot(value_columns[head * HEAD_DIM : (head + 1) * HEAD_DIM, :], shares))
            totals[0, head : head + 1, columns] = top + jnp.log(summed)
        mixed[columns, :] = jnp.concatenate(outs, axis=0).T.astype(BF16)

    total[...] += dot(mixed[...], w_out[...])

    @pl.when(step == pl.num_programs(0) - 1)
    def _():
        part_own[...] = total[upper, :].astype(BF16)
        part_other[...] = total[lower, :].astype(BF16)


def attention_specs(pairs, width):
    whole = lambda *shape: pl.BlockSpec(shape, lambda p, s: (0,) * len(shape))
    half = SEQ_LEN // 2
    rows = whole(half, width)
    weights = pl.BlockSpec((3, LANES, width), lambda p, s: (0, p, 0))
    w_out = pl.BlockSpec((LANES, width), lambda p, s: (p, 0))
    table = whole(SEQ_LEN, LANES)
    column = pl.BlockSpec((SEQ_LEN, LANES), lambda p, s: (0, p))
    totals = pl.BlockSpec((1, 8, SEQ_LEN), lambda p, s: (p, 0, 0))
    return (rows, weights, w_out, table, whole(SEQ_LEN, 1), column, totals)


def attention_forward(scalars, own, other, weights, w_out, cosine, sine, valid, ready):
    width = own.shape[1]
    pairs = weights.shape[1] // LANES
    rows, spec_w, spec_o, table, spec_v, column, totals = attention_specs(pairs, width)
    half = SEQ_LEN // 2
    shape = jax.ShapeDtypeStruct
    return pl.pallas_call(
        attention_kernel,
        grid_spec=pltpu.PrefetchScalarGridSpec(
            num_scalar_prefetch=1,
            grid=(pairs,),
            in_specs=[rows, rows, spec_w, spec_o, table, table, spec_v]
            + [pl.BlockSpec(memory_space=pl.ANY)] * len(ready),
            out_specs=[rows, rows, column, column, column, column, totals],
            scratch_shapes=[
                pltpu.VMEM((SEQ_LEN, SEQ_LEN), F32),
                pltpu.VMEM((SEQ_LEN, LANES), BF16),
                pltpu.VMEM((LANES, SEQ_LEN), BF16),
                pltpu.VMEM((SEQ_LEN, width), F32),
            ],
        ),
        out_shape=[
            shape((half, width), BF16),
            pltpu.HBM((half, width), BF16),
            *[pltpu.HBM((SEQ_LEN, pairs * LANES), BF16)] * 4,
            shape((pairs, 8, SEQ_LEN), F32),
        ],
        compiler_params=pltpu.CompilerParams(vmem_limit_bytes=48 * 2**20),
        cost_estimate=lasting(COST_FORWARD),
        name="attention_forward",
    )(scalars, own, other, weights, w_out, cosine, sine, valid, *ready)


def attention_back_kernel(
    scalars, own, other, weights, w_out, cosine, sine, valid,
    grad_own, grad_other, queries, keys, values, mixed, totals, *refs
):
    part_own, part_other, grad_w, grad_o, gain_row = refs[-12:-7]
    bias, grad_rows, key_columns, total, grad_q, grad_k, grad_v = refs[-7:]
    step = pl.program_id(0)
    half = SEQ_LEN // 2
    upper, lower = pl.ds(0, half), pl.ds(half, half)

    @pl.when(step == 0)
    def _():
        fill_bias(scalars, valid, bias)
        total[...] = jnp.zeros_like(total)

    grad_rows[upper, :] = dot_nt(grad_own[...], w_out[...]).astype(BF16)
    grad_rows[lower, :] = dot_nt(grad_other[...], w_out[...]).astype(BF16)
    columns_mixed = mixed[...].T
    grad_o[...] = (
        dot(columns_mixed[:, :half], grad_own[...]) + dot(columns_mixed[:, half:], grad_other[...])
    ).astype(BF16)
    key_columns[...] = keys[...].T
    grad_k[...] = jnp.zeros_like(grad_k)
    grad_v[...] = jnp.zeros_like(grad_v)

    @pl.loop(0, SEQ_LEN // QUERY_BLOCK)
    def _(index):
        columns = pl.ds(pl.multiple_of(index * QUERY_BLOCK, QUERY_BLOCK), QUERY_BLOCK)
        query = queries[columns, :] * 0.125
        grad = grad_rows[columns, :]
        outs = []
        for head in range(2):
            query_head = head_lanes(query, head)
            grad_head = head_lanes(grad, head)
            scores = dot_nt(keys[...], query_head) + bias[:, columns]
            shares = jnp.exp(scores - totals[0, head : head + 1, columns])
            grad_shares = dot_nt(values[...], grad_head)
            grad_v[...] += dot(shares.astype(BF16), grad_head)
            product = shares * grad_shares
            inner = jnp.sum(product, axis=0, keepdims=True)
            grad_scores = (product - shares * inner).astype(BF16)
            grad_k[...] += dot(grad_scores, query_head)
            outs.append(dot(key_columns[head * HEAD_DIM : (head + 1) * HEAD_DIM, :], grad_scores))
        grad_q[columns, :] = jnp.concatenate(outs, axis=0).T * 0.125

    for kind, source in ((0, grad_q), (1, grad_k), (2, grad_v)):
        y = source[...]
        if kind < 2:
            y = y * cosine[...] - swap_halves(y) * sine[...]
        y = y.astype(BF16)
        total[...] += dot(y, weights[kind])
        columns_y = y.T
        grad_w[kind] = (
            dot(columns_y[:, :half], own[...]) + dot(columns_y[:, half:], other[...])
        ).astype(BF16)

    @pl.when(step == pl.num_programs(0) - 1)
    def _():
        part_own[...] = total[upper, :].astype(BF16)
        part_other[...] = total[lower, :].astype(BF16)
        product = total[upper, :] * own[...].astype(F32) + total[lower, :] * other[...].astype(F32)
        gain_row[...] = jnp.sum(product.reshape(half // 8, 8, product.shape[1]), axis=0)


def attention_backward(
    scalars, own, other, weights, w_out, cosine, sine, valid, grad_own, grad_other, saved, ready
):
    width = own.shape[1]
    pairs = weights.shape[1] // LANES
    rows, spec_w, spec_o, table, spec_v, column, totals = attention_specs(pairs, width)
    half = SEQ_LEN // 2
    shape = jax.ShapeDtypeStruct
    return pl.pallas_call(
        attention_back_kernel,
        grid_spec=pltpu.PrefetchScalarGridSpec(
            num_scalar_prefetch=1,
            grid=(pairs,),
            in_specs=[
                rows, rows, spec_w, spec_o, table, table, spec_v,
                rows, rows, column, column, column, column, totals,
                *[pl.BlockSpec(memory_space=pl.ANY)] * len(ready),
            ],
            out_specs=[
                rows,
                rows,
                spec_w,
                spec_o,
                pl.BlockSpec((8, width), lambda p, s: (0, 0)),
            ],
            scratch_shapes=[
                pltpu.VMEM((SEQ_LEN, SEQ_LEN), F32),
                pltpu.VMEM((SEQ_LEN, LANES), BF16),
                pltpu.VMEM((LANES, SEQ_LEN), BF16),
                pltpu.VMEM((SEQ_LEN, width), F32),
                *[pltpu.VMEM((SEQ_LEN, LANES), F32)] * 3,
            ],
        ),
        out_shape=[
            shape((half, width), BF16),
            pltpu.HBM((half, width), BF16),
            shape((3, pairs * LANES, width), BF16),
            shape((pairs * LANES, width), BF16),
            shape((8, width), F32),
        ],
        compiler_params=pltpu.CompilerParams(vmem_limit_bytes=48 * 2**20),
        cost_estimate=lasting(COST_BACKWARD),
        name="attention_backward",
    )(
        scalars, own, other, weights, w_out, cosine, sine, valid, grad_own, grad_other, *saved, *ready
    )


def most_tiles(rows):
    return (2 * rows + EXP_FFN * (TILE - 1)) // TILE


def most_groups(tiles, experts):
    return (tiles + experts * (GROUP - 1)) // GROUP


def expert_plan(routes, valid, chunks):
    tokens = routes.shape[0]
    rows = tokens // chunks
    tiles = most_tiles(rows)
    numbers = jnp.arange(8, dtype=I32)[:, None]
    named = ((routes[:, 0][None, :] == numbers) | (routes[:, 1][None, :] == numbers)) & (
        valid[None, :] > 0
    )
    named = (named & (numbers < EXP_FFN)).reshape(8 * chunks, rows)
    before = (jnp.arange(rows)[:, None] < jnp.arange(rows)[None, :]).astype(BF16)
    place = dot(named.astype(BF16), before).astype(I32)
    place = jnp.where(named, place, -1).reshape(8, chunks, rows)
    count = jnp.sum(named.astype(I32), axis=1).reshape(8, chunks)[:EXP_FFN]
    number = (count + TILE - 1) // TILE
    number = jnp.where(jnp.arange(chunks)[None, :] == 0, jnp.maximum(number, 1), number)
    earlier = jnp.arange(EXP_FFN)[:, None] > jnp.arange(EXP_FFN)[None, :]
    first = jnp.sum(jnp.where(earlier[:, :, None], number[None], 0), axis=1)
    total = jnp.sum(number, axis=0)
    slot = jnp.arange(tiles, dtype=I32)
    expert = jnp.sum((first + number)[:, :, None] <= slot, axis=0)
    expert = jnp.minimum(expert, EXP_FFN - 1)
    pick = jnp.arange(EXP_FFN)[:, None, None] == expert[None]
    base = (slot - jnp.sum(jnp.where(pick, first[:, :, None], 0), axis=0)) * TILE
    meta = jnp.concatenate([expert, base, total[:, None], first.T, number.T], axis=1).astype(I32)
    return (place.transpose(1, 0, 2), meta.reshape(-1), number, first)


def expert_kernel(
    tiles, span, sources, meta, chunk, place, carry, routes, w_router, w_up_all, w_down_all, *refs
):
    taken = refs[: sum(map(len, sources))]
    part, feed, x_out, hidden_out, grad_out, both_out = refs[-18:-12]
    rows = feed.shape[0]
    width = feed.shape[1]
    table, hits, picked, back, total, hidden_rows, grad_rows, both_rows = refs[-12:-4]
    w_up, w_down, load_sems, save_sems = refs[-4:]
    hidden_width = w_down.shape[1]
    offset = chunk[0] * span
    number = meta[offset + 2 * tiles]
    groups = (number + GATHER - 1) // GATHER
    span_rows = GATHER * TILE

    def loads(expert):
        slot = lax.rem(expert, 2)
        return (
            pltpu.make_async_copy(w_up_all.at[expert], w_up.at[slot], load_sems.at[slot, 0]),
            pltpu.make_async_copy(w_down_all.at[expert], w_down.at[slot], load_sems.at[slot, 1]),
        )

    def saves(tile):
        source = pl.ds(pl.multiple_of(tile * TILE, TILE), TILE)
        goal = pl.ds(pl.multiple_of((chunk[0] * tiles + tile) * TILE, TILE), TILE)
        pairs = (
            (picked.at[source, pl.ds(0, width)], x_out),
            (hidden_rows.at[source], hidden_out),
            (grad_rows.at[source], grad_out),
            (both_rows.at[source], both_out),
        )
        return [
            pltpu.make_async_copy(ref, out.at[goal], save_sems.at[tile, k])
            for k, (ref, out) in enumerate(pairs)
        ]

    for copy in loads(0):
        copy.start()

    first = 0
    for option, group in enumerate(sources):
        refs_here = taken[first : first + len(group)]
        first += len(group)

        @pl.when(chunk[1] == option)
        def _(refs_here=refs_here, group=group):
            at = {"x": 0, "cot": 0}
            for ref, kind in zip(refs_here, group):
                columns = pl.ds(0 if kind == "x" else width + LANES, width)
                table[pl.ds(at[kind], ref.shape[0]), columns] = ref[...]
                at[kind] += ref.shape[0]

    logits = dot(table[:, :width], w_router[...]) + carry[0]
    lane = lax.broadcasted_iota(I32, logits.shape, 1)
    one, two = lane == routes[0, :, 0:1], lane == routes[0, :, 1:2]
    score_one = jnp.sum(jnp.where(one, logits, 0.0), axis=1, keepdims=True)
    score_two = jnp.sum(jnp.where(two, logits, 0.0), axis=1, keepdims=True)
    top = jnp.maximum(score_one, score_two)
    score_one, score_two = jnp.exp(score_one - top), jnp.exp(score_two - top)
    both = score_one + score_two
    gates = jnp.where(one, score_one / both, 0.0) + jnp.where(two, score_two / both, 0.0)
    high = gates.astype(BF16).astype(F32)
    low = gates - high
    table[:, width : width + LANES] = (high + pltpu.roll(low, LANES // 2, 1)).astype(BF16)
    total[...] = jnp.zeros_like(total)

    @pl.loop(0, groups)
    def _(group):
        for at in range(GATHER):
            tile = group * GATHER + at
            slot = jnp.minimum(tile, tiles - 1)
            base = jnp.where(tile < number, meta[offset + tiles + slot], rows)
            row = lax.broadcasted_iota(I32, (TILE, rows), 0) + base
            hit = place[0, pl.ds(meta[offset + slot], 1), :] == row
            goal = pl.ds(pl.multiple_of(tile * TILE, TILE), TILE)
            hits[goal, :] = jnp.where(hit, 1.0, 0.0).astype(BF16)

            @pl.when(tile >= number)
            def _():
                back[goal, :] = jnp.zeros((TILE, back.shape[1]), BF16)

        here = pl.ds(pl.multiple_of(group * span_rows, TILE), span_rows)
        picked[here, :] = dot(hits[here, :], table[...]).astype(BF16)

    @pl.loop(0, EXP_FFN)
    def _(expert):
        slot = lax.rem(expert, 2)
        for copy in loads(expert):
            copy.wait()

        @pl.when(expert + 1 < EXP_FFN)
        def _():
            for copy in loads(expert + 1):
                copy.start()

        start = meta[offset + 2 * tiles + 1 + expert]
        amount = meta[offset + 2 * tiles + 1 + EXP_FFN + expert]

        @pl.loop(start, start + amount)
        def _(tile):
            mine = pl.ds(pl.multiple_of(tile * TILE, TILE), TILE)
            inputs = picked[mine, :width]
            lane = lax.broadcasted_iota(I32, (TILE, LANES), 1)
            own = (lane == expert) | (lane == expert + LANES // 2)
            scale = jnp.sum(
                jnp.where(own, picked[mine, width : width + LANES].astype(F32), 0.0),
                axis=1,
                keepdims=True,
            )
            upstream = picked[mine, width + LANES :].astype(F32)
            both = dot(inputs, w_up[slot])
            gate, up = both[:, :hidden_width], both[:, hidden_width:]
            sigma = 1.0 / (1.0 + jnp.exp(-gate))
            active = gate * sigma
            hidden = (active * up).astype(BF16)
            outputs = dot(hidden, w_down[slot])
            gate_term = jnp.sum(upstream * outputs, axis=1, keepdims=True)
            grad_row = (upstream * scale).astype(BF16)
            grad_hidden = dot_nt(grad_row, w_down[slot])
            grad_gate = (grad_hidden * up * sigma * (1.0 + gate * (1.0 - sigma))).astype(BF16)
            grad_up = (grad_hidden * active).astype(BF16)
            grad_both = jnp.concatenate([grad_gate, grad_up], axis=1)
            grad_x = dot_nt(grad_both, w_up[slot])
            hidden_rows[mine, :] = hidden
            grad_rows[mine, :] = grad_row
            both_rows[mine, :] = grad_both
            for copy in saves(tile):
                copy.start()
            back[mine, :width] = (outputs * scale).astype(BF16)
            back[mine, width : 2 * width] = grad_x.astype(BF16)
            back[mine, 2 * width :] = jnp.where(lane == expert, gate_term, 0.0).astype(BF16)

    @pl.loop(0, groups)
    def _(group):
        here = pl.ds(pl.multiple_of(group * span_rows, TILE), span_rows)
        total[...] += dot_tn(hits[here, :], back[here, :])

    feed[...] = total[:, :width].astype(BF16)
    part[:rows, :] = total[:, width : 2 * width].astype(BF16)
    terms = total[:, 2 * width :].T[:16]
    part[rows:, :] = jnp.concatenate([terms, jnp.zeros((16, width - rows), F32)], axis=1).astype(
        BF16
    )

    @pl.loop(0, number)
    def _(tile):
        for copy in saves(tile):
            copy.wait()


def expert_chunk(meta, chunk, options, place, carry, routes, w_router, w_up, w_down, saved):
    rows, width = options[0]["x"][0].shape
    sources = [[kind for kind in ("x", "cot") for _ in option[kind]] for option in options]
    taken = [ref for option in options for kind in ("x", "cot") for ref in option[kind]]
    chunks = place.shape[0]
    hidden_width = w_down.shape[1]
    tiles = most_tiles(rows)
    span = 2 * tiles + 1 + 2 * EXP_FFN
    held = (tiles + GATHER - 1) // GATHER * GATHER * TILE
    shape = jax.ShapeDtypeStruct
    whole = lambda *dims: pl.BlockSpec(dims, lambda i, m, c: (0,) * len(dims))
    mine = lambda *dims: pl.BlockSpec((1, *dims), lambda i, m, c: (c[0], 0, 0))
    stay = pl.BlockSpec(memory_space=pl.ANY)
    columns = (width, hidden_width, width, 2 * hidden_width)
    extra = () if saved is None else tuple(saved)
    return pl.pallas_call(
        functools.partial(expert_kernel, tiles, span, sources),
        grid_spec=pltpu.PrefetchScalarGridSpec(
            num_scalar_prefetch=2,
            grid=(1,),
            in_specs=[
                mine(8, rows),
                mine(rows, LANES),
                mine(rows, 2),
                whole(width, LANES),
                stay,
                stay,
                *[whole(*ref.shape) for ref in taken],
                *[stay] * len(extra),
            ],
            out_specs=[whole(rows + 16, width), whole(rows, width), *[stay] * len(columns)],
            scratch_shapes=[
                pltpu.VMEM((rows, 2 * width + LANES), BF16),
                pltpu.VMEM((held, rows), BF16),
                pltpu.VMEM((held, 2 * width + LANES), BF16),
                pltpu.VMEM((held, 2 * width + LANES), BF16),
                pltpu.VMEM((rows, 2 * width + LANES), F32),
                *[pltpu.VMEM((held, c), BF16) for c in columns[1:]],
                pltpu.VMEM((2, width, 2 * hidden_width), BF16),
                pltpu.VMEM((2, hidden_width, width), BF16),
                pltpu.SemaphoreType.DMA((2, 2)),
                pltpu.SemaphoreType.DMA((tiles, len(columns))),
            ],
        ),
        out_shape=[
            pltpu.HBM((rows + 16, width), BF16),
            pltpu.HBM((rows, width), BF16),
            *[shape((chunks * tiles * TILE, c), BF16) for c in columns],
        ],
        input_output_aliases={8 + len(taken) + k: 2 + k for k in range(len(extra))},
        compiler_params=pltpu.CompilerParams(vmem_limit_bytes=52 * 2**20),
        cost_estimate=lasting(COST_EXPERT),
        name="expert_chunk",
    )(meta, chunk, place, carry, routes, w_router, w_up, w_down, *taken, *extra)


def grad_walk(number, first, tiles):
    experts, chunks = number.shape
    flat = number.reshape(-1)
    groups = flat.shape[0]
    earlier = jnp.arange(groups)[:, None] > jnp.arange(groups)[None, :]
    start = jnp.sum(jnp.where(earlier, flat[None, :], 0), axis=1)
    held = jnp.sum(number, axis=1)
    held_groups = (held + GROUP - 1) // GROUP
    earlier = jnp.arange(experts)[:, None] > jnp.arange(experts)[None, :]
    held_start = jnp.sum(jnp.where(earlier, held[None, :], 0), axis=1)
    group_start = jnp.sum(jnp.where(earlier, held_groups[None, :], 0), axis=1)
    steps = most_groups(chunks * tiles, experts)
    everything = jnp.sum(held_groups)
    step = jnp.minimum(jnp.arange(steps, dtype=I32), everything - 1)
    owner = jnp.sum((group_start + held_groups)[:, None] <= step[None, :], axis=0)
    pick = jnp.arange(experts)[:, None] == owner[None, :]
    look = lambda values: jnp.sum(jnp.where(pick, values[:, None], 0), axis=0)
    done = (step - look(group_start)) * GROUP
    left = look(held) - done
    place_in = done[:, None] + jnp.minimum(jnp.arange(GROUP)[None, :], left[:, None] - 1)
    spot = (look(held_start)[:, None] + place_in).reshape(-1)
    group = jnp.sum((start + flat)[:, None] <= spot[None, :], axis=0)
    pick = jnp.arange(groups)[:, None] == group[None, :]
    offset = jnp.arange(chunks)[None, :] * tiles + first
    block = jnp.sum(jnp.where(pick, (offset.reshape(-1) - start)[:, None], 0), axis=0) + spot
    return jnp.concatenate([owner, block, left, everything[None]]).astype(I32)


def packing(width, hidden_width):
    columns = 2 * hidden_width
    spare = columns - width
    height = hidden_width * width // columns
    pieces = [(slice(width, width + height), slice(0, width), slice(0, height), slice(0, width))]
    short = hidden_width - height
    for at in range(width // spare):
        pieces.append(
            (
                slice(width + at * short, width + (at + 1) * short),
                slice(width, columns),
                slice(height, hidden_width),
                slice(at * spare, (at + 1) * spare),
            )
        )
    return pieces


def packed_height(width, hidden_width):
    return width + width // 2


def weight_grad_kernel(steps, walk, *refs):
    kept, packed = refs[:4], refs[4]
    rows, (sum_up, sum_down, out, load_sems, save_sems) = refs[5:9], refs[9:]
    number = walk[(2 + GROUP) * steps]
    width, hidden_width = sum_up.shape[0], sum_down.shape[0]

    def loads(step):
        slot = lax.rem(step, 2)
        copies = []
        for at in range(GROUP):
            block = walk[steps + step * GROUP + at]
            source = pl.ds(pl.multiple_of(block * TILE, TILE), TILE)
            for kind in range(4):
                copies.append(
                    pltpu.make_async_copy(
                        kept[kind].at[source],
                        rows[kind].at[slot, pl.ds(at * TILE, TILE)],
                        load_sems.at[slot, at, kind],
                    )
                )
        return copies

    def save(expert):
        slot, height = lax.rem(expert, 2), out.shape[1]
        goal = pl.ds(pl.multiple_of(expert * height, height), height)
        return pltpu.make_async_copy(out.at[slot], packed.at[goal], save_sems.at[slot])

    def store(side, up, down):
        out[side, :width] = up.astype(BF16)
        for goal, columns, source, taken in packing(width, hidden_width):
            out[side, goal, columns] = down[source, taken].astype(BF16)

    for copy in loads(0):
        copy.start()

    @pl.loop(0, number)
    def _(step):
        slot = lax.rem(step, 2)
        expert = walk[step]
        left = walk[(1 + GROUP) * steps + step]
        for copy in loads(step):
            copy.wait()

        @pl.when(step + 1 < number)
        def _():
            for copy in loads(step + 1):
                copy.start()

        row = lax.broadcasted_iota(I32, (GROUP * TILE, 1), 0)
        live = row < left * TILE
        side = lax.rem(expert, 2)

        def products():
            return (
                dot_tn(jnp.where(live, rows[0][slot], 0), rows[3][slot]),
                dot_tn(jnp.where(live, rows[1][slot], 0), rows[2][slot]),
            )

        fresh = (step == 0) | (walk[jnp.maximum(step - 1, 0)] != expert)
        done = (step == number - 1) | (walk[jnp.minimum(step + 1, steps - 1)] != expert)

        @pl.when(done & (expert >= 2))
        def _():
            save(expert - 2).wait()

        @pl.when(fresh & done)
        def _():
            store(side, *products())

        @pl.when(fresh & jnp.logical_not(done))
        def _():
            sum_up[...], sum_down[...] = products()

        @pl.when(jnp.logical_not(fresh | done))
        def _():
            up, down = products()
            sum_up[...] += up
            sum_down[...] += down

        @pl.when(jnp.logical_not(fresh) & done)
        def _():
            up, down = products()
            store(side, sum_up[...] + up, sum_down[...] + down)

        @pl.when(done)
        def _():
            save(expert).start()

    for expert in (EXP_FFN - 2, EXP_FFN - 1):
        save(expert).wait()


def weight_grads(walk, saved):
    width, hidden_width = saved[0].shape[1], saved[1].shape[1]
    height = packed_height(width, hidden_width)
    steps = most_groups(saved[0].shape[0] // TILE, EXP_FFN)
    shape = jax.ShapeDtypeStruct
    stay = pl.BlockSpec(memory_space=pl.ANY)
    return pl.pallas_call(
        functools.partial(weight_grad_kernel, steps),
        grid_spec=pltpu.PrefetchScalarGridSpec(
            num_scalar_prefetch=1,
            grid=(1,),
            in_specs=[stay] * 4,
            out_specs=stay,
            scratch_shapes=[
                *[pltpu.VMEM((2, GROUP * TILE, kept.shape[1]), BF16) for kept in saved],
                pltpu.VMEM((width, 2 * hidden_width), F32),
                pltpu.VMEM((hidden_width, width), F32),
                pltpu.VMEM((2, height, 2 * hidden_width), BF16),
                pltpu.SemaphoreType.DMA((2, GROUP, 4)),
                pltpu.SemaphoreType.DMA((2,)),
            ],
        ),
        out_shape=shape((EXP_FFN * height, 2 * hidden_width), BF16),
        compiler_params=pltpu.CompilerParams(vmem_limit_bytes=48 * 2**20),
        cost_estimate=lasting(COST_GRADS),
        name="weight_grads",
    )(walk, *saved)


def widen_kernel(source, up, down):
    width = down.shape[1]
    split = source.shape[1] // LANES
    for row in range(split):
        at = row % 2 * (source.shape[1] // 2) + row // 2 * LANES
        up[pl.ds(row, width, stride=split), :] = source[:width, at : at + LANES].astype(F32)
    for place, columns, goal, taken in packing(width, down.shape[0]):
        down[goal, taken] = source[place, columns].astype(F32)


def widen(packed, width, hidden_width):
    height = packed_height(width, hidden_width)
    rows = width * packed.shape[1] // LANES
    shape = jax.ShapeDtypeStruct
    return pl.pallas_call(
        widen_kernel,
        grid=(EXP_FFN,),
        in_specs=[pl.BlockSpec((height, packed.shape[1]), lambda i: (i, 0))],
        out_specs=[
            pl.BlockSpec((rows, LANES), lambda i: (i, 0)),
            pl.BlockSpec((hidden_width, width), lambda i: (i, 0)),
        ],
        out_shape=[
            shape((EXP_FFN * rows, LANES), F32),
            shape((EXP_FFN * hidden_width, width), F32),
        ],
        compiler_params=pltpu.CompilerParams(vmem_limit_bytes=60 * 2**20),
        cost_estimate=lasting(COST_WIDEN),
        name="widen",
    )(packed)


def shards(
    dp_size,
    stream,
    cotangent,
    gain_attention,
    w_inputs,
    w_output,
    gain_experts,
    w_router,
    w_carry,
    w_gate_up,
    w_down,
    w_constant,
    constant_vectors,
    previous_logits,
    routes,
    valid,
    prefix,
):
    rows, width = stream.shape
    tokens = routes.shape[0]
    chunks = tokens // rows
    head_columns = w_inputs.shape[2]
    here = lax.axis_index("tensor")
    index = lax.axis_index("dp")
    outer = (here == 0) | (here == chunks - 1)
    bits = list(range(dp_size.bit_length() - 1))
    first_row = here * rows
    valid_all = valid.astype(F32)
    cut = lambda array, at: lax.dynamic_slice_in_dim(array, at, rows, 0)
    valid_here = cut(valid_all, first_row)
    routes_here = cut(routes, first_row)
    previous_here = cut(previous_logits, first_row)

    w_in_rows = w_inputs.transpose(0, 2, 1)
    packed = jnp.concatenate([w_in_rows, w_output[None]], axis=0).reshape(-1, width)
    piece_rows = packed.shape[0] // dp_size
    position = (index >> 1) | ((index & 1) << (len(bits) - 1))
    piece = lax.dynamic_slice_in_dim(packed, position * piece_rows, piece_rows, 0)
    normed_here, inverse_one = norm_forward(stream, gain_attention)
    normed_low = normed_here.astype(BF16)
    normed_other = along_z(normed_low, SIDE)
    piece = along_z(piece, CROSS)
    cot_low = behind(cotangent, piece).astype(BF16)
    cot_side, cot_middle = along_z(cot_low, SIDE), along_z(cot_low, MIDDLE)
    for level, bit in enumerate([*bits[1:], bits[0]]):
        if level == 0:
            place, meta, number, first = expert_plan(*behind((routes, valid), piece), chunks)
        if level == 1:
            number, first = behind((number, first), piece)
            walk = grad_walk(number, first, most_tiles(rows))
        other = along_dp(piece, bit, dp_size)
        piece = jnp.where(
            (index >> bit) & 1 == 0,
            jnp.concatenate([piece, other], axis=0),
            jnp.concatenate([other, piece], axis=0),
        )
    carry = jnp.dot(behind(previous_logits, place), w_carry, precision=HIGHEST, preferred_element_type=F32)
    columns = carry.shape[1]
    carry_wide = jnp.pad(carry, ((0, 0), (0, LANES - columns))).reshape(chunks, rows, LANES)
    routes_live = jnp.where(valid[:, None] > 0, routes, -1).reshape(chunks, rows, 2)
    router_wide = jnp.pad(w_router, ((0, 0), (0, LANES - columns)))
    partner = piece.reshape(4, head_columns, width)
    both_in = jnp.concatenate([w_in_rows, partner[:3]], axis=1)
    both_out = jnp.concatenate([w_output, partner[3]], axis=0)

    core = index & 1
    offset = (here % 2) * rows
    sequence = here // 2
    scalars = jnp.stack([offset, prefix[sequence]]).astype(I32)
    cosine, sine = rope_tables(offset)
    valid_rows = jnp.concatenate([cut(valid, first_row), cut(valid, (here ^ 1) * rows)])[:, None]
    fixed = (both_in, both_out, cosine, sine, valid_rows)
    ready = (place, meta, walk, cot_side, cot_middle, carry_wide, routes_live, router_wide)
    part_own, part_other, *saved_attention = attention_forward(
        scalars, normed_low, normed_other, *fixed, ready
    )
    attention_other = along_z(part_other, SIDE)

    cot_far, cot_across = along_z(cot_middle, OUTWARD), along_z(cot_side, MIDDLE)
    cot_far, cot_across = behind((cot_far, cot_across), part_own)
    w_up = behind(w_gate_up, (part_own, cot_far, cot_across)).reshape(EXP_FFN, width, -1)
    attention_other = behind(attention_other, w_up)
    attention = part_own.astype(F32) + attention_other.astype(F32)
    middle = stream + attention
    second, inverse_two = norm_forward(middle, gain_experts)
    second_low = second.astype(BF16)

    which = slot_chunks(here)

    def chunk(slot, options, saved):
        choice = outer.astype(I32) * (len(options) - 1)
        return expert_chunk(
            meta,
            jnp.stack([which[slot], choice]),
            options,
            place,
            carry_wide,
            routes_live,
            router_wide,
            w_up,
            w_down,
            saved,
        )

    third_rows = rows // 3 // 16 * 16
    cuts = (0, third_rows, 2 * third_rows, rows)
    cot_pieces = [cot_across[low:high] for low, high in zip(cuts[:-1], cuts[1:])]
    side, middle_rows = along_z(second_low, SIDE), along_z(second_low, MIDDLE)
    cot_last = [along_z(behind(cot_pieces[0], second_low), OUTWARD)]
    part_0, feed_0, *saved = chunk(0, [{"x": [second_low], "cot": [cot_low]}], None)
    side, middle_rows, cot_last[0] = behind((side, middle_rows, cot_last[0]), part_0)
    far, across = along_z(middle_rows, OUTWARD), along_z(side, MIDDLE)
    cot_last.append(along_z(behind(cot_pieces[1], part_0), OUTWARD))
    part_1, feed_1, *saved = chunk(1, [{"x": [side], "cot": [cot_side]}], saved)
    near, feed_near = along_z(part_1, INWARD), along_z(feed_1, INWARD)
    far, across, cot_last[1] = behind((far, across, cot_last[1]), part_1)
    last = along_z(across, OUTWARD)
    cot_last.append(along_z(behind(cot_pieces[2], part_1), OUTWARD))
    part_2, feed_2, *saved = chunk(
        2, [{"x": [middle_rows], "cot": [cot_middle]}, {"x": [far], "cot": [cot_far]}], saved
    )
    third = along_z(part_2, INWARD)
    last, cot_last[2] = behind((last, cot_last[2]), part_2)
    part_3, feed_3, *saved = chunk(
        3,
        [{"x": [across], "cot": [cot_across]}, {"x": [last], "cot": cot_last}],
        saved,
    )

    inward = along_z(part_3, INWARD)
    packed = weight_grads(walk, saved)
    inward, packed = lax.optimization_barrier((inward, packed))
    packed = lax.psum_scatter(packed, "dp", scatter_dimension=0, tiled=True)
    feed_outward = along_z(behind(feed_3, inward), INWARD)
    inward = part_3 + inward
    inward, feed_outward = lax.optimization_barrier((along_z(inward, MIDDLE), feed_outward))
    third = along_z(part_2 + third, MIDDLE)
    outward = along_z(part_1 + inward, OUTWARD)
    summed = part_0.astype(F32) + near.astype(F32) + third.astype(F32) + outward.astype(F32)

    logits = dot(second_low, w_router) + cut(carry, first_row)
    picked = routes_here[:, :, None] == jnp.arange(columns, dtype=I32)[None, None, :]
    chosen = jnp.sum(jnp.where(picked, logits[:, None, :], 0.0), axis=-1)
    gates_here = jax.nn.softmax(chosen, axis=-1)
    live_gates = gates_here * valid_here[:, None]
    copy_gate = jnp.sum(jnp.where(routes_here == EXP_FFN + 1, live_gates, 0.0), axis=-1)
    constant_gates = jnp.stack(
        [
            jnp.sum(jnp.where(routes_here == EXP_FFN + 2 + number, live_gates, 0.0), axis=-1)
            for number in range(2)
        ],
        axis=1,
    )
    alphas = jax.nn.softmax(
        jnp.einsum("td,cad->tca", second, w_constant, precision=HIGHEST, preferred_element_type=F32),
        axis=-1,
    )
    constant_out = (
        alphas[:, :, 0:1] * second[:, None, :] + alphas[:, :, 1:2] * constant_vectors[None, :, :]
    )
    extra = copy_gate[:, None] * second + jnp.sum(
        constant_gates[:, :, None] * constant_out, axis=1
    )
    copy_terms = jnp.sum(cotangent * second, axis=-1)
    constant_terms = jnp.sum(cotangent[:, None, :] * constant_out, axis=-1)
    grad_constant_out = constant_gates[:, :, None] * cotangent[:, None, :]
    grad_vectors = jnp.sum(alphas[:, :, 1:2] * grad_constant_out, axis=0)
    grad_alphas = jnp.stack(
        [
            jnp.sum(grad_constant_out * second[:, None, :], axis=-1),
            jnp.sum(grad_constant_out * constant_vectors[None, :, :], axis=-1),
        ],
        axis=-1,
    )
    grad_mix = alphas * (grad_alphas - jnp.sum(alphas * grad_alphas, axis=-1, keepdims=True))
    grad_constant = jnp.einsum(
        "tca,td->cad", grad_mix, second, precision=HIGHEST, preferred_element_type=F32
    )
    grad_local = (
        copy_gate[:, None] * cotangent
        + jnp.sum(alphas[:, :, 0:1] * grad_constant_out, axis=1)
        + jnp.einsum(
            "tca,cad->td", grad_mix, w_constant, precision=HIGHEST, preferred_element_type=F32
        )
    )

    gate_grads = summed[rows : rows + EXP_FFN, :rows].T
    gate_table = jnp.concatenate(
        [gate_grads, jnp.zeros((rows, 1), F32), copy_terms[:, None], constant_terms], axis=1
    )
    grad_gates = jnp.sum(jnp.where(picked, gate_table[:, None, :], 0.0), axis=-1)
    grad_gates = grad_gates * valid_here[:, None]
    grad_chosen = gates_here * (
        grad_gates - jnp.sum(gates_here * grad_gates, axis=-1, keepdims=True)
    )
    grad_logits = jnp.sum(jnp.where(picked, grad_chosen[:, :, None], 0.0), axis=1)
    grad_router = jnp.dot(
        second_low.astype(F32).T, grad_logits, precision=HIGHEST, preferred_element_type=F32
    )
    grad_carry = jnp.dot(
        previous_here.T, grad_logits, precision=HIGHEST, preferred_element_type=F32
    )
    grad_previous = jnp.dot(
        grad_logits, w_carry.T, precision=HIGHEST, preferred_element_type=F32
    )
    grad_second = (
        summed[:rows]
        + grad_local
        + jnp.dot(
            grad_logits, w_router.astype(F32).T, precision=HIGHEST, preferred_element_type=F32
        )
    )
    grad_gain_experts = jnp.sum(grad_second * middle * inverse_two, axis=0)
    grad_middle = cotangent + norm_backward(middle, inverse_two, gain_experts, grad_second)

    grad_low = grad_middle.astype(BF16)
    grad_other = along_z(grad_low, SIDE)
    feed_outward = feed_3 + feed_outward

    part_own, part_other, grad_w, grad_o, gain_rows = attention_backward(
        scalars, normed_low, normed_other, *fixed, grad_low, grad_other, saved_attention, ()
    )
    grad_normed = part_own.astype(F32) + along_z(part_other, SIDE).astype(F32)
    grad_stream = grad_middle + norm_backward(stream, inverse_one, gain_attention, grad_normed)

    feed_2, feed_outward = behind((feed_2, feed_outward), part_own)
    feed_third, feed_outward = along_z(feed_2, INWARD), along_z(feed_outward, MIDDLE)
    feed_third = along_z(feed_2 + feed_third, MIDDLE)
    feed_outward = along_z(feed_1 + feed_outward, OUTWARD)
    feed = feed_0.astype(F32) + feed_near.astype(F32)
    feed = feed + feed_third.astype(F32) + feed_outward.astype(F32)
    experts = feed + extra
    block_out = middle + experts
    squares = [
        jnp.sum(valid_here[:, None] * part * part) for part in (block_out, attention, experts)
    ]
    squares = jnp.stack([*squares, jnp.sum(valid_here)])

    own_grads = jnp.concatenate([grad_w[:, :head_columns], grad_o[None, :head_columns]], axis=0)
    far_grads = jnp.concatenate([grad_w[:, head_columns:], grad_o[None, head_columns:]], axis=0)
    order = bits
    own_piece = reduce_blocks(own_grads.reshape(-1, width), order[:1], index, dp_size)
    far_piece = reduce_blocks(far_grads.reshape(-1, width), order[:1], index, dp_size)
    packed = lax.all_gather(behind(packed, own_piece), "dp", axis=0, tiled=True)
    own_piece = reduce_blocks(own_piece, order[1:], index, dp_size)
    far_piece = reduce_blocks(far_piece, order[1:], index, dp_size)
    own_piece = own_piece + along_z(far_piece, CROSS)
    grad_gate_up, grad_down = widen(packed, width, w_down.shape[1])
    grad_gate_up = grad_gate_up.reshape(EXP_FFN, width, -1, 2, LANES).transpose(0, 1, 3, 2, 4)
    grad_gate_up = grad_gate_up.reshape(EXP_FFN, width, 2, -1)
    grad_down = grad_down.reshape(EXP_FFN, -1, width)

    attention_grads = spread_blocks(own_piece, order, index, dp_size).astype(F32)
    attention_grads = attention_grads.reshape(4, head_columns, width)
    grad_inputs = attention_grads[:3].transpose(0, 2, 1)
    grad_output = attention_grads[3]

    wide = lambda array: jnp.pad(array, ((0, 0), (0, width - array.shape[1])))
    small = jnp.concatenate(
        [
            grad_gain_experts[None],
            grad_router.T,
            wide(grad_carry),
            grad_constant.reshape(-1, width),
            grad_vectors,
            wide(squares[None]),
            jnp.sum(gain_rows, axis=0, keepdims=True) / gain_attention[None],
        ],
        axis=0,
    )
    small = sum_everywhere(small, bits, dp_size, grad_down)
    at = 1 + 2 * columns
    squares = small[at + 6, :3]
    counted = small[at + 6, 3]
    rms_values = jnp.sqrt(squares / (jnp.maximum(counted, 1.0) * width))
    return (
        block_out,
        grad_stream,
        small[at + 7],
        grad_inputs,
        grad_output,
        small[0],
        small[1 : 1 + columns].T,
        small[1 + columns : at, :columns],
        grad_gate_up,
        grad_down,
        small[at : at + 4].reshape(2, 2, width),
        small[at + 4 : at + 6],
        grad_previous,
        rms_values,
    )


def solution(mesh):
    return jax.shard_map(
        functools.partial(shards, mesh.shape["dp"]),
        mesh=mesh,
        in_specs=(
            P(("dp", "tensor"), None),
            P(("dp", "tensor"), None),
            P(),
            P(None, None, "tensor"),
            P("tensor", None),
            P(),
            P(),
            P(),
            P(None, None, None, "tensor"),
            P(None, "tensor", None),
            P(),
            P(),
            P("dp", None),
            P("dp", None),
            P("dp"),
            P("dp"),
        ),
        out_specs=(
            P(("dp", "tensor"), None),
            P(("dp", "tensor"), None),
            P(),
            P(None, None, "tensor"),
            P("tensor", None),
            P(),
            P(),
            P(),
            P(None, None, None, "tensor"),
            P(None, "tensor", None),
            P(),
            P(),
            P(("dp", "tensor"), None),
            P(),
        ),
        check_vma=False,
    )
```
